32 devices in a mesh: wide: 16 (over z, y, x), narrow: 2 (over core).
Axes of the slice: x: 2, y: 2, z: 4, core: 2. Of those that a mesh axis runs over, the one named last changes fastest.
Arguments:
- stream: bfloat16 [32768, 768], P(('wide', 'narrow')), may hold values from -6 to 6
- seq_lengths: int32 [16, 2], P('wide'), may hold values from 0 to 2048, as said below
- cotangent: float32 [32768, 768], P(('wide', 'narrow')), may hold values from -6 to 6
- w_qkv: bfloat16 [2, 768, 3, 768], P(None, None, None, 'narrow'), may hold values from -0.21875 to 0.21875
- w_out: bfloat16 [2, 768, 768], P(None, 'narrow'), may hold values from -6 to 6
- w_in: bfloat16 [2, 768, 3072], P(None, None, 'narrow'), may hold values from -0.21875 to 0.21875
- w_back: bfloat16 [2, 3072, 768], P(None, 'narrow'), may hold values from -0.109375 to 0.109375
- norm_params: float32 [2, 4, 768], replicated, may hold values from -2.5 to 2.5, as said below
- qkv_master: float32 [2, 768, 3, 768], P(None, 'wide', None, 'narrow'), may hold values from -0.21875 to 0.21875
- qkv_first: float32 [2, 768, 3, 768], P(None, 'wide', None, 'narrow'), may hold values from -0.00390625 to 0.00390625
- qkv_second: float32 [2, 768, 3, 768], P(None, 'wide', None, 'narrow'), may hold values from 7.06119e-08 to 2.824476e-07
- out_master: float32 [2, 768, 768], P(None, ('narrow', 'wide')), may hold values from -0.21875 to 0.21875
- out_first: float32 [2, 768, 768], P(None, ('narrow', 'wide')), may hold values from -0.00036621094 to 0.00036621094
- out_second: float32 [2, 768, 768], P(None, ('narrow', 'wide')), may hold values from 6.2061234e-10 to 2.4824494e-09
- in_master: float32 [2, 768, 3072], P(None, 'wide', 'narrow'), may hold values from -0.21875 to 0.21875
- in_first: float32 [2, 768, 3072], P(None, 'wide', 'narrow'), may hold values from -0.00390625 to 0.00390625
- in_second: float32 [2, 768, 3072], P(None, 'wide', 'narrow'), may hold values from 7.06119e-08 to 2.824476e-07
- back_master: float32 [2, 3072, 768], P(None, ('narrow', 'wide')), may hold values from -0.109375 to 0.109375
- back_first: float32 [2, 3072, 768], P(None, ('narrow', 'wide')), may hold values from -0.00390625 to 0.00390625
- back_second: float32 [2, 3072, 768], P(None, ('narrow', 'wide')), may hold values from 7.06119e-08 to 2.824476e-07
- norm_master: float32 [2, 4, 768], P(None, None, ('wide', 'narrow')), may hold values from -2.5 to 2.5, as said below
- norm_first: float32 [2, 4, 768], P(None, None, ('wide', 'narrow')), may hold values from -0.00390625 to 0.00390625
- norm_second: float32 [2, 4, 768], P(None, None, ('wide', 'narrow')), may hold values from 7.06119e-08 to 2.824476e-07
Outputs:
- output: float32 [32768, 768], P(('wide', 'narrow'))
- stream_grad: float32 [32768, 768], P(('wide', 'narrow'))
- qkv_master_new: float32 [2, 768, 3, 768], P(None, 'wide', None, 'narrow')
- qkv_first_new: float32 [2, 768, 3, 768], P(None, 'wide', None, 'narrow')
- qkv_second_new: float32 [2, 768, 3, 768], P(None, 'wide', None, 'narrow')
- out_master_new: float32 [2, 768, 768], P(None, ('narrow', 'wide'))
- out_first_new: float32 [2, 768, 768], P(None, ('narrow', 'wide'))
- out_second_new: float32 [2, 768, 768], P(None, ('narrow', 'wide'))
- in_master_new: float32 [2, 768, 3072], P(None, 'wide', 'narrow')
- in_first_new: float32 [2, 768, 3072], P(None, 'wide', 'narrow')
- in_second_new: float32 [2, 768, 3072], P(None, 'wide', 'narrow')
- back_master_new: float32 [2, 3072, 768], P(None, ('narrow', 'wide'))
- back_first_new: float32 [2, 3072, 768], P(None, ('narrow', 'wide'))
- back_second_new: float32 [2, 3072, 768], P(None, ('narrow', 'wide'))
- norm_master_new: float32 [2, 4, 768], P(None, None, ('wide', 'narrow'))
- norm_first_new: float32 [2, 4, 768], P(None, None, ('wide', 'narrow'))
- norm_second_new: float32 [2, 4, 768], P(None, None, ('wide', 'narrow'))
- clip_norm: float32 [1], replicated
The draws below stay inside these ranges and needn't reach their ends.
Inputs may be any that keep to these rules, and one draw needn't show every extreme that they name: `seq_lengths`: row b holds the lengths of bucket b's sequences, laid end to end from the bucket's first slot; the rest of the bucket is padding. Either both entries are 1024, or the first lies from 1024 to 2048 and the second is 0. Some bucket holds one sequence of 2048, some bucket two of 1024. `norm_params`: rows 0 and 2 of each layer are positive gains, rows 1 and 3 shifts. `norm_master`: rows 0 and 2 of each layer are positive gains, rows 1 and 3 shifts.
All inputs are finite; a program needn't handle non-finite values.
Results may differ from the reference program's by a relative error of at most 0.023.
Values may be sent and summed in bfloat16 or wider, within the bound.
No kernel may reach another device: no remote copies, remote signals or barrier semaphores. Data moves between devices by JAX's collectives and lax.ppermute only.
A program may use at most 320 MiB of HBM per device.

```python
import math
import jax
import jax.numpy as jnp
from jax import lax

D = 768
HEADS = 12
FF = 3072
LAYERS = 2
CAP = 2048
BLOCK = 512
TOKENS = 32768
N_WIDE = 16


def norm_table(key):
    gain_key, shift_key = jax.random.split(key)
    ramp = jnp.arange(D, dtype=jnp.float32) / float(D - 1)
    slope = 0.6 + 1.2 * ramp
    gains = slope[None, None, :] + 0.1 * jnp.clip(jax.random.normal(gain_key, (LAYERS, 2, D), jnp.float32), -2.0, 2.0)
    shifts = 0.3 * jnp.clip(jax.random.normal(shift_key, (LAYERS, 2, D), jnp.float32), -5.0, 5.0)
    return jnp.stack([gains, shifts], axis=2).reshape(LAYERS, 4, D)


def draw_norm_params(key, part):
    return norm_table(jax.random.fold_in(key, 11))


def draw_norm_master(key, part):
    return norm_table(jax.random.fold_in(key, 23))


def draw_seq_lengths(key, part):
    kind_key, size_key, pick_key = jax.random.split(jax.random.fold_in(key, 37), 3)
    kinds = jax.random.randint(kind_key, (N_WIDE,), 0, 4)
    picked = jax.random.permutation(pick_key, N_WIDE)
    kinds = kinds.at[picked[0]].set(0).at[picked[1]].set(1)
    partial_len = jax.random.randint(size_key, (N_WIDE,), CAP // 2, CAP + 1)
    first_len = jnp.where(kinds == 0, CAP, jnp.where(kinds == 3, partial_len, CAP // 2))
    second_len = jnp.where((kinds == 1) | (kinds == 2), CAP // 2, 0)
    return jnp.stack([first_len, second_len], axis=1).astype(jnp.int32)


def block_scale(rng, dims, cuts, least, top_value):
    gain, own = 1.0, jax.random.fold_in(rng, 6)
    for dim, shards_of in cuts:
        steps = jnp.exp(jax.random.uniform(jax.random.fold_in(own, dim), (shards_of,), jnp.float32, least / len(cuts), top_value / len(cuts)))
        gain = gain * jnp.repeat(steps, dims[dim] // shards_of).reshape([-1 if axis == dim else 1 for axis in range(len(dims))])
    return gain


def centred(stream_key, shape, deviation, limit, cuts=(), kind=jnp.bfloat16):
    loudness = block_scale(stream_key, shape, cuts, -0.22, 0.18) if cuts else 1.0
    array = jax.random.normal(stream_key, shape, jnp.float32) * deviation * loudness
    return jnp.minimum(jnp.maximum(array, -limit), limit).astype(kind)


def setup_inputs(seed: int = 0) -> dict:
    key_list = jax.random.split(jax.random.key(seed), 24)
    return {
        "stream": centred(key_list[0], (TOKENS, D), 1.0, 6.0, ((0, 32),)),
        "seq_lengths": draw_seq_lengths(jax.random.fold_in(key_list[23], 71), 0),
        "cotangent": centred(key_list[2], (TOKENS, D), 1.0, 6.0, ((0, 32),), jnp.float32),
        "w_qkv": centred(key_list[3], (LAYERS, D, 3, D), D ** -0.5, 0.21875, ((3, 2),)),
        "w_out": centred(key_list[4], (LAYERS, D, D), ((CAP // 2 * D ** -1) ** 0.5), 6.0, ((1, 2),)),
        "w_in": centred(key_list[5], (LAYERS, D, FF), D ** -0.5, 0.21875, ((2, 2),)),
        "w_back": centred(key_list[6], (LAYERS, FF, D), FF ** -0.5, 0.109375, ((1, 2),)),
        "norm_params": draw_norm_params(jax.random.fold_in(key_list[23], 71), 0),
        "qkv_master": centred(key_list[8], (LAYERS, D, 3, D), D ** -0.5, 0.21875, ((1, 16), (3, 2)), jnp.float32),
        "qkv_first": centred(key_list[9], (LAYERS, D, 3, D), ((LAYERS * (4 * D * D + 2 * D * FF + 4 * D)) ** -0.5), 0.00390625, ((1, 16), (3, 2)), jnp.float32),
        "qkv_second": jnp.clip(jnp.exp(math.log(2.8244758709661255e-07) - 1.3862944 * jax.random.uniform(key_list[10], (LAYERS, D, 3, D), jnp.float32) ** block_scale(key_list[10], (LAYERS, D, 3, D), ((1, 16), (3, 2)), -0.2, 0.2)), 7.061189677415314e-08, 2.8244758709661255e-07),
        "out_master": centred(key_list[11], (LAYERS, D, D), D ** -0.5, 0.21875, ((1, 32),), jnp.float32),
        "out_first": centred(key_list[12], (LAYERS, D, D), (3 * (CAP // 2) ** -0.5 * (LAYERS * (4 * D * D + 2 * D * FF + 4 * D)) ** -0.5), 0.00036621094, ((1, 32),), jnp.float32),
        "out_second": jnp.clip(jnp.exp(math.log(2.482449357188443e-09) - 1.3862944 * jax.random.uniform(key_list[13], (LAYERS, D, D), jnp.float32) ** block_scale(key_list[13], (LAYERS, D, D), ((1, 32),), -0.2, 0.2)), 6.206123392971108e-10, 2.482449357188443e-09),
        "in_master": centred(key_list[14], (LAYERS, D, FF), D ** -0.5, 0.21875, ((1, 16), (2, 2)), jnp.float32),
        "in_first": centred(key_list[15], (LAYERS, D, FF), ((LAYERS * (4 * D * D + 2 * D * FF + 4 * D)) ** -0.5), 0.00390625, ((1, 16), (2, 2)), jnp.float32),
        "in_second": jnp.clip(jnp.exp(math.log(2.8244758709661255e-07) - 1.3862944 * jax.random.uniform(key_list[16], (LAYERS, D, FF), jnp.float32) ** block_scale(key_list[16], (LAYERS, D, FF), ((1, 16), (2, 2)), -0.2, 0.2)), 7.061189677415314e-08, 2.8244758709661255e-07),
        "back_master": centred(key_list[17], (LAYERS, FF, D), FF ** -0.5, 0.109375, ((1, 32),), jnp.float32),
        "back_first": centred(key_list[18], (LAYERS, FF, D), ((LAYERS * (4 * D * D + 2 * D * FF + 4 * D)) ** -0.5), 0.00390625, ((1, 32),), jnp.float32),
        "back_second": jnp.clip(jnp.exp(math.log(2.8244758709661255e-07) - 1.3862944 * jax.random.uniform(key_list[19], (LAYERS, FF, D), jnp.float32) ** block_scale(key_list[19], (LAYERS, FF, D), ((1, 32),), -0.2, 0.2)), 7.061189677415314e-08, 2.8244758709661255e-07),
        "norm_master": draw_norm_master(jax.random.fold_in(key_list[23], 71), 0),
        "norm_first": centred(key_list[21], (LAYERS, 4, D), ((LAYERS * (4 * D * D + 2 * D * FF + 4 * D)) ** -0.5), 0.00390625, ((2, 32),), jnp.float32),
        "norm_second": jnp.clip(jnp.exp(math.log(2.8244758709661255e-07) - 1.3862944 * jax.random.uniform(key_list[22], (LAYERS, 4, D), jnp.float32) ** block_scale(key_list[22], (LAYERS, 4, D), ((2, 32),), -0.2, 0.2)), 7.061189677415314e-08, 2.8244758709661255e-07),
    }


HIGH = lax.Precision.HIGHEST
EPS_NORM = 1e-05
CLIP = 1.0
BETA_ONE = 0.5
BETA_TWO = 0.5
ADAM_EPS = 1e-08
LR_MATRIX = 0.1
LR_NORMS = 0.5
DECAY_MATRIX = 0.1
STEP_NUMBER = 4.0

@jax.custom_vjp
def low(v):
    return lax.optimization_barrier(v.astype(jnp.bfloat16)).astype(jnp.float32)

@jax.custom_vjp
def low_back(v):
    return v

def low_keep(v):
    return (low(v), None)

def low_pass(kept, grad):
    return (grad,)

def back_keep(v):
    return (v, None)

def back_low(kept, grad):
    return (low(grad),)
low.defvjp(low_keep, low_pass)
low_back.defvjp(back_keep, back_low)

def row_layout(lengths, row_count):
    row_index = jnp.arange(row_count, dtype=jnp.int32)
    first_len = lengths[0].astype(jnp.int32)
    second_len = lengths[1].astype(jnp.int32)
    in_first = row_index < first_len
    in_second = (row_index >= first_len) & (row_index < first_len + second_len)
    segment = jnp.where(in_first, 0, jnp.where(in_second, 1, -1)).astype(jnp.int32)
    position = jnp.where(in_first, row_index, jnp.where(in_second, row_index - first_len, row_index))
    seq_span = jnp.where(in_first, first_len, jnp.where(in_second, second_len, 1))
    phase_angle = 0.5 * math.pi * position.astype(jnp.float32) / seq_span.astype(jnp.float32)
    return (segment, jnp.cos(phase_angle), jnp.sin(phase_angle))

def attend(packed, segment, cosine, sine, block_rows, head_count):
    row_count = packed.shape[0]
    width = packed.shape[2]
    head_size = width // head_count
    block_count = row_count // block_rows

    def split_blocks(values):
        return values.reshape((block_count, block_rows) + values.shape[1:])
    queries = packed[:, 0].reshape(row_count, head_count, head_size)
    keys = packed[:, 1].reshape(row_count, head_count, head_size)
    value_rows = packed[:, 2].reshape(row_count, head_count, head_size)
    block_inputs = (split_blocks(queries), split_blocks(keys), split_blocks(value_rows), split_blocks(segment), split_blocks(cosine), split_blocks(sine))
    local_index = jnp.arange(block_rows, dtype=jnp.int32)

    @jax.checkpoint
    def block_step(carry_in, pieces):
        kv_state, key_total, before = carry_in
        query_part, key_part, value_part, seg_part, cos_part, sin_part = pieces
        query_feat = jax.nn.relu(query_part)
        key_feat = jax.nn.relu(key_part)
        query_cat = jnp.concatenate([query_feat * cos_part[:, None, None], query_feat * sin_part[:, None, None]], axis=2)
        key_cat = jnp.concatenate([key_feat * cos_part[:, None, None], key_feat * sin_part[:, None, None]], axis=2)
        live_mask = seg_part >= 0
        same_seq = (seg_part[:, None] == seg_part[None, :]) & (local_index[None, :] <= local_index[:, None]) & live_mask[:, None]
        scores = jnp.einsum('ihf,jhf->hij', query_cat, key_cat, precision=HIGH)
        scores = jnp.where(same_seq[None], scores, 0.0)
        numerator = jnp.einsum('hij,jhd->ihd', scores, value_part, precision=HIGH)
        denominator = jnp.transpose(lax.optimization_barrier(jnp.sum(scores, axis=2)))
        carried = ((seg_part == before) & live_mask).astype(query_feat.dtype)
        numerator = numerator + carried[:, None, None] * jnp.einsum('ihf,hfd->ihd', query_cat, kv_state, precision=HIGH)
        denominator = denominator + carried[:, None] * jnp.einsum('ihf,hf->ih', query_cat, key_total, precision=HIGH)
        block_out = numerator / jnp.maximum(denominator, 1.0)[:, :, None]
        last_seg = seg_part[block_rows - 1]
        keep_state = (last_seg == before).astype(query_feat.dtype)
        take_rows = ((seg_part == last_seg) & live_mask).astype(query_feat.dtype)
        kept_keys = key_cat * take_rows[:, None, None]
        kv_state = keep_state * kv_state + jnp.einsum('jhf,jhd->hfd', kept_keys, value_part, precision=HIGH)
        key_total = keep_state * key_total + lax.optimization_barrier(jnp.sum(kept_keys, axis=0))
        return ((kv_state, key_total, last_seg), block_out.reshape(block_rows, width))
    start_carry = (jnp.zeros((head_count, 2 * head_size, head_size), jnp.float32), jnp.zeros((head_count, 2 * head_size), jnp.float32), jnp.asarray(-1, dtype=jnp.int32))
    carry_end, outputs_all = lax.scan(block_step, start_carry, block_inputs)
    return outputs_all.reshape(row_count, width)

def normalize(residual_in, gain_row, shift_row):
    row_mean = lax.optimization_barrier(jnp.mean(residual_in, axis=-1, keepdims=True))
    centered = residual_in - row_mean
    variance = lax.optimization_barrier(jnp.mean(centered * centered, axis=-1, keepdims=True))
    return centered * lax.rsqrt(variance + EPS_NORM) * gain_row + shift_row

def adamw(master, moment_one, moment_two, gradient, factor, fix_one, fix_two, step_rate, decay_rate):
    clipped = gradient * factor
    moment_one = BETA_ONE * moment_one + (1.0 - BETA_ONE) * clipped
    moment_two = BETA_TWO * moment_two + (1.0 - BETA_TWO) * clipped * clipped
    update = moment_one / fix_one / (jnp.sqrt(moment_two / fix_two) + ADAM_EPS)
    master = master - step_rate * (update + decay_rate * master)
    return (master, moment_one, moment_two)

def forward(current, w_qkv, w_out, w_in, w_back, norm_params, segment, cosine, sine):
    for layer_index in range(LAYERS):
        attn_in = low(current)
        projected = low_back(jnp.einsum('td,dce->tce', attn_in, w_qkv[layer_index], precision=HIGH))
        mixed = attend(projected, segment, cosine, sine, BLOCK, HEADS)
        mixed_low = low(mixed)
        branch = low_back(jnp.dot(mixed_low, w_out[layer_index], precision=HIGH))
        first_norm = normalize(current + branch, norm_params[layer_index, 0], norm_params[layer_index, 1])
        ffn_in = low(first_norm)
        hidden_pre = low_back(jnp.dot(ffn_in, w_in[layer_index], precision=HIGH))
        hidden_low = low(jax.nn.gelu(hidden_pre))
        ffn_out = low_back(jnp.dot(hidden_low, w_back[layer_index], precision=HIGH))
        current = normalize(first_norm + ffn_out, norm_params[layer_index, 2], norm_params[layer_index, 3])
    return current

def reference(stream, seq_lengths, cotangent, w_qkv, w_out, w_in, w_back, norm_params, qkv_master, qkv_first, qkv_second, out_master, out_first, out_second, in_master, in_first, in_second, back_master, back_first, back_second, norm_master, norm_first, norm_second):
    weight_args = (w_qkv.astype(jnp.float32), w_out.astype(jnp.float32), w_in.astype(jnp.float32), w_back.astype(jnp.float32), norm_params.astype(jnp.float32))
    stream_blocks = stream.astype(jnp.float32).reshape(N_WIDE, CAP, D)
    cot_blocks = cotangent.astype(jnp.float32).reshape(N_WIDE, CAP, D)

    def bucket_pass(grad_sums, inputs):
        bucket_in, bucket_cot, lengths = inputs
        segment, cosine, sine = row_layout(lengths, CAP)
        live_rows = (segment >= 0).astype(jnp.float32)

        def run_layers(start_rows, *params):
            return forward(start_rows, *params, segment, cosine, sine)
        bucket_out, pullback = jax.vjp(run_layers, bucket_in, *weight_args)
        cotangents = pullback(bucket_cot * live_rows[:, None])
        grad_sums = tuple((acc + piece for acc, piece in zip(grad_sums, cotangents[1:])))
        return (grad_sums, (bucket_out, cotangents[0]))
    zero_grads = tuple((jnp.zeros(param.shape, jnp.float32) for param in weight_args))
    grad_sums, (outputs_all, input_grads) = lax.scan(bucket_pass, zero_grads, (stream_blocks, cot_blocks, seq_lengths))
    squares = jnp.zeros((), jnp.float32)
    for piece in grad_sums:
        squares = squares + jnp.sum(piece * piece)
    clip_norm = jnp.sqrt(squares)
    factor = jnp.minimum(1.0, CLIP / clip_norm)
    fix_one = 1.0 - BETA_ONE ** STEP_NUMBER
    fix_two = 1.0 - BETA_TWO ** STEP_NUMBER
    qkv_new = adamw(qkv_master, qkv_first, qkv_second, grad_sums[0], factor, fix_one, fix_two, LR_MATRIX, DECAY_MATRIX)
    out_new = adamw(out_master, out_first, out_second, grad_sums[1], factor, fix_one, fix_two, LR_MATRIX, DECAY_MATRIX)
    in_new = adamw(in_master, in_first, in_second, grad_sums[2], factor, fix_one, fix_two, LR_MATRIX, DECAY_MATRIX)
    back_new = adamw(back_master, back_first, back_second, grad_sums[3], factor, fix_one, fix_two, LR_MATRIX, DECAY_MATRIX)
    norm_new = adamw(norm_master, norm_first, norm_second, grad_sums[4], factor, fix_one, fix_two, LR_NORMS, 0.0)
    return (outputs_all.reshape(TOKENS, D), input_grads.reshape(TOKENS, D), qkv_new[0], qkv_new[1], qkv_new[2], out_new[0], out_new[1], out_new[2], in_new[0], in_new[1], in_new[2], back_new[0], back_new[1], back_new[2], norm_new[0], norm_new[1], norm_new[2], clip_norm.reshape(1))
```

```python
import functools
import math

import jax
import jax.numpy as jnp
from jax import lax
from jax.experimental import pallas as pl
from jax.experimental.pallas import tpu as pltpu
from jax.sharding import PartitionSpec as P

HEAD = 64
LAYERS = 2
CHUNK = 256
FF_BLOCK = 512
VMEM = 56 * 1024 * 1024

EPS_NORM = 1e-05
CLIP = 1.0
BETA_ONE = 0.5
BETA_TWO = 0.5
ADAM_EPS = 1e-08
LR_MATRIX = 0.1
LR_NORMS = 0.5
DECAY_MATRIX = 0.1
STEP_NUMBER = 4.0

F32 = jnp.float32
BF16 = jnp.bfloat16


def params(axes=1):
    return pltpu.CompilerParams(
        vmem_limit_bytes=VMEM, dimension_semantics=("arbitrary",) * axes
    )


def cost(flops, nbytes):
    return pl.CostEstimate(flops=int(flops), bytes_accessed=int(nbytes), transcendentals=0)


def dot(a, b):
    return jnp.dot(a, b, preferred_element_type=F32)


def dot_nt(a, b):
    return lax.dot_general(a, b, (((1,), (1,)), ((), ())), preferred_element_type=F32)


def dot_tn(a, b):
    return lax.dot_general(a, b, (((0,), (0,)), ((), ())), preferred_element_type=F32)


def low_lanes(rows):
    return lax.broadcasted_iota(jnp.int32, (rows, 128), 1) < HEAD


def shape(dims, dtype):
    return jax.ShapeDtypeStruct(dims, dtype)


def whole(array_shape):
    return pl.BlockSpec(array_shape, lambda *_: (0,) * len(array_shape))


def row_spec(rows, cols, index=lambda i: i):
    return pl.BlockSpec((rows, cols), lambda i: (index(i), 0))


def layer_spec(array, layer):
    rest = array.shape[1:]
    return pl.BlockSpec((None,) + rest, lambda *_: (layer,) + (0,) * len(rest))


def vext_of(v_pair):
    return jnp.concatenate([v_pair, jnp.ones_like(v_pair)], axis=1)


def project_kernel(x_ref, w_ref, cos_ref, sin_ref, qc_ref, kc_ref, v_ref, kv_ref):
    rows = x_ref.shape[0]
    pairs = v_ref.shape[1] // 128

    @pl.when(pl.program_id(0) == 0)
    def _():
        kv_ref[...] = jnp.zeros_like(kv_ref)

    x = x_ref[...]
    low = low_lanes(rows)
    cos, sin = cos_ref[...], sin_ref[...]

    def features(values, out_ref):
        cats = []
        for pair in range(pairs):
            tile = jnp.maximum(values[:, pair * 128 : pair * 128 + 128], 0.0)
            along = tile * cos
            across = pltpu.roll(tile, HEAD, 1) * sin
            for cat in (jnp.where(low, along, across), jnp.where(low, across, along)):
                cats.append(cat.astype(BF16))
        for head, cat in enumerate(cats):
            out_ref[:, head * 128 : head * 128 + 128] = cat
        return cats

    features(dot(x, w_ref[0]), qc_ref)
    k_cats = features(dot(x, w_ref[1]), kc_ref)
    v = dot(x, w_ref[2]).astype(BF16)
    v_ref[...] = v
    for pair in range(pairs):
        vext = vext_of(v[:, pair * 128 : pair * 128 + 128])
        for head in (2 * pair, 2 * pair + 1):
            kv_ref[head] += dot_tn(k_cats[head], vext)


def project(x, w, layer, cos, sin):
    rows, width = x.shape
    half = w.shape[3]
    heads = half // HEAD
    return pl.pallas_call(
        project_kernel,
        grid=(rows // CHUNK,),
        in_specs=[
            row_spec(CHUNK, width),
            layer_spec(w, layer),
            row_spec(CHUNK, 128),
            row_spec(CHUNK, 128),
        ],
        out_specs=[
            row_spec(CHUNK, heads * 128),
            row_spec(CHUNK, heads * 128),
            row_spec(CHUNK, half),
            whole((heads, 128, 256)),
        ],
        out_shape=[
            shape((rows, heads * 128), BF16),
            shape((rows, heads * 128), BF16),
            shape((rows, half), BF16),
            shape((heads, 128, 256), F32),
        ],
        compiler_params=params(),
        cost_estimate=cost(2 * rows * width * 3 * half, 8e6),
        name="project",
    )(x, w, cos, sin)


def norm_rows(r, gain, shift):
    mean = jnp.mean(r, axis=1, keepdims=True)
    centered = r - mean
    var = jnp.mean(centered * centered, axis=1, keepdims=True)
    rstd = lax.rsqrt(var + EPS_NORM)
    x_hat = centered * rstd
    return x_hat * gain + shift, x_hat, rstd


def attend_kernel(
    flag_ref, qo_ref, qp_ref, ko_ref, kp_ref, vo_ref, vp_ref, kvo_ref, kvp_ref, wo_ref, wp_ref,
    resid_ref, norm_ref,
    mo_ref, mp_ref, rden_ref, first_ref, low_ref, xhat_ref, rstd_ref, state_out_ref,
    state,
):
    rows = qo_ref.shape[0]
    half = vo_ref.shape[1]
    pairs = half // 128
    heads = 2 * pairs

    @pl.when(pl.program_id(0) == 0)
    def _():
        carry = flag_ref[0, 0]
        state[:heads] = kvo_ref[...] * carry
        state[heads:] = kvp_ref[...] * carry

    low = low_lanes(rows)
    row = lax.broadcasted_iota(jnp.int32, (rows, rows), 0)
    col = lax.broadcasted_iota(jnp.int32, (rows, rows), 1)
    causal = col <= row
    branch = None
    for side, (q_ref, k_ref, v_ref, m_ref, w_ref) in enumerate(
        ((qo_ref, ko_ref, vo_ref, mo_ref, wo_ref), (qp_ref, kp_ref, vp_ref, mp_ref, wp_ref))
    ):
        for pair in range(pairs):
            vext = vext_of(v_ref[:, pair * 128 : pair * 128 + 128])
            sums = []
            for head in (2 * pair, 2 * pair + 1):
                at = side * heads + head
                q = q_ref[:, head * 128 : head * 128 + 128]
                k = k_ref[:, head * 128 : head * 128 + 128]
                kv = state[at]
                kv_low = kv.astype(BF16)
                state_out_ref[0, at] = kv_low
                scores = jnp.where(causal, dot_nt(q, k), 0.0).astype(BF16)
                sums.append(
                    dot(
                        jnp.concatenate([scores, q], axis=1),
                        jnp.concatenate([vext, kv_low], axis=0),
                    )
                )
                state[at] = kv + dot_tn(k, vext)
            num = jnp.where(low, sums[0][:, :128], sums[1][:, :128])
            den = jnp.where(low, sums[0][:, 128:], sums[1][:, 128:])
            rden = 1.0 / jnp.maximum(den, 1.0)
            base = side * half + pair * 128
            rden_ref[:, base : base + 128] = rden
            m_ref[:, pair * 128 : pair * 128 + 128] = (num * rden).astype(BF16)
        part = dot(m_ref[...], w_ref[...])
        branch = part if branch is None else branch + part
    r = resid_ref[...].astype(F32) + branch
    y, x_hat, rstd = norm_rows(r, norm_ref[0:1], norm_ref[1:2])
    first_ref[...] = y
    low_ref[...] = y.astype(BF16)
    xhat_ref[...] = x_hat.astype(BF16)
    rstd_ref[...] = rstd


def attend(flag, own, peer, kv_own, kv_peer, w_own, w_peer, layer, resid, norms):
    rows, width = resid.shape
    half = own[2].shape[1]
    heads = half // HEAD
    steps = rows // CHUNK
    cat, narrow = row_spec(CHUNK, heads * 128), row_spec(CHUNK, half)
    full = row_spec(CHUNK, width)
    return pl.pallas_call(
        attend_kernel,
        grid=(steps,),
        in_specs=[
            pl.BlockSpec(memory_space=pltpu.SMEM),
            cat, cat, cat, cat, narrow, narrow,
            whole(kv_own.shape), whole(kv_peer.shape),
            layer_spec(w_own, layer), layer_spec(w_peer, layer),
            full, layer_spec(norms, layer),
        ],
        out_specs=[
            narrow, narrow, full, full, full, full, row_spec(CHUNK, 1),
            pl.BlockSpec((1, 2 * heads, 128, 256), lambda i: (i, 0, 0, 0)),
        ],
        out_shape=[
            shape((rows, half), BF16),
            shape((rows, half), BF16),
            shape((rows, width), F32),
            shape((rows, width), F32),
            shape((rows, width), BF16),
            shape((rows, width), BF16),
            shape((rows, 1), F32),
            shape((steps, 2 * heads, 128, 256), BF16),
        ],
        scratch_shapes=[pltpu.VMEM((2 * heads, 128, 256), F32)],
        compiler_params=params(),
        cost_estimate=cost(rows * width * (2 * width + 8 * CHUNK), 25e6),
        name="attend",
    )(
        flag, own[0], peer[0], own[1], peer[1], own[2], peer[2], kv_own, kv_peer,
        w_own, w_peer, resid, norms,
    )


def gelu_both(u):
    root = math.sqrt(2.0 / math.pi)
    square = u * u
    t = jnp.tanh(u * (root + (root * 0.044715) * square))
    gate = 0.5 + 0.5 * t
    slope = gate + (u * (0.5 - 0.5 * (t * t))) * (root + (3.0 * root * 0.044715) * square)
    return u * gate, slope


def feed_kernel(
    x_ref, first_ref, wio_ref, wip_ref, wbo_ref, wbp_ref, norm_ref,
    ho_ref, hp_ref, slope_ref, out_ref, low_ref, xhat_ref, rstd_ref,
    acc,
):
    step, steps = pl.program_id(0), pl.num_programs(0)
    rows = x_ref.shape[0]

    def side(w_in, w_back, h_ref, fresh):
        def part(i, _):
            at = pl.ds(pl.multiple_of(i * CHUNK, CHUNK), CHUNK)
            act, slope = gelu_both(dot(x_ref[at, :], w_in[...]))
            act = act.astype(BF16)
            h_ref[at, :] = act
            slope_ref[at, :] = slope.astype(BF16)
            acc[at, :] += dot(act, w_back[...])
            return 0

        lax.fori_loop(0, rows // CHUNK, part, 0, unroll=True)

    @pl.when(step == 0)
    def _():
        acc[...] = first_ref[...]

    @pl.when(step < steps // 2)
    def _():
        side(wio_ref, wbo_ref, ho_ref, step == 0)

    @pl.when(step >= steps // 2)
    def _():
        side(wip_ref, wbp_ref, hp_ref, False)

    @pl.when(step == steps - 1)
    def _():
        def part(i, _):
            at = pl.ds(pl.multiple_of(i * CHUNK, CHUNK), CHUNK)
            y, x_hat, rstd = norm_rows(acc[at, :], norm_ref[2:3], norm_ref[3:4])
            out_ref[at, :] = y
            low_ref[at, :] = y.astype(BF16)
            xhat_ref[at, :] = x_hat.astype(BF16)
            rstd_ref[at, :] = rstd
            return 0

        lax.fori_loop(0, rows // CHUNK, part, 0)


def ff_specs(layer, width, blocks):
    own = lambda j: jnp.minimum(j, blocks - 1)
    peer = lambda j: jnp.maximum(j - blocks, 0)
    w_in = [
        pl.BlockSpec((None, width, FF_BLOCK), lambda j, f=f: (layer, 0, f(j))) for f in (own, peer)
    ]
    w_back = [
        pl.BlockSpec((None, FF_BLOCK, width), lambda j, f=f: (layer, f(j), 0)) for f in (own, peer)
    ]
    return own, peer, w_in, w_back


def feed(x, first, wi_own, wi_peer, wb_own, wb_peer, layer, norms):
    rows, width = x.shape
    half = wi_own.shape[2]
    blocks = half // FF_BLOCK
    own, peer, w_in, w_back = ff_specs(layer, width, blocks)
    return pl.pallas_call(
        feed_kernel,
        grid=(2 * blocks,),
        in_specs=[
            whole((rows, width)), whole((rows, width)), *w_in, *w_back, layer_spec(norms, layer)
        ],
        out_specs=[
            pl.BlockSpec((rows, FF_BLOCK), lambda j: (0, own(j))),
            pl.BlockSpec((rows, FF_BLOCK), lambda j: (0, peer(j))),
            pl.BlockSpec((rows, FF_BLOCK), lambda j: (0, j)),
            whole((rows, width)), whole((rows, width)), whole((rows, width)), whole((rows, 1)),
        ],
        out_shape=[
            shape((rows, half), BF16),
            shape((rows, half), BF16),
            shape((rows, 2 * half), BF16),
            shape((rows, width), F32),
            shape((rows, width), BF16),
            shape((rows, width), BF16),
            shape((rows, 1), F32),
        ],
        scratch_shapes=[pltpu.VMEM((rows, width), F32)],
        compiler_params=params(),
        cost_estimate=cost(8 * rows * width * half, 40e6),
        name="feed",
    )(x, first, wi_own, wi_peer, wb_own, wb_peer, norms)


def norm_back(y, x_hat, rstd, gain):
    scaled = y * gain
    mean = jnp.mean(scaled, axis=1, keepdims=True)
    along = jnp.mean(scaled * x_hat, axis=1, keepdims=True)
    gain_grad = jnp.sum(y * x_hat, axis=0, keepdims=True)
    shift_grad = jnp.sum(y, axis=0, keepdims=True)
    return (scaled - mean - x_hat * along) * rstd, gain_grad, shift_grad


def feed_back_kernel(
    up_ref, live_ref, xh2_ref, rs2_ref, xh1_ref, rs1_ref, slope_ref,
    wio_ref, wip_ref, wbo_ref, wbp_ref, norm_ref,
    gf_ref, gho_ref, ghp_ref, first_ref, gb_ref, ng_ref,
    acc,
):
    step, steps = pl.program_id(0), pl.num_programs(0)
    rows = up_ref.shape[0]

    @pl.when(step == 0)
    def _():
        ng_ref[...] = jnp.zeros_like(ng_ref)

        def part(i, _):
            at = pl.ds(pl.multiple_of(i * CHUNK, CHUNK), CHUNK)
            y = up_ref[at, :] * live_ref[at, :]
            grad, gain_grad, shift_grad = norm_back(
                y, xh2_ref[at, :].astype(F32), rs2_ref[at, :], norm_ref[2:3]
            )
            acc[at, :] = grad
            gf_ref[at, :] = grad.astype(BF16)
            ng_ref[2:3] += gain_grad
            ng_ref[3:4] += shift_grad
            return 0

        lax.fori_loop(0, rows // CHUNK, part, 0)

    def side(w_in, w_back, gh_ref):
        def part(i, _):
            at = pl.ds(pl.multiple_of(i * CHUNK, CHUNK), CHUNK)
            act = dot_nt(gf_ref[at, :], w_back[...])
            gh = (act * slope_ref[at, :].astype(F32)).astype(BF16)
            gh_ref[at, :] = gh
            acc[at, :] += dot_nt(gh, w_in[...])
            return 0

        lax.fori_loop(0, rows // CHUNK, part, 0, unroll=True)

    @pl.when(step < steps // 2)
    def _():
        side(wio_ref, wbo_ref, gho_ref)

    @pl.when(step >= steps // 2)
    def _():
        side(wip_ref, wbp_ref, ghp_ref)

    @pl.when(step == steps - 1)
    def _():
        def part(i, _):
            at = pl.ds(pl.multiple_of(i * CHUNK, CHUNK), CHUNK)
            grad, gain_grad, shift_grad = norm_back(
                acc[at, :], xh1_ref[at, :].astype(F32), rs1_ref[at, :], norm_ref[0:1]
            )
            first_ref[at, :] = grad
            gb_ref[at, :] = grad.astype(BF16)
            ng_ref[0:1] += gain_grad
            ng_ref[1:2] += shift_grad
            return 0

        lax.fori_loop(0, rows // CHUNK, part, 0)


def feed_back(
    up, live, xh2, rs2, xh1, rs1, slope, wi_own, wi_peer, wb_own, wb_peer, layer, norms
):
    rows, width = up.shape
    half = wi_own.shape[2]
    blocks = half // FF_BLOCK
    own, peer, w_in, w_back = ff_specs(layer, width, blocks)
    full, thin = whole((rows, width)), whole((rows, 1))
    return pl.pallas_call(
        feed_back_kernel,
        grid=(2 * blocks,),
        in_specs=[
            full, thin, full, thin, full, thin,
            pl.BlockSpec((rows, FF_BLOCK), lambda j: (0, j)),
            *w_in, *w_back, layer_spec(norms, layer),
        ],
        out_specs=[
            full,
            pl.BlockSpec((rows, FF_BLOCK), lambda j: (0, own(j))),
            pl.BlockSpec((rows, FF_BLOCK), lambda j: (0, peer(j))),
            full, full, whole((4, width)),
        ],
        out_shape=[
            shape((rows, width), BF16),
            shape((rows, half), BF16),
            shape((rows, half), BF16),
            shape((rows, width), F32),
            shape((rows, width), BF16),
            shape((4, width), F32),
        ],
        scratch_shapes=[pltpu.VMEM((rows, width), F32)],
        compiler_params=params(),
        cost_estimate=cost(8 * rows * width * half, 45e6),
        name="feed_back",
    )(up, live, xh2, rs2, xh1, rs1, slope, wi_own, wi_peer, wb_own, wb_peer, norms)


def mix_back_kernel(
    gb_ref, wo_ref, wp_ref, rden_ref, mo_ref, mp_ref, qo_ref, qp_ref, gext_ref, dkv_ref
):
    rows = gb_ref.shape[0]
    half = mo_ref.shape[1]
    pairs = half // 128
    heads = 2 * pairs

    @pl.when(pl.program_id(0) == 0)
    def _():
        dkv_ref[...] = jnp.zeros_like(dkv_ref)

    low = low_lanes(rows)
    r = lax.broadcasted_iota(jnp.int32, (256, 256), 0) % 128
    c = lax.broadcasted_iota(jnp.int32, (256, 256), 1)
    spread = jnp.where((r < HEAD) == (c < 128), -1.0 / 128.0, 0.0).astype(BF16)
    gb = gb_ref[...]
    for side, (w_ref, m_ref, q_ref) in enumerate(
        ((wo_ref, mo_ref, qo_ref), (wp_ref, mp_ref, qp_ref))
    ):
        gm = dot_nt(gb, w_ref[...])
        for pair in range(pairs):
            base = side * half + pair * 128
            rden = rden_ref[:, base : base + 128]
            g = gm[:, pair * 128 : pair * 128 + 128] * rden
            m = m_ref[:, pair * 128 : pair * 128 + 128].astype(F32)
            prod = jnp.where(rden < 1.0, g * m, 0.0)
            high = prod.astype(BF16)
            rest = (prod - high.astype(F32)).astype(BF16)
            minus_c = dot(jnp.concatenate([high, rest], axis=1), spread).astype(BF16)
            for odd in (0, 1):
                head = 2 * pair + odd
                at = side * heads + head
                mine = jnp.where(low, 0.0, g) if odd else jnp.where(low, g, 0.0)
                gext = jnp.concatenate(
                    [mine.astype(BF16), minus_c[:, odd * 128 : odd * 128 + 128]], axis=1
                )
                gext_ref[:, at * 256 : at * 256 + 256] = gext
                dkv_ref[at] += dot_tn(q_ref[:, head * 128 : head * 128 + 128], gext)


def mix_back(gb, w_own, w_peer, layer, rden, m_own, m_peer, q_own, q_peer):
    rows, width = gb.shape
    half = m_own.shape[1]
    heads = half // HEAD
    full, narrow, cat = (row_spec(CHUNK, n) for n in (width, half, heads * 128))
    return pl.pallas_call(
        mix_back_kernel,
        grid=(rows // CHUNK,),
        in_specs=[
            full, layer_spec(w_own, layer), layer_spec(w_peer, layer),
            full, narrow, narrow, cat, cat,
        ],
        out_specs=[row_spec(CHUNK, heads * 512), whole((2 * heads, 128, 256))],
        out_shape=[
            shape((rows, heads * 512), BF16),
            shape((2 * heads, 128, 256), F32),
        ],
        compiler_params=params(),
        cost_estimate=cost(3 * rows * width * width, 25e6),
        name="mix_back",
    )(gb, w_own, w_peer, rden, m_own, m_peer, q_own, q_peer)


def attend_back_kernel(
    flag_ref, qo_ref, qp_ref, ko_ref, kp_ref, vo_ref, vp_ref, gext_ref, state_ref, dkv_ref,
    cos_ref, sin_ref,
    go_ref, gp_ref,
    dstate,
):
    rows = qo_ref.shape[0]
    half = vo_ref.shape[1]
    pairs = half // 128
    heads = 2 * pairs

    @pl.when(pl.program_id(0) == 0)
    def _():
        dstate[...] = dkv_ref[...] * flag_ref[0, 0]

    low = low_lanes(rows)
    row = lax.broadcasted_iota(jnp.int32, (rows, rows), 0)
    col = lax.broadcasted_iota(jnp.int32, (rows, rows), 1)
    causal, anti = col <= row, row <= col
    cos, sin = cos_ref[...], sin_ref[...]
    trig_even = jnp.where(low, cos, sin)
    trig_odd = jnp.where(low, sin, cos)
    for side, (q_ref, k_ref, v_ref, out_ref) in enumerate(
        ((qo_ref, ko_ref, vo_ref, go_ref), (qp_ref, kp_ref, vp_ref, gp_ref))
    ):
        for pair in range(pairs):
            vext = vext_of(v_ref[:, pair * 128 : pair * 128 + 128])
            dq, dk, dv = [], [], None
            for odd in (0, 1):
                head = 2 * pair + odd
                at = side * heads + head
                trig = trig_odd if odd else trig_even
                q = q_ref[:, head * 128 : head * 128 + 128]
                k = k_ref[:, head * 128 : head * 128 + 128]
                gext = gext_ref[:, at * 256 : at * 256 + 256]
                back = dstate[at]
                back_low = back.astype(BF16)
                score_t = jnp.where(anti, dot_nt(k, q), 0.0).astype(BF16)
                ds = jnp.where(causal, dot_nt(gext, vext), 0.0).astype(BF16)
                ds_t = jnp.where(anti, dot_nt(vext, gext), 0.0).astype(BF16)
                q_grad = (dot(ds, k) + dot_nt(gext, state_ref[0, at])) * trig
                k_grad = (dot(ds_t, q) + dot_nt(vext, back_low)) * trig
                v_grad = dot(
                    jnp.concatenate([score_t, k], axis=1),
                    jnp.concatenate([gext[:, :128], back_low[:, :128]], axis=0),
                )
                dstate[at] = back + dot_tn(q, gext)
                q_grad = q_grad + pltpu.roll(q_grad, HEAD, 1)
                k_grad = k_grad + pltpu.roll(k_grad, HEAD, 1)
                dq.append(jnp.where(q > 0, q_grad, 0.0))
                dk.append(jnp.where(k > 0, k_grad, 0.0))
                dv = v_grad if dv is None else dv + v_grad
            for kind, value in enumerate(
                (jnp.where(low, dq[0], dq[1]), jnp.where(low, dk[0], dk[1]), dv)
            ):
                base = kind * half + pair * 128
                out_ref[:, base : base + 128] = value.astype(BF16)


def attend_back(flag, own, peer, gext, states, dkv, cos, sin):
    rows = cos.shape[0]
    half = own[2].shape[1]
    heads = half // HEAD
    steps = rows // CHUNK
    back = lambda i: steps - 1 - i
    cat, narrow, trig = (row_spec(CHUNK, n, back) for n in (heads * 128, half, 128))
    return pl.pallas_call(
        attend_back_kernel,
        grid=(steps,),
        in_specs=[
            pl.BlockSpec(memory_space=pltpu.SMEM),
            cat, cat, cat, cat, narrow, narrow,
            row_spec(CHUNK, heads * 512, back),
            pl.BlockSpec((1, 2 * heads, 128, 256), lambda i: (back(i), 0, 0, 0)),
            whole(dkv.shape), trig, trig,
        ],
        out_specs=[row_spec(CHUNK, 3 * half, back)] * 2,
        out_shape=[shape((rows, 3 * half), BF16)] * 2,
        scratch_shapes=[pltpu.VMEM((2 * heads, 128, 256), F32)],
        compiler_params=params(),
        cost_estimate=cost(40 * rows * half * CHUNK, 25e6),
        name="attend_back",
    )(
        flag, own[0], peer[0], own[1], peer[1], own[2], peer[2], gext, states, dkv, cos, sin
    )


def input_back_kernel(go_ref, gp_ref, wo_ref, wp_ref, first_ref, out_ref):
    half = wo_ref.shape[2]
    total = first_ref[...]
    for g_ref, w_ref in ((go_ref, wo_ref), (gp_ref, wp_ref)):
        for kind in range(3):
            total = total + dot_nt(g_ref[:, kind * half : kind * half + half], w_ref[kind])
    out_ref[...] = total


def input_back(g_own, g_peer, w_own, w_peer, layer, first):
    rows, width = first.shape
    third = row_spec(CHUNK, g_own.shape[1])
    full = row_spec(CHUNK, width)
    return pl.pallas_call(
        input_back_kernel,
        grid=(rows // CHUNK,),
        in_specs=[third, third, layer_spec(w_own, layer), layer_spec(w_peer, layer), full],
        out_specs=full,
        out_shape=shape((rows, width), F32),
        compiler_params=params(),
        cost_estimate=cost(4 * rows * width * g_own.shape[1], 15e6),
        name="input_back",
    )(g_own, g_peer, w_own, w_peer, first)


def weight_kernel(a_ref, b_ref, c_ref, d_ref, out_ref):
    out_ref[...] = (dot_tn(a_ref[...], b_ref[...]) + dot_tn(c_ref[...], d_ref[...])).astype(
        out_ref.dtype
    )


def weight_grad(a, b, c, d, block_m, block_n, name):
    rows, m = a.shape
    n = b.shape[1]
    left = pl.BlockSpec((rows, block_m), lambda i, j: (0, i))
    right = pl.BlockSpec((rows, block_n), lambda i, j: (0, j))
    return pl.pallas_call(
        weight_kernel,
        grid=(m // block_m, n // block_n),
        in_specs=[left, right, left, right],
        out_specs=pl.BlockSpec((block_m, block_n), lambda i, j: (i, j)),
        out_shape=shape((m, n), BF16),
        compiler_params=params(2),
        cost_estimate=cost(4 * rows * m * n, 4 * rows * (m + n) + 2 * m * n),
        name=name,
    )(a, b, c, d)


def swap(values):
    return lax.ppermute(values, "narrow", [(0, 1), (1, 0)])


def halve(values, bit, count):
    me = (lax.axis_index("wide") // bit) % 2
    keep = lax.dynamic_index_in_dim(values, me, 0, keepdims=False)
    send = lax.dynamic_index_in_dim(values, 1 - me, 0, keepdims=False)
    got = lax.ppermute(send, "wide", [(i, i ^ bit) for i in range(count)])
    return (keep.astype(F32) + got.astype(F32)).astype(BF16)


def scatter_sum(values, count, bits):
    if bits is None:
        return lax.psum_scatter(values, "wide", scatter_dimension=0, tiled=False)
    order = len(bits)
    rest = values.shape[1:]
    values = values.reshape((2,) * order + rest)
    axes = list(range(order - 1, -1, -1))
    place = {1 << k: order - 1 - k for k in range(order)}
    left = [1 << k for k in range(order - 1, -1, -1)]
    for bit in bits:
        at = left.index(bit)
        values = jnp.moveaxis(values, at, 0)
        left.remove(bit)
        values = halve(values, bit, count)
    return values


def adamw(master, first, second, gradient, factor, step_rate, decay_rate):
    fix_one = 1.0 - BETA_ONE**STEP_NUMBER
    fix_two = 1.0 - BETA_TWO**STEP_NUMBER
    clipped = gradient * factor
    first = BETA_ONE * first + (1.0 - BETA_ONE) * clipped
    second = BETA_TWO * second + (1.0 - BETA_TWO) * clipped * clipped
    update = first / fix_one / (jnp.sqrt(second / fix_two) + ADAM_EPS)
    master = master - step_rate * (update + decay_rate * master)
    return (master, first, second)


def row_tables(lengths, rows):
    index = lax.axis_index("narrow") * rows + jnp.arange(rows, dtype=jnp.int32)
    first_len, second_len = lengths[0], lengths[1]
    in_first = index < first_len
    in_second = (index >= first_len) & (index < first_len + second_len)
    live = (in_first | in_second).astype(F32)
    position = jnp.where(in_second, index - first_len, index)
    span = jnp.where(in_first, first_len, jnp.where(in_second, second_len, 1))
    angle = 0.5 * math.pi * position.astype(F32) / span.astype(F32)
    cos = (jnp.cos(angle) * live)[:, None]
    sin = (jnp.sin(angle) * live)[:, None]
    goes_on = (first_len > rows).astype(F32).reshape(1, 1)
    return (
        jnp.broadcast_to(cos, (rows, 128)),
        jnp.broadcast_to(sin, (rows, 128)),
        live[:, None],
        goes_on,
    )


def shards(
    stream, seq_lengths, cotangent, w_qkv, w_out, w_in, w_back, norm_params,
    qkv_master, qkv_first, qkv_second, out_master, out_first, out_second,
    in_master, in_first, in_second, back_master, back_first, back_second,
    norm_master, norm_first, norm_second,
):
    rows, width = stream.shape
    half = w_qkv.shape[3]
    wide = lax.axis_size("wide")
    narrow = lax.axis_size("narrow")
    bits = [1, 2, 4, 8] if wide == 16 else None
    cos, sin, live, flag = row_tables(seq_lengths[0], rows)

    qkv = jnp.transpose(w_qkv, (0, 2, 1, 3))
    qkv_peer = swap(qkv)
    out_peer, in_peer, back_peer = swap(w_out), swap(w_in), swap(w_back)

    low = stream
    current = stream
    kept = []
    for layer in range(LAYERS):
        *own, kv_own = project(low, qkv, layer, cos, sin)
        *peer, kv_peer = project(low, qkv_peer, layer, cos, sin)
        kv_in_peer = lax.ppermute(kv_own, "narrow", [(0, 1)])
        kv_in_own = lax.ppermute(kv_peer, "narrow", [(0, 1)])
        attn_in_peer = swap(low)
        m_own, m_peer, rden, first, ffn_in, xh1, rs1, states = attend(
            flag, own, peer, kv_in_own, kv_in_peer, w_out, out_peer, layer, current, norm_params
        )
        h_own, h_peer, slope, out, out_low, xh2, rs2 = feed(
            ffn_in, first, w_in, in_peer, w_back, back_peer, layer, norm_params
        )
        kept.append(
            (low, attn_in_peer, own, peer, m_own, swap(m_peer), m_peer, rden, ffn_in, swap(ffn_in), xh1, rs1,
             states, h_own, swap(h_peer), slope, xh2, rs2)
        )
        current, low = out, out_low

    up = cotangent
    chunks = []
    norm_grads = []
    for layer in reversed(range(LAYERS)):
        (low, low_peer, own, peer, m_own, m_got, m_peer, rden, ffn_in, ffn_peer, xh1, rs1,
         states, h_own, h_got, slope, xh2, rs2) = kept[layer]
        alive = live if layer == LAYERS - 1 else jnp.ones_like(live)
        gf, gh_own, gh_peer, grad_first, gb, ng = feed_back(
            up, alive, xh2, rs2, xh1, rs1, slope, w_in, in_peer, w_back, back_peer, layer, norm_params
        )
        gf_got, gh_got, gb_got = swap(gf), swap(gh_peer), swap(gb)
        gext, dkv = mix_back(gb, w_out, out_peer, layer, rden, m_own, m_peer, own[0], peer[0])
        heads = half // HEAD
        dkv_in = lax.ppermute(
            jnp.concatenate([dkv[heads:], dkv[:heads]], axis=0), "narrow", [(1, 0)]
        )
        back_grad = weight_grad(h_own, gf, h_got, gf_got, 512, width, "back_grad")
        in_grad = weight_grad(ffn_in, gh_own, ffn_peer, gh_got, width, 512, "in_grad")
        g_own, g_peer = attend_back(flag, own, peer, gext, states, dkv_in, cos, sin)
        g_got = swap(g_peer)
        up = input_back(g_own, g_peer, qkv, qkv_peer, layer, grad_first)
        out_grad = weight_grad(m_own, gb, m_got, gb_got, half, width, "out_grad")
        qkv_grad = weight_grad(low, g_own, low_peer, g_got, width, half, "qkv_grad")
        qkv_grad = qkv_grad.reshape(wide, width // wide, 3, half)
        back_grad, in_grad, out_grad = (
            g.reshape((wide, g.shape[0] // wide) + g.shape[1:]) for g in (back_grad, in_grad, out_grad)
        )
        chunks.insert(0, [scatter_sum(g, wide, bits).astype(F32) for g in (qkv_grad, out_grad, in_grad, back_grad)])
        norm_grads.insert(0, ng)

    stacked = [jnp.stack([chunks[l][kind] for l in range(LAYERS)]) for kind in range(4)]
    stacked[0] = stacked[0]
    norm_reduced = lax.psum_scatter(
        jnp.stack(norm_grads), ("wide", "narrow"), scatter_dimension=2, tiled=True
    )
    squares = sum(jnp.sum(g * g) for g in stacked + [norm_reduced])
    clip_norm = jnp.sqrt(lax.psum(squares, ("wide", "narrow")))
    factor = jnp.minimum(1.0, CLIP / clip_norm)
    matrix = lambda m, f, s, g: adamw(m, f, s, g, factor, LR_MATRIX, DECAY_MATRIX)
    qkv_new = matrix(qkv_master, qkv_first, qkv_second, stacked[0])
    out_new = matrix(out_master, out_first, out_second, stacked[1])
    in_new = matrix(in_master, in_first, in_second, stacked[2])
    back_new = matrix(back_master, back_first, back_second, stacked[3])
    norm_new = adamw(norm_master, norm_first, norm_second, norm_reduced, factor, LR_NORMS, 0.0)
    return (current, up, *qkv_new, *out_new, *in_new, *back_new, *norm_new, clip_norm.reshape(1))


def solution(mesh):
    rows = P(("wide", "narrow"), None)
    qkv = P(None, "wide", None, "narrow")
    deep = P(None, ("narrow", "wide"), None)
    in_part = P(None, "wide", "narrow")
    norm = P(None, None, ("wide", "narrow"))
    states = (qkv,) * 3 + (deep,) * 3 + (in_part,) * 3 + (deep,) * 3 + (norm,) * 3
    in_specs = (
        rows, P("wide", None), rows,
        P(None, None, None, "narrow"), P(None, "narrow", None), P(None, None, "narrow"),
        P(None, "narrow", None), P(),
    ) + states
    out_specs = (rows, rows) + states + (P(),)
    return jax.shard_map(shards, mesh=mesh, in_specs=in_specs, out_specs=out_specs, check_vma=False)
```

```python
import functools
import math

import jax
import jax.numpy as jnp
from jax import lax
from jax.experimental import pallas as pl
from jax.experimental.pallas import tpu as pltpu
from jax.sharding import Mesh
from jax.sharding import PartitionSpec as P

HEAD = 64
LAYERS = 2
CHUNK = 256
FF_BLOCK = 768
VMEM = 64 * 1024 * 1024 - 128 * 1024
FOLD_WEIGHT = 1e12

EPS_NORM = 1e-05
CLIP = 1.0
BETA_ONE = 0.5
BETA_TWO = 0.5
ADAM_EPS = 1e-08
LR_MATRIX = 0.1
LR_NORMS = 0.5
DECAY_MATRIX = 0.1
STEP_NUMBER = 4.0

F32 = jnp.float32
BF16 = jnp.bfloat16


def run(
    kernel, args, in_specs, out_specs, out_shape, grid, name,
    scratch=(), after=(), aliases=None, weight=0,
):
    count, extra = len(args), len(after)

    def body(*refs):
        kernel(*refs[:count], *refs[count + extra :])

    return pl.pallas_call(
        body,
        grid=grid,
        in_specs=list(in_specs) + [pl.BlockSpec(memory_space=pl.ANY)] * extra,
        out_specs=out_specs,
        out_shape=out_shape,
        scratch_shapes=list(scratch),
        input_output_aliases=aliases or {},
        compiler_params=pltpu.CompilerParams(
            vmem_limit_bytes=VMEM, dimension_semantics=("arbitrary",) * len(grid)
        ),
        cost_estimate=pl.CostEstimate(
            flops=int(weight), bytes_accessed=int(weight), transcendentals=0
        ),
        name=name,
    )(*args, *after)


def dot(a, b):
    return jnp.dot(a, b, preferred_element_type=F32)


def dot_nt(a, b):
    return lax.dot_general(a, b, (((1,), (1,)), ((), ())), preferred_element_type=F32)


def dot_tn(a, b):
    return lax.dot_general(a, b, (((0,), (0,)), ((), ())), preferred_element_type=F32)


def low_lanes(rows):
    return lax.broadcasted_iota(jnp.int32, (rows, 128), 1) < HEAD


def shape(dims, dtype):
    return jax.ShapeDtypeStruct(dims, dtype)


IN_SMEM = pl.BlockSpec(memory_space=pltpu.SMEM)


def whole(array_shape):
    return pl.BlockSpec(array_shape, lambda *_: (0,) * len(array_shape))


def row_spec(rows, cols, index=lambda i: i):
    return pl.BlockSpec((rows, cols), lambda i: (index(i), 0))


def layer_spec(array, layer):
    rest = array.shape[1:]
    return pl.BlockSpec((None,) + rest, lambda *_: (layer,) + (0,) * len(rest))


def vext_of(v_pair):
    return jnp.concatenate([v_pair, jnp.ones_like(v_pair)], axis=1)


def project_kernel(x_ref, *refs):
    sides = (len(refs) - 3) // 4
    weights, (cos_ref, sin_ref) = refs[:sides], refs[sides : sides + 2]
    outs, kv_ref = refs[sides + 2 : -1], refs[-1]
    rows = x_ref.shape[0]
    x = x_ref[...]
    low = low_lanes(rows)
    cos, sin = cos_ref[...], sin_ref[...]
    first = pl.program_id(0) == 0

    def features(values, out_ref):
        for pair in range(values.shape[1] // 128):
            tile = jnp.maximum(values[:, pair * 128 : pair * 128 + 128], 0.0)
            along = tile * cos
            across = pltpu.roll(tile, HEAD, 1) * sin
            base = pair * 256
            out_ref[:, base : base + 128] = jnp.where(low, along, across).astype(BF16)
            out_ref[:, base + 128 : base + 256] = jnp.where(low, across, along).astype(BF16)

    for side in range(sides):
        w_ref = weights[side]
        q_ref, k_ref, v_ref = outs[3 * side : 3 * side + 3]
        other = sides - 1 - side
        v = dot(x, w_ref[2]).astype(BF16)
        v_ref[...] = v
        features(dot(x, w_ref[1]), k_ref)
        features(dot(x, w_ref[0]), q_ref)
        for pair in range(v.shape[1] // 128):
            both = dot_tn(
                k_ref[:, pair * 256 : pair * 256 + 256],
                vext_of(v[:, pair * 128 : pair * 128 + 128]),
            )
            for odd in (0, 1):
                part = both[odd * 128 : odd * 128 + 128]
                head = 2 * pair + odd
                kv_ref[other, head] = jnp.where(first, part, kv_ref[other, head] + part)


def project(x, weights, layer, cos, sin, after=()):
    rows, width = x.shape
    half = weights[0].shape[3]
    heads = half // HEAD
    block = rows // 2
    cat = row_spec(block, heads * 128)
    return run(
        project_kernel,
        (x, *weights, cos, sin),
        [row_spec(block, width)]
        + [layer_spec(w, layer) for w in weights]
        + [row_spec(block, 128)] * 2,
        [cat, cat, row_spec(block, half)] * len(weights)
        + [whole((len(weights), heads, 128, 256))],
        [
            shape((rows, heads * 128), BF16),
            shape((rows, heads * 128), BF16),
            shape((rows, half), BF16),
        ]
        * len(weights)
        + [shape((len(weights), heads, 128, 256), F32)],
        (rows // block,),
        "project",
        (),
        after,
    )


def norm_rows(r, gain, shift):
    mean = jnp.mean(r, axis=1, keepdims=True)
    centered = r - mean
    var = jnp.mean(centered * centered, axis=1, keepdims=True)
    rstd = lax.rsqrt(var + EPS_NORM)
    x_hat = centered * rstd
    return x_hat * gain + shift, x_hat, rstd


def attend_kernel(
    flag_ref, qo_ref, qp_ref, ko_ref, kp_ref, vo_ref, vp_ref, kvo_ref, kvp_ref, wo_ref, wp_ref,
    resid_ref, norm_ref,
    mo_ref, mp_ref, rden_ref, first_ref, low_ref, xhat_ref, rstd_ref, state_out_ref,
    state,
):
    rows = qo_ref.shape[0]
    half = vo_ref.shape[1]
    pairs = half // 128
    heads = 2 * pairs

    @pl.when(pl.program_id(0) == 0)
    def _():
        carry = flag_ref[0, 0]
        state[:heads] = kvo_ref[...] * carry
        state[heads:] = kvp_ref[...] * carry

    low = low_lanes(rows)
    row = lax.broadcasted_iota(jnp.int32, (rows, rows), 0)
    col = lax.broadcasted_iota(jnp.int32, (rows, rows), 1)
    causal = col <= row
    branch = None
    for side, (q_ref, k_ref, v_ref, m_ref, w_ref) in enumerate(
        ((qo_ref, ko_ref, vo_ref, mo_ref, wo_ref), (qp_ref, kp_ref, vp_ref, mp_ref, wp_ref))
    ):
        for pair in range(pairs):
            vext = vext_of(v_ref[:, pair * 128 : pair * 128 + 128])
            sums = []
            for head in (2 * pair, 2 * pair + 1):
                at = side * heads + head
                q = q_ref[:, head * 128 : head * 128 + 128]
                k = k_ref[:, head * 128 : head * 128 + 128]
                kv = state[at]
                kv_low = kv.astype(BF16)
                state_out_ref[0, at] = kv_low
                scores = jnp.where(causal, dot_nt(q, k), 0.0).astype(BF16)
                sums.append(
                    dot(
                        jnp.concatenate([scores, q], axis=1),
                        jnp.concatenate([vext, kv_low], axis=0),
                    )
                )
                state[at] = kv + dot_tn(k, vext)
            num = jnp.where(low, sums[0][:, :128], sums[1][:, :128])
            den = jnp.where(low, sums[0][:, 128:], sums[1][:, 128:])
            rden = 1.0 / jnp.maximum(den, 1.0)
            base = side * half + pair * 128
            rden_ref[:, base : base + 128] = rden
            m_ref[:, pair * 128 : pair * 128 + 128] = (num * rden).astype(BF16)
        part = dot(m_ref[...], w_ref[...])
        branch = part if branch is None else branch + part
    r = resid_ref[...].astype(F32) + branch
    y, x_hat, rstd = norm_rows(r, norm_ref[0:1], norm_ref[1:2])
    first_ref[...] = y
    low_ref[...] = y.astype(BF16)
    xhat_ref[...] = x_hat.astype(BF16)
    rstd_ref[...] = jnp.broadcast_to(rstd, rstd_ref.shape)


def attend(flag, own, peer, kv, kv_at, w_own, w_peer, layer, resid, norms, after=()):
    rows, width = resid.shape
    half = own[2].shape[1]
    heads = half // HEAD
    steps = rows // CHUNK
    cat, narrow = row_spec(CHUNK, heads * 128), row_spec(CHUNK, half)
    full = row_spec(CHUNK, width)
    return run(
        attend_kernel,
        (flag, own[0], peer[0], own[1], peer[1], own[2], peer[2], *kv,
         w_own, w_peer, resid, norms),
        [
            IN_SMEM,
            cat, cat, cat, cat, narrow, narrow,
            *(pl.BlockSpec((None,) + a.shape[1:], lambda *_, n=n: (n, 0, 0, 0)) for a, n in zip(kv, kv_at)),
            layer_spec(w_own, layer), layer_spec(w_peer, layer),
            full, layer_spec(norms, layer),
        ],
        [
            narrow, narrow, full, full, full, full, row_spec(CHUNK, 128),
            pl.BlockSpec((1, 2 * heads, 128, 256), lambda i: (i, 0, 0, 0)),
        ],
        [
            shape((rows, half), BF16),
            shape((rows, half), BF16),
            shape((rows, width), F32),
            shape((rows, width), F32),
            shape((rows, width), BF16),
            shape((rows, width), BF16),
            shape((rows, 128), F32),
            shape((steps, 2 * heads, 128, 256), BF16),
        ],
        (steps,),
        "attend",
        [pltpu.VMEM((2 * heads, 128, 256), F32)],
        after,
    )


def gelu_both(u):
    root = math.sqrt(2.0 / math.pi)
    a = root + (root * 0.044715) * (u * u)
    gate = 0.5 + 0.5 * jnp.tanh(u * a)
    act = u * gate
    return act, gate + (act - act * gate) * (6.0 * a - 4.0 * root)


def feed_kernel(
    x_ref, first_ref, wio_ref, wip_ref, wbo_ref, wbp_ref, norm_ref,
    ho_ref, hp_ref, slope_ref, out_ref, low_ref, xhat_ref, rstd_ref,
    acc,
):
    step, steps = pl.program_id(0), pl.num_programs(0)
    rows = x_ref.shape[0]

    def side(w_in, w_back, h_ref, base):
        for i in range(rows // CHUNK):
            at = slice(i * CHUNK, i * CHUNK + CHUNK)
            act, slope = gelu_both(dot(x_ref[at, :], w_in[...]))
            act = act.astype(BF16)
            h_ref[at, :] = act
            slope_ref[at, :] = slope.astype(BF16)
            acc[at, :] = base[at, :] + dot(act, w_back[...])

    @pl.when(step == 0)
    def _():
        side(wio_ref, wbo_ref, ho_ref, first_ref)

    @pl.when((step > 0) & (step < steps // 2))
    def _():
        side(wio_ref, wbo_ref, ho_ref, acc)

    @pl.when(step >= steps // 2)
    def _():
        side(wip_ref, wbp_ref, hp_ref, acc)

    @pl.when(step == steps - 1)
    def _():
        def part(i, _):
            at = pl.ds(pl.multiple_of(i * CHUNK, CHUNK), CHUNK)
            y, x_hat, rstd = norm_rows(acc[at, :], norm_ref[2:3], norm_ref[3:4])
            out_ref[at, :] = y
            low_ref[at, :] = y.astype(BF16)
            xhat_ref[at, :] = x_hat.astype(BF16)
            rstd_ref[at, :] = jnp.broadcast_to(rstd, (CHUNK, 128))
            return 0

        lax.fori_loop(0, rows // CHUNK, part, 0)


def ff_specs(layer, width, blocks):
    own = lambda j: jnp.minimum(j, blocks - 1)
    peer = lambda j: jnp.maximum(j - blocks, 0)
    w_in = [
        pl.BlockSpec((None, width, FF_BLOCK), lambda j, f=f: (layer, 0, f(j))) for f in (own, peer)
    ]
    w_back = [
        pl.BlockSpec((None, FF_BLOCK, width), lambda j, f=f: (layer, f(j), 0)) for f in (own, peer)
    ]
    return own, peer, w_in, w_back


def feed(x, first, wi_own, wi_peer, wb_own, wb_peer, layer, norms, last, after=()):
    rows, width = x.shape
    half = wi_own.shape[2]
    blocks = half // FF_BLOCK
    own, peer, w_in, w_back = ff_specs(layer, width, blocks)
    full = whole((rows, width))
    return run(
        feed_kernel,
        (x, first, wi_own, wi_peer, wb_own, wb_peer, norms),
        [full, full, *w_in, *w_back, layer_spec(norms, layer)],
        [
            pl.BlockSpec((rows, FF_BLOCK), lambda j: (0, own(j))),
            pl.BlockSpec((rows, FF_BLOCK), lambda j: (0, peer(j))),
            pl.BlockSpec((rows, FF_BLOCK), lambda j: (0, j)),
            full, full, full, whole((rows, 128)),
        ],
        [
            shape((rows, half), BF16),
            shape((rows, half), BF16),
            shape((rows, 2 * half), BF16),
            shape((rows, width), F32),
            shape((rows, width), BF16),
            shape((rows, width), BF16),
            shape((rows, 128), F32),
        ],
        (2 * blocks,),
        "feed",
        [pltpu.VMEM((rows, width), F32)],
        after,
    )


def norm_back(y, x_hat, rstd, gain):
    scaled = y * gain
    mean = jnp.mean(scaled, axis=1, keepdims=True)
    along = jnp.mean(scaled * x_hat, axis=1, keepdims=True)
    gain_grad = jnp.sum(y * x_hat, axis=0, keepdims=True)
    shift_grad = jnp.sum(y, axis=0, keepdims=True)
    return (scaled - mean - x_hat * along) * rstd, gain_grad, shift_grad


def feed_back_kernel(
    up_ref, live_ref, xh2_ref, rs2_ref, xh1_ref, rs1_ref, slope_ref,
    wio_ref, wip_ref, wbo_ref, wbp_ref, norm_ref,
    gfb_ref, gho_ref, ghp_ref, first_ref, ng_ref,
    acc,
):
    step, steps = pl.program_id(0), pl.num_programs(0)
    rows, width = up_ref.shape
    tiles = width // 128

    def chunk(i):
        return pl.ds(pl.multiple_of(i * CHUNK, CHUNK), CHUNK)

    def wide(ref, at):
        return jnp.concatenate([ref[at, :]] * tiles, axis=1)

    @pl.when(step == 0)
    def _():
        ng_ref[...] = jnp.zeros_like(ng_ref)

        def part(i, _):
            at = chunk(i)
            y = up_ref[at, :]
            if live_ref is not None:
                y = y * wide(live_ref, at)
            grad, gain_grad, shift_grad = norm_back(
                y, xh2_ref[at, :].astype(F32), wide(rs2_ref, at), norm_ref[2:3]
            )
            acc[at, :] = grad
            gfb_ref[0, at, :] = grad.astype(BF16)
            ng_ref[2:3] += gain_grad
            ng_ref[3:4] += shift_grad
            return 0

        lax.fori_loop(0, rows // CHUNK, part, 0)

    def side(w_in, w_back, gh_ref):
        for i in range(rows // CHUNK):
            at = slice(i * CHUNK, i * CHUNK + CHUNK)
            act = dot_nt(gfb_ref[0, at, :], w_back[...])
            gh = (act * slope_ref[at, :].astype(F32)).astype(BF16)
            gh_ref[at, :] = gh
            acc[at, :] += dot_nt(gh, w_in[...])

    @pl.when(step < steps // 2)
    def _():
        side(wio_ref, wbo_ref, gho_ref)

    @pl.when(step >= steps // 2)
    def _():
        side(wip_ref, wbp_ref, ghp_ref)

    @pl.when(step == steps - 1)
    def _():
        def part(i, _):
            at = chunk(i)
            grad, gain_grad, shift_grad = norm_back(
                acc[at, :], xh1_ref[at, :].astype(F32), wide(rs1_ref, at), norm_ref[0:1]
            )
            first_ref[at, :] = grad
            gfb_ref[1, at, :] = grad.astype(BF16)
            ng_ref[0:1] += gain_grad
            ng_ref[1:2] += shift_grad
            return 0

        lax.fori_loop(0, rows // CHUNK, part, 0)


def feed_back(
    up, live, xh2, rs2, xh1, rs1, slope, wi_own, wi_peer, wb_own, wb_peer, layer, norms, after=()
):
    rows, width = up.shape
    half = wi_own.shape[2]
    blocks = half // FF_BLOCK
    own, peer, w_in, w_back = ff_specs(layer, width, blocks)
    full, thin = whole((rows, width)), whole((rows, 128))
    if live is None:

        def kernel(up_ref, *refs):
            feed_back_kernel(up_ref, None, *refs)

        args, specs = (up,), [full]
    else:
        kernel, args, specs = feed_back_kernel, (up, live), [full, thin]
    return run(
        kernel,
        args + (xh2, rs2, xh1, rs1, slope, wi_own, wi_peer, wb_own, wb_peer, norms),
        specs
        + [
            full, thin, full, thin,
            pl.BlockSpec((rows, FF_BLOCK), lambda j: (0, j)),
            *w_in, *w_back, layer_spec(norms, layer),
        ],
        [
            whole((2, rows, width)),
            pl.BlockSpec((rows, FF_BLOCK), lambda j: (0, own(j))),
            pl.BlockSpec((rows, FF_BLOCK), lambda j: (0, peer(j))),
            full, whole((4, width)),
        ],
        [
            shape((2, rows, width), BF16),
            shape((rows, half), BF16),
            shape((rows, half), BF16),
            shape((rows, width), F32),
            shape((4, width), F32),
        ],
        (2 * blocks,),
        "feed_back",
        [pltpu.VMEM((rows, width), F32)],
        after,
    )


def mix_back_kernel(
    gfb_ref, wo_ref, wp_ref, rden_ref, mo_ref, mp_ref, qo_ref, qp_ref, gx_ref, dkv_ref
):
    rows = gfb_ref.shape[0]
    half = mo_ref.shape[1]
    pairs = half // 128
    first = pl.program_id(0) == 0
    wide_low = jnp.concatenate([low_lanes(rows)] * 2, axis=1)
    r = lax.broadcasted_iota(jnp.int32, (256, 128), 0) % 128
    c = lax.broadcasted_iota(jnp.int32, (256, 128), 1)
    spread_c = jnp.where((r < HEAD) == (c < HEAD), -1.0 / HEAD, 0.0).astype(BF16)
    gb = gfb_ref[...]
    for side, (w_ref, m_ref, q_ref) in enumerate(
        ((wo_ref, mo_ref, qo_ref), (wp_ref, mp_ref, qp_ref))
    ):
        gm = dot_nt(gb, w_ref[...])
        for pair in range(pairs):
            base = side * half + pair * 128
            rden = rden_ref[:, base : base + 128]
            g = gm[:, pair * 128 : pair * 128 + 128] * rden
            m = m_ref[:, pair * 128 : pair * 128 + 128].astype(F32)
            prod = jnp.where(rden < 1.0, g * m, 0.0)
            high = prod.astype(BF16)
            rest = (prod - high.astype(F32)).astype(BF16)
            minus_c = dot(jnp.concatenate([high, rest], axis=1), spread_c).astype(BF16)
            gx = jnp.concatenate([g.astype(BF16), minus_c], axis=1)
            gx_ref[:, 2 * base : 2 * base + 256] = gx
            for odd in (0, 1):
                at = side * 2 * pairs + 2 * pair + odd
                part = dot_tn(
                    q_ref[:, (2 * pair + odd) * 128 : (2 * pair + odd) * 128 + 128],
                    own_lanes(gx, wide_low, odd),
                )
                dkv_ref[at] = jnp.where(first, part, dkv_ref[at] + part)


def own_lanes(gx, wide_low, odd):
    zero = jnp.zeros_like(gx)
    return jnp.where(wide_low, zero, gx) if odd else jnp.where(wide_low, gx, zero)


def mix_back(gfb, w_own, w_peer, layer, rden, m_own, m_peer, q_own, q_peer, after=()):
    _, rows, width = gfb.shape
    half = m_own.shape[1]
    heads = half // HEAD
    full, narrow, cat = (row_spec(CHUNK, n) for n in (width, half, heads * 128))
    return run(
        mix_back_kernel,
        (gfb, w_own, w_peer, rden, m_own, m_peer, q_own, q_peer),
        [
            pl.BlockSpec((None, CHUNK, width), lambda i: (1, i, 0)),
            layer_spec(w_own, layer), layer_spec(w_peer, layer),
            full, narrow, narrow, cat, cat,
        ],
        [row_spec(CHUNK, 2 * width), whole((2 * heads, 128, 256))],
        [
            shape((rows, 2 * width), BF16),
            shape((2 * heads, 128, 256), F32),
        ],
        (rows // CHUNK,),
        "mix_back",
        (),
        after,
    )


def attend_back_kernel(
    flag_ref, qo_ref, qp_ref, ko_ref, kp_ref, vo_ref, vp_ref, gx_ref, state_ref, dkv_ref,
    cos_ref, sin_ref,
    go_ref, gp_ref,
    dstate,
):
    rows = qo_ref.shape[0]
    half = vo_ref.shape[1]
    pairs = half // 128
    heads = 2 * pairs

    @pl.when(pl.program_id(0) == 0)
    def _():
        carry = flag_ref[0, 0]
        dstate[:heads] = dkv_ref[heads:] * carry
        dstate[heads:] = dkv_ref[:heads] * carry

    low = low_lanes(rows)
    wide_low = jnp.concatenate([low, low], axis=1)
    row = lax.broadcasted_iota(jnp.int32, (rows, rows), 0)
    col = lax.broadcasted_iota(jnp.int32, (rows, rows), 1)
    causal, anti = col <= row, row <= col
    cos, sin = cos_ref[...], sin_ref[...]
    trig_even = jnp.where(low, cos, sin)
    trig_odd = jnp.where(low, sin, cos)
    for side, (q_ref, k_ref, v_ref, out_ref) in enumerate(
        ((qo_ref, ko_ref, vo_ref, go_ref), (qp_ref, kp_ref, vp_ref, gp_ref))
    ):
        for pair in range(pairs):
            vext = vext_of(v_ref[:, pair * 128 : pair * 128 + 128])
            wide = 2 * (side * half + pair * 128)
            gx = gx_ref[:, wide : wide + 256]
            dq, dk, left, right = [], [], [], []
            for odd in (0, 1):
                head = 2 * pair + odd
                at = side * heads + head
                trig = trig_odd if odd else trig_even
                q = q_ref[:, head * 128 : head * 128 + 128]
                k = k_ref[:, head * 128 : head * 128 + 128]
                gext = own_lanes(gx, wide_low, odd)
                back = dstate[at]
                back_low = back.astype(BF16)
                score_t = jnp.where(anti, dot_nt(k, q), 0.0).astype(BF16)
                ds = jnp.where(causal, dot_nt(gext, vext), 0.0).astype(BF16)
                q_grad = (dot(ds, k) + dot_nt(gext, state_ref[0, at])) * trig
                k_grad = (dot_tn(ds, q) + dot_nt(vext, back_low)) * trig
                left += [score_t, k]
                right += [gext[:, :128], back_low[:, :128]]
                dstate[at] = back + dot_tn(q, gext)
                q_grad = q_grad + pltpu.roll(q_grad, HEAD, 1)
                k_grad = k_grad + pltpu.roll(k_grad, HEAD, 1)
                dq.append(jnp.where(q > 0, q_grad, 0.0))
                dk.append(jnp.where(k > 0, k_grad, 0.0))
            dv = dot(jnp.concatenate(left, axis=1), jnp.concatenate(right, axis=0))
            for kind, value in enumerate(
                (jnp.where(low, dq[0], dq[1]), jnp.where(low, dk[0], dk[1]), dv)
            ):
                base = kind * half + pair * 128
                out_ref[:, base : base + 128] = value.astype(BF16)


def attend_back(flag, own, peer, gx, states, dkv, cos, sin, after=()):
    rows = cos.shape[0]
    half = own[2].shape[1]
    heads = half // HEAD
    steps = rows // CHUNK
    back = lambda i: steps - 1 - i
    cat, narrow, trig = (row_spec(CHUNK, n, back) for n in (heads * 128, half, 128))
    return run(
        attend_back_kernel,
        (flag, own[0], peer[0], own[1], peer[1], own[2], peer[2], gx, states, dkv, cos, sin),
        [
            IN_SMEM,
            cat, cat, cat, cat, narrow, narrow,
            row_spec(CHUNK, heads * 256, back),
            pl.BlockSpec((1, 2 * heads, 128, 256), lambda i: (back(i), 0, 0, 0)),
            whole(dkv.shape), trig, trig,
        ],
        [row_spec(CHUNK, 3 * half, back)] * 2,
        [shape((rows, 3 * half), BF16)] * 2,
        (steps,),
        "attend_back",
        [pltpu.VMEM((2 * heads, 128, 256), F32)],
        after,
    )


def input_back_kernel(go_ref, gp_ref, wo_ref, wp_ref, first_ref, out_ref):
    half = wo_ref.shape[2]
    total = first_ref[...]
    for g_ref, w_ref in ((go_ref, wo_ref), (gp_ref, wp_ref)):
        for kind in range(3):
            total = total + dot_nt(g_ref[:, kind * half : kind * half + half], w_ref[kind])
    out_ref[...] = total


def input_back(g_own, g_peer, w_own, w_peer, layer, first, after=()):
    rows, width = first.shape
    block = rows // 2
    third, full = row_spec(block, g_own.shape[1]), row_spec(block, width)
    return run(
        input_back_kernel,
        (g_own, g_peer, w_own, w_peer, first),
        [third, third, layer_spec(w_own, layer), layer_spec(w_peer, layer), full],
        full,
        shape((rows, width), F32),
        (rows // block,),
        "input_back",
        (),
        after,
    )


def weight_kernel(a_ref, b_ref, c_ref, d_ref, out_ref):
    out_ref[...] = (dot_tn(a_ref[...], b_ref[...]) + dot_tn(c_ref[...], d_ref[...])).astype(
        out_ref.dtype
    )


def weight_grad(a, b, c, d, block_m, block_n, name):
    rows, m = a.shape
    n = b.shape[1]
    left = pl.BlockSpec((rows, block_m), lambda i, j: (0, i))
    right = pl.BlockSpec((rows, block_n), lambda i, j: (0, j))
    return run(
        weight_kernel,
        (a, b, c, d),
        [left, right, left, right],
        pl.BlockSpec((block_m, block_n), lambda i, j: (i, j)),
        shape((m, n), BF16),
        (m // block_m, n // block_n),
        name,
    )


FF_ROWS = 224
Q_ROWS = 144


def blocks_of(index_ref, scr, rows, z_local, x_first, other, kept):
    x, y = index_ref[0, 0], index_ref[0, 1]
    if x_first:
        spot = other * 2 + (x if kept else 1 - x)
    else:
        spot = (y if kept else 1 - y) * 2 + other
    start = pl.multiple_of((z_local * 4 + spot) * rows, 8)
    return scr[pl.ds(start, rows), :]


def back_pack_kernel(index_ref, a_ref, b_ref, c_ref, d_ref, ka, sa, kb, sb, scr):
    rows = scr.shape[0] // 4
    scr[...] = dot_tn(a_ref[...], b_ref[...]) + dot_tn(c_ref[...], d_ref[...])
    z = pl.program_id(0)
    for x_first, (keep, send) in ((True, (ka, sa)), (False, (kb, sb))):

        @pl.when((z < 2) == x_first)
        def _():
            for other in range(2):
                for kept, out in ((True, keep), (False, send)):
                    out[0, other] = blocks_of(
                        index_ref, scr, rows, 0, x_first, other, kept
                    ).astype(BF16)


def half_spec(array, at):
    return pl.BlockSpec((None,) + array.shape[1:], lambda *_: (at, 0, 0))


def back_pack(index, a, b, c, d, after=()):
    rows, m = a.shape
    n = b.shape[2]
    block = m // 4
    left = pl.BlockSpec((rows, block), lambda z: (0, z))
    buffer = shape((2, 2, FF_ROWS, n), BF16)
    low = pl.BlockSpec((1, 2, block // 4, n), lambda z: (jnp.minimum(z, 1), 0, 0, 0))
    high = pl.BlockSpec((1, 2, block // 4, n), lambda z: (jnp.maximum(z - 2, 0), 0, 0, 0))
    return run(
        back_pack_kernel,
        (index, a, b, c, d),
        [IN_SMEM, left, half_spec(b, 0), left, half_spec(d, 0)],
        [low, low, high, high],
        [buffer] * 4,
        (4,),
        "back_grad",
        [pltpu.VMEM((block, n), F32)],
        after,
    )


def spread(index_ref, scr, rows, outs, tail=None):
    ka, sa, kb, sb = outs
    for x_first, keep, send in ((True, ka, sa), (False, kb, sb)):
        for z in range(2):
            z_local = z if x_first else z + 2
            for other in range(2):
                for kept, out in ((True, keep), (False, send)):
                    value = blocks_of(index_ref, scr, rows, z_local, x_first, other, kept)
                    if tail is not None:
                        x, y = index_ref[0, 0], index_ref[0, 1]
                        if x_first:
                            w = z_local * 4 + other * 2 + (x if kept else 1 - x)
                        else:
                            w = z_local * 4 + (y if kept else 1 - y) * 2 + other
                        value = jnp.concatenate([value, tail(w)], axis=0)
                    out[z, other] = value.astype(BF16)


def in_pack_kernel(index_ref, a_ref, b_ref, c_ref, d_ref, _ka, _sa, _kb, _sb, ka, sa, kb, sb, scr):
    scr[...] = dot_tn(a_ref[...], b_ref[...]) + dot_tn(c_ref[...], d_ref[...])
    spread(index_ref, scr, scr.shape[0] // 16, (ka, sa, kb, sb))


def column_pack(index, a, b, c, d, buffers, block_n, block_rows, first_block, name, after=()):
    rows, m = a.shape
    n = b.shape[1]
    right = pl.BlockSpec((rows, block_n), lambda j: (0, j))
    out = pl.BlockSpec((2, 2, m // 16, block_n), lambda j: (0, 0, first_block + j, 0))
    specs = [IN_SMEM, whole(a.shape), right, whole(c.shape), right]
    scratch = [pltpu.VMEM((m, block_n), F32)]
    if buffers is None:

        def fresh(index_ref, a_ref, b_ref, c_ref, d_ref, *outs):
            in_pack_kernel(index_ref, a_ref, b_ref, c_ref, d_ref, *([None] * 4), *outs)

        return run(
            fresh, (index, a, b, c, d), specs, [out] * 4,
            [shape((2, 2, block_rows, block_n), BF16)] * 4, (n // block_n,), name, scratch, after,
        )
    return run(
        in_pack_kernel,
        (index, a, b, c, d, *buffers),
        specs + [pl.BlockSpec(memory_space=pl.ANY)] * 4,
        [out] * 4,
        [shape(buffer.shape, BF16) for buffer in buffers],
        (n // block_n,),
        name,
        scratch,
        after,
        {5 + i: i for i in range(4)},
    )


def out_pack_kernel(
    index_ref, a_ref, b_ref, c_ref, d_ref, norm_ref, _ka, _sa, _kb, _sb, ka, sa, kb, sb, scr
):
    scr[...] = dot_tn(a_ref[...], b_ref[...]) + dot_tn(c_ref[...], d_ref[...])
    blank = jnp.zeros((8, scr.shape[1] - 128), F32)
    spread(
        index_ref, scr, scr.shape[0] // 16, (ka, sa, kb, sb),
        lambda w: jnp.concatenate([norm_ref[w], blank], axis=1),
    )


def out_pack(index, a, b, c, d, norms, buffers, after=()):
    m, n = a.shape[1], b.shape[2]
    block = m // 16 + 8
    out = pl.BlockSpec((2, 2, block, n), lambda j: (0, 0, (FF_ROWS - block) // block, 0))
    return run(
        out_pack_kernel,
        (index, a, b, c, d, norms, *buffers),
        [IN_SMEM, whole(a.shape), half_spec(b, 1), whole(c.shape), half_spec(d, 1)]
        + [whole(norms.shape)]
        + [pl.BlockSpec(memory_space=pl.ANY)] * 4,
        [out] * 4,
        [shape(buffer.shape, BF16) for buffer in buffers],
        (1,),
        "out_grad",
        [pltpu.VMEM((m, n), F32)],
        after,
        {6 + i: i for i in range(4)},
    )


def swap(values, axis="narrow"):
    return lax.ppermute(values, axis, [(0, 1), (1, 0)])


def sum_of(a_ref, b_ref, *at):
    return (a_ref[at].astype(F32) + b_ref[at].astype(F32)).astype(BF16)


def fold_split_kernel(index_ref, ka, ga, kb, gb, ka_out, sa_out, kb_out, sb_out):
    x, y = index_ref[0, 0], index_ref[0, 1]
    ka_out[0] = sum_of(ka, ga, 0, y)
    sa_out[0] = sum_of(ka, ga, 0, 1 - y)
    kb_out[0] = sum_of(kb, gb, 0, x)
    sb_out[0] = sum_of(kb, gb, 0, 1 - x)


def fold_split(index, ka, ga, kb, gb, after=()):
    _, _, r, c = ka.shape
    return run(
        fold_split_kernel,
        (index, ka, ga, kb, gb),
        [IN_SMEM]
        + [pl.BlockSpec((1, 2, r, c), lambda z: (z, 0, 0, 0))] * 4,
        [pl.BlockSpec((1, r, c), lambda z: (z, 0, 0))] * 4,
        [shape((2, r, c), BF16)] * 4,
        (2,),
        "fold_split",
        (),
        after,
        weight=FOLD_WEIGHT,
    )


def fold_join_kernel(ka, ga, kb, gb, out):
    out[0, 0] = sum_of(ka, ga, 0)
    out[1, 0] = sum_of(kb, gb, 0)


def fold_join(ka, ga, kb, gb, after=()):
    _, r, c = ka.shape
    return run(
        fold_join_kernel,
        (ka, ga, kb, gb),
        [pl.BlockSpec((1, r, c), lambda z: (z, 0, 0))] * 4,
        pl.BlockSpec((2, 1, r, c), lambda z: (0, z, 0, 0)),
        shape((2, 2, r, c), BF16),
        (2,),
        "fold_join",
        (),
        after,
        weight=FOLD_WEIGHT,
    )


def fold_near_kernel(index_ref, ka, ga, kb, gb, keep, send):
    z = index_ref[0, 2]
    for half, (k, g) in enumerate(((ka, ga), (kb, gb))):
        keep[half] = sum_of(k, g, z)
        send[half] = sum_of(k, g, 1 - z)


def fold_near(index, ka, ga, kb, gb, after=()):
    return run(
        fold_near_kernel,
        (index, ka, ga, kb, gb),
        [IN_SMEM] + [whole(ka.shape)] * 4,
        [whole(ka.shape)] * 2,
        [shape(ka.shape, BF16)] * 2,
        (1,),
        "fold_near",
        (),
        after,
        weight=FOLD_WEIGHT,
    )


def fold_far_kernel(index_ref, k, g, keep, send):
    z = index_ref[0, 3]
    keep[...] = sum_of(k, g, z)
    send[...] = sum_of(k, g, 1 - z)


def fold_far(index, keep, got):
    return run(
        fold_far_kernel,
        (index, keep, got),
        [IN_SMEM] + [whole(keep.shape)] * 2,
        [whole(keep.shape[1:])] * 2,
        [shape(keep.shape[1:], BF16)] * 2,
        (1,),
        "fold_far",
    )


def shuffle(values, axis, bit):
    return lax.ppermute(values, axis, [(i, i ^ bit) for i in range(lax.axis_size(axis))])


def adamw(master, first, second, gradient, factor, step_rate, decay_rate):
    fix_one = 1.0 - BETA_ONE**STEP_NUMBER
    fix_two = 1.0 - BETA_TWO**STEP_NUMBER
    clipped = gradient * factor
    first = BETA_ONE * first + (1.0 - BETA_ONE) * clipped
    second = BETA_TWO * second + (1.0 - BETA_TWO) * clipped * clipped
    update = first / fix_one / (jnp.sqrt(second / fix_two) + ADAM_EPS)
    master = master - step_rate * (update + decay_rate * master)
    return (master, first, second)


def row_tables(lengths, rows):
    index = lax.axis_index("narrow") * rows + jnp.arange(rows, dtype=jnp.int32)
    first_len, second_len = lengths[0], lengths[1]
    in_first = index < first_len
    in_second = (index >= first_len) & (index < first_len + second_len)
    live = (in_first | in_second).astype(F32)
    position = jnp.where(in_second, index - first_len, index)
    span = jnp.where(in_first, first_len, jnp.where(in_second, second_len, 1))
    angle = 0.5 * math.pi * position.astype(F32) / span.astype(F32)
    cos = (jnp.cos(angle) * live)[:, None]
    sin = (jnp.sin(angle) * live)[:, None]
    goes_on = (first_len > rows).astype(F32).reshape(1, 1)
    second = lax.axis_index("narrow").astype(F32)
    return (
        jnp.broadcast_to(cos, (rows, 128)),
        jnp.broadcast_to(sin, (rows, 128)),
        jnp.broadcast_to(live[:, None], (rows, 128)),
        goes_on * second,
        goes_on * (1.0 - second),
    )


def shards(
    stream, seq_lengths, cotangent, w_qkv, w_out, w_in, w_back, norm_params,
    qkv_master, qkv_first, qkv_second, out_master, out_first, out_second,
    in_master, in_first, in_second, back_master, back_first, back_second,
    norm_master, norm_first, norm_second,
    wide_axes,
):
    rows, width = stream.shape
    half = w_qkv.shape[3]
    heads = half // HEAD
    every = wide_axes + ("narrow",)
    wide = math.prod(lax.axis_size(axis) for axis in wide_axes)
    by_axes = len(wide_axes) == 3
    cos, sin, live, takes, gives = row_tables(seq_lengths[0], rows)
    if by_axes:
        z, y, x = (lax.axis_index(axis) for axis in wide_axes)
        index = jnp.stack([x, y, z % 2, z // 2]).astype(jnp.int32).reshape(1, 4)

    qkv = jnp.transpose(w_qkv, (0, 2, 1, 3))
    qkv_peer = swap(qkv)
    out_peer, in_peer, back_peer = swap(w_out), swap(w_in), swap(w_back)

    low = stream
    current = stream
    kept = []
    got = [None] * LAYERS
    for layer in range(LAYERS):
        before = () if layer == 0 else got[layer - 1][1:3]
        if layer == 0:
            *own, kv_own = project(low, (qkv,), layer, cos, sin)
            *peer, kv_peer = project(low, (qkv_peer,), layer, cos, sin)
            kv, kv_at = (swap(kv_peer), swap(kv_own)), (0, 0)
        else:
            *parts, kv = project(low, (qkv, qkv_peer), layer, cos, sin, before)
            own, peer = parts[:3], parts[3:]
            kv, kv_at = (swap(kv),) * 2, (0, 1)
        low_got = swap(low)
        before = () if layer == 0 else (got[layer - 1][0], got[layer - 1][3])
        m_own, m_peer, rden, first, ffn_in, xh1, rs1, states = attend(
            takes, own, peer, kv, kv_at, w_out, out_peer, layer, current, norm_params, before
        )
        last = layer == LAYERS - 1
        h_own, h_peer, slope, out, out_low, xh2, rs2 = feed(
            ffn_in, first, w_in, in_peer, w_back, back_peer, layer, norm_params, last,
            (low_got,) if last else (),
        )
        got[layer] = (low_got, swap(m_peer), swap(ffn_in), swap(h_peer))
        kept.append(
            (low, own, peer, m_own, m_peer, rden, ffn_in, xh1, rs1, states, h_own, slope, xh2, rs2)
        )
        current, low = out, out_low

    up = cotangent
    norm_grads = [None] * LAYERS
    shares = [None] * LAYERS
    scatter_z = lambda joined: lax.psum_scatter(joined.reshape((4,) + joined.shape[2:]), "z")
    after = got[LAYERS - 1][1:3]
    for layer in reversed(range(LAYERS)):
        (low, own, peer, m_own, m_peer, rden, ffn_in, xh1, rs1, states, h_own, slope, xh2, rs2) = (
            kept[layer]
        )
        low_got, m_got, ffn_got, h_got = got[layer]
        last = layer == 0
        gfb, gh_own, gh_peer, grad_first, norm_grads[layer] = feed_back(
            up, None if last else live, xh2, rs2, xh1, rs1, slope, w_in, in_peer, w_back, back_peer,
            layer, norm_params, after,
        )
        gfb_got, gh_got = swap(gfb), swap(gh_peer)
        after = ()
        if last and by_axes:
            share_ff = fold_join(*ff_second, (gfb,))
            share_ff = scatter_z(share_ff)
            ka, sa, kb, sb = fold_split(index, *q_first, (gfb,))
            q_second = (ka, swap(sa, "y"), kb, swap(sb, "x"))
            after = (ka,)
        gx, dkv = mix_back(
            gfb, w_out, out_peer, layer, rden, m_own, m_peer, own[0], peer[0], after
        )
        dkv_got = swap(dkv)
        norm_sum = jnp.stack(norm_grads) if last else None
        if not by_axes:
            back_grad = weight_grad(h_own, gfb[0], h_got, gfb_got[0], 512, width, "back_grad")
            in_grad = weight_grad(ffn_in, gh_own, ffn_got, gh_got, width, 512, "in_grad")
            out_grad = weight_grad(m_own, gfb[1], m_got, gfb_got[1], half, width, "out_grad")
            g_own, g_peer = attend_back(gives, own, peer, gx, states, dkv_got, cos, sin)
            up = input_back(g_own, g_peer, qkv, qkv_peer, layer, grad_first)
            qkv_grad = weight_grad(low, g_own, low_got, swap(g_peer), width, half, "qkv_grad")
            shares[layer] = [
                lax.psum_scatter(g, wide_axes, scatter_dimension=0, tiled=True).astype(F32)
                for g in (qkv_grad, out_grad, in_grad, back_grad)
            ]
            shares[layer][0] = shares[layer][0].reshape(-1, 3, half)
            after = ()
            continue
        if last:
            pair = norm_sum.reshape(8, width)
            pair = pair + swap(pair)
            pair = jnp.transpose(pair.reshape(8, wide, width // wide), (1, 0, 2))
            pair = jnp.pad(pair, ((0, 0), (0, 0), (0, 128 - width // wide)))
        else:
            pair = jnp.zeros((wide, 8, 128), F32)
        buffers = back_pack(index, h_own, gfb, h_got, gfb_got, (gx,))
        buffers = column_pack(
            index, ffn_in, gh_own, ffn_got, gh_got, buffers, width, FF_ROWS, 2, "in_grad"
        )
        after = ()
        if last:
            joined = fold_join(*q_second, (buffers[0],))
            share_q = scatter_z(joined)
            after = (joined,)
        ka, sa, kb, sb = out_pack(index, m_own, gfb, m_got, gfb_got, pair, buffers, after)
        ff_first = (ka, swap(sa, "x"), kb, swap(sb, "y"))
        g_own, g_peer = attend_back(gives, own, peer, gx, states, dkv_got, cos, sin, (ka,))
        g_got = swap(g_peer)
        up = input_back(g_own, g_peer, qkv, qkv_peer, layer, grad_first)
        ka, sa, kb, sb = fold_split(index, *ff_first, (up,))
        ff_second = (ka, swap(sa, "y"), kb, swap(sb, "x"))
        q_ka, q_sa, q_kb, q_sb = column_pack(
            index, low, g_own, low_got, g_got, None, half, Q_ROWS, 0, "qkv_grad", (ka,)
        )
        q_first = (q_ka, swap(q_sa, "x"), q_kb, swap(q_sb, "y"))
        after = (q_ka,)
        if not last:
            continue
        joined = fold_join(*ff_second, (q_ka,))
        share_ff0 = scatter_z(joined)
        ka, sa, kb, sb = fold_split(index, *q_first, (joined,))
        keep, send = fold_near(index, ka, swap(sa, "y"), kb, swap(sb, "x"))
        keep, send = fold_far(index, keep, shuffle(send, "z", 1))
        share_q0 = keep.astype(F32) + shuffle(send, "z", 2).astype(F32)
        for at, ff, q in ((0, share_ff0, share_q0), (1, share_ff, share_q)):
            ff, q = ff.astype(F32), q.astype(F32)
            rows_in = width // wide
            shares[at] = [
                jnp.transpose(q.reshape(3, rows_in, half), (1, 0, 2)),
                ff[192:216],
                jnp.concatenate([ff[96:144], ff[144:192]], axis=1),
                ff[:96],
            ]

    stacked = [jnp.stack([shares[l][kind] for l in range(LAYERS)]) for kind in range(4)]
    if by_axes:
        part = width // wide // 2
        norm_reduced = lax.dynamic_slice_in_dim(
            share_ff0[216:224].astype(F32), lax.axis_index("narrow") * part, part, 1
        ).reshape(LAYERS, 4, part)
    else:
        norm_reduced = lax.psum_scatter(norm_sum, every, scatter_dimension=2, tiled=True)
    squares = sum(jnp.sum(g * g) for g in stacked + [norm_reduced])
    count = wide * lax.axis_size("narrow")
    squares = lax.all_to_all(
        jnp.broadcast_to(squares, (count, 128)), every, 0, 0, tiled=True
    ).sum(0)[:1]
    clip_norm = jnp.sqrt(squares)
    factor = jnp.minimum(1.0, CLIP / clip_norm[0])
    matrix = lambda m, f, s, g: adamw(m, f, s, g, factor, LR_MATRIX, DECAY_MATRIX)
    qkv_new = matrix(qkv_master, qkv_first, qkv_second, stacked[0])
    out_new = matrix(out_master, out_first, out_second, stacked[1])
    in_new = matrix(in_master, in_first, in_second, stacked[2])
    back_new = matrix(back_master, back_first, back_second, stacked[3])
    norm_new = adamw(norm_master, norm_first, norm_second, norm_reduced, factor, LR_NORMS, 0.0)
    return (current, up, *qkv_new, *out_new, *in_new, *back_new, *norm_new, clip_norm)


def solution(mesh):
    wide_axes = ("wide",)
    if mesh.shape["wide"] == 16:
        wide_axes = ("z", "y", "x")
        mesh = Mesh(mesh.devices.reshape(4, 2, 2, 2), wide_axes + ("narrow",))
    rows = P(wide_axes + ("narrow",), None)
    qkv = P(None, wide_axes, None, "narrow")
    deep = P(None, ("narrow",) + wide_axes, None)
    in_part = P(None, wide_axes, "narrow")
    norm = P(None, None, wide_axes + ("narrow",))
    states = (qkv,) * 3 + (deep,) * 3 + (in_part,) * 3 + (deep,) * 3 + (norm,) * 3
    in_specs = (
        rows, P(wide_axes, None), rows,
        P(None, None, None, "narrow"), P(None, "narrow", None), P(None, None, "narrow"),
        P(None, "narrow", None), P(),
    ) + states
    out_specs = (rows, rows) + states + (P(),)
    return jax.shard_map(
        functools.partial(shards, wide_axes=wide_axes),
        mesh=mesh, in_specs=in_specs, out_specs=out_specs, check_vma=False,
    )
```

```python
import functools
import math

import jax
import jax.numpy as jnp
from jax import lax
from jax.experimental import pallas as pl
from jax.experimental.pallas import tpu as pltpu
from jax.sharding import Mesh
from jax.sharding import PartitionSpec as P

HEAD = 64
LAYERS = 2
CHUNK = 256
FF_BLOCK = 768
VMEM = 64 * 1024 * 1024 - 128 * 1024
FOLD_WEIGHT = 1e12

EPS_NORM = 1e-05
CLIP = 1.0
BETA_ONE = 0.5
BETA_TWO = 0.5
ADAM_EPS = 1e-08
LR_MATRIX = 0.1
LR_NORMS = 0.5
DECAY_MATRIX = 0.1
STEP_NUMBER = 4.0

F32 = jnp.float32
BF16 = jnp.bfloat16


def run(
    kernel, args, in_specs, out_specs, out_shape, grid, name,
    scratch=(), after=(), aliases=None, weight=0, vmem=None,
):
    count, extra = len(args), len(after)

    def body(*refs):
        kernel(*refs[:count], *refs[count + extra :])

    return pl.pallas_call(
        body,
        grid=grid,
        in_specs=list(in_specs) + [pl.BlockSpec(memory_space=pl.ANY)] * extra,
        out_specs=out_specs,
        out_shape=out_shape,
        scratch_shapes=list(scratch),
        input_output_aliases=aliases or {},
        compiler_params=pltpu.CompilerParams(
            vmem_limit_bytes=vmem or VMEM, dimension_semantics=("arbitrary",) * len(grid)
        ),
        cost_estimate=pl.CostEstimate(
            flops=int(weight), bytes_accessed=int(weight), transcendentals=0
        ),
        name=name,
    )(*args, *after)


def dot(a, b):
    return jnp.dot(a, b, preferred_element_type=F32)


def dot_nt(a, b):
    return lax.dot_general(a, b, (((1,), (1,)), ((), ())), preferred_element_type=F32)


def dot_tn(a, b):
    return lax.dot_general(a, b, (((0,), (0,)), ((), ())), preferred_element_type=F32)


def low_lanes(rows):
    return lax.broadcasted_iota(jnp.int32, (rows, 128), 1) < HEAD


def shape(dims, dtype):
    return jax.ShapeDtypeStruct(dims, dtype)


IN_SMEM = pl.BlockSpec(memory_space=pltpu.SMEM)


def whole(array_shape):
    return pl.BlockSpec(array_shape, lambda *_: (0,) * len(array_shape))


def row_spec(rows, cols, index=lambda i: i):
    return pl.BlockSpec((rows, cols), lambda i: (index(i), 0))


def layer_spec(array, layer):
    rest = array.shape[1:]
    return pl.BlockSpec((None,) + rest, lambda *_: (layer,) + (0,) * len(rest))


def wide_low_lanes(rows):
    return jnp.concatenate([low_lanes(rows)] * 2, axis=1)


def own_lanes(pair, wide_low, odd):
    zero = jnp.zeros_like(pair)
    return jnp.where(wide_low, zero, pair) if odd else jnp.where(wide_low, pair, zero)


def pair_state(features, right):
    both = dot_tn(features, right)
    return jnp.where(wide_low_lanes(128), both[:128], both[128:])


def vext_of(v_pair):
    return jnp.concatenate([v_pair, jnp.ones_like(v_pair)], axis=1)


def tables_kernel(here_ref, cos_ref, sin_ref, live_ref):
    rows = cos_ref.shape[0]
    core, first_len, second_len = (here_ref[0, n] for n in (4, 5, 6))
    index = core * rows + lax.broadcasted_iota(jnp.int32, (rows, 128), 0)
    in_first = index < first_len
    in_second = jnp.logical_and(index >= first_len, index < first_len + second_len)
    live = jnp.where(jnp.logical_or(in_first, in_second), 1.0, 0.0)
    position = jnp.where(in_second, index - first_len, index).astype(F32)
    span = jnp.where(in_first, first_len, jnp.where(in_second, second_len, 1)).astype(F32)
    angle = jnp.where(live > 0.0, 0.5 * math.pi * position / span, 0.0)
    square = angle * angle
    cos = sin = jnp.zeros_like(angle)
    for n in range(7, -1, -1):
        cos = cos * square + (-1.0) ** n / math.factorial(2 * n)
        sin = sin * square + (-1.0) ** n / math.factorial(2 * n + 1)
    cos_ref[...] = cos * live
    sin_ref[...] = sin * angle * live
    live_ref[...] = live


def tables(here, rows):
    return run(
        tables_kernel, (here,), [IN_SMEM], [whole((rows, 128))] * 3,
        [shape((rows, 128), F32)] * 3, (1,), "tables",
    )


def project_kernel(x_ref, *refs):
    sides = (len(refs) - 3) // 4
    weights, (cos_ref, sin_ref) = refs[:sides], refs[sides : sides + 2]
    outs, kv_ref = refs[sides + 2 : -1], refs[-1]
    rows = x_ref.shape[0]
    x = x_ref[...]
    low = low_lanes(rows)
    cos, sin = cos_ref[...], sin_ref[...]
    first = pl.program_id(0) == 0

    def features(values, out_ref):
        for pair in range(values.shape[1] // 128):
            tile = jnp.maximum(values[:, pair * 128 : pair * 128 + 128], 0.0)
            along = tile * cos
            across = pltpu.roll(tile, HEAD, 1) * sin
            base = pair * 256
            out_ref[:, base : base + 128] = jnp.where(low, along, across).astype(BF16)
            out_ref[:, base + 128 : base + 256] = jnp.where(low, across, along).astype(BF16)

    for side in range(sides):
        w_ref = weights[side]
        q_ref, k_ref, v_ref = outs[3 * side : 3 * side + 3]
        other = sides - 1 - side
        v = dot(x, w_ref[2]).astype(BF16)
        v_ref[...] = v
        features(dot(x, w_ref[1]), k_ref)
        features(dot(x, w_ref[0]), q_ref)
        for pair in range(v.shape[1] // 128):
            part = pair_state(
                k_ref[:, pair * 256 : pair * 256 + 256],
                vext_of(v[:, pair * 128 : pair * 128 + 128]),
            )
            kv_ref[other, pair] = jnp.where(first, part, kv_ref[other, pair] + part)


def project(x, weights, layer, cos, sin, after=()):
    rows, width = x.shape
    half = weights[0].shape[3]
    heads = half // HEAD
    block = rows // 2
    cat = row_spec(block, heads * 128)
    return run(
        project_kernel,
        (x, *weights, cos, sin),
        [row_spec(block, width)]
        + [layer_spec(w, layer) for w in weights]
        + [row_spec(block, 128)] * 2,
        [cat, cat, row_spec(block, half)] * len(weights)
        + [whole((len(weights), heads // 2, 128, 256))],
        [
            shape((rows, heads * 128), BF16),
            shape((rows, heads * 128), BF16),
            shape((rows, half), BF16),
        ]
        * len(weights)
        + [shape((len(weights), heads // 2, 128, 256), F32)],
        (rows // block,),
        "project",
        (),
        after,
    )


def norm_rows(r, gain, shift):
    mean = jnp.mean(r, axis=1, keepdims=True)
    centered = r - mean
    var = jnp.mean(centered * centered, axis=1, keepdims=True)
    rstd = lax.rsqrt(var + EPS_NORM)
    x_hat = centered * rstd
    return x_hat * gain + shift, x_hat, rstd


def attend_kernel(
    here_ref, qo_ref, qp_ref, ko_ref, kp_ref, vo_ref, vp_ref, kvo_ref, kvp_ref, wo_ref, wp_ref,
    resid_ref, norm_ref,
    mo_ref, mp_ref, rden_ref, low_ref, xhat_ref, rstd_ref, state_out_ref,
    state,
):
    rows = qo_ref.shape[0]
    half = vo_ref.shape[1]
    pairs = half // 128

    @pl.when(pl.program_id(0) == 0)
    def _():
        carry = here_ref[0, 7].astype(F32) * here_ref[0, 4].astype(F32)
        state[:pairs] = kvo_ref[...] * carry
        state[pairs:] = kvp_ref[...] * carry

    low = low_lanes(rows)
    row = lax.broadcasted_iota(jnp.int32, (rows, rows), 0)
    col = lax.broadcasted_iota(jnp.int32, (rows, rows), 1)
    causal = col <= row
    branch = None
    for side, (q_ref, k_ref, v_ref, m_ref, w_ref) in enumerate(
        ((qo_ref, ko_ref, vo_ref, mo_ref, wo_ref), (qp_ref, kp_ref, vp_ref, mp_ref, wp_ref))
    ):
        for pair in range(pairs):
            at = side * pairs + pair
            vext = vext_of(v_ref[:, pair * 128 : pair * 128 + 128])
            k_pair = k_ref[:, pair * 256 : pair * 256 + 256]
            q = [q_ref[:, n * 128 : n * 128 + 128] for n in (2 * pair, 2 * pair + 1)]
            kv = state[at]
            kv_low = kv.astype(BF16)
            state_out_ref[0, at] = kv_low
            far = dot(jnp.concatenate(q, axis=0), kv_low)
            sums = []
            for odd in (0, 1):
                scores = dot_nt(q[odd], k_pair[:, odd * 128 : odd * 128 + 128])
                scores = jnp.where(causal, scores, 0.0).astype(BF16)
                sums.append(dot(scores, vext) + far[odd * rows : odd * rows + rows])
            state[at] = kv + pair_state(k_pair, vext)
            num = jnp.where(low, sums[0][:, :128], sums[1][:, :128])
            den = jnp.where(low, sums[0][:, 128:], sums[1][:, 128:])
            rden = 1.0 / jnp.maximum(den, 1.0)
            base = side * half + pair * 128
            rden_low = jnp.where(den > 1.0, jnp.minimum(rden, 1.0 - 2.0**-8), 1.0)
            rden_ref[:, base : base + 128] = rden_low.astype(BF16)
            m_ref[:, pair * 128 : pair * 128 + 128] = (num * rden).astype(BF16)
        part = dot(m_ref[...], w_ref[...])
        branch = part if branch is None else branch + part
    y, x_hat, rstd = norm_rows(resid_ref[...].astype(F32) + branch, norm_ref[0:1], norm_ref[1:2])
    low_ref[...] = y.astype(BF16)
    xhat_ref[...] = x_hat.astype(BF16)
    rstd_ref[...] = jnp.broadcast_to(rstd, rstd_ref.shape)


def attend(here, own, peer, kv, kv_at, w_own, w_peer, layer, resid, norms, after=()):
    rows, width = resid.shape
    half = own[2].shape[1]
    heads = half // HEAD
    steps = rows // CHUNK
    cat, narrow = row_spec(CHUNK, heads * 128), row_spec(CHUNK, half)
    full = row_spec(CHUNK, width)
    return run(
        attend_kernel,
        (here, own[0], peer[0], own[1], peer[1], own[2], peer[2], *kv,
         w_own, w_peer, resid, norms),
        [
            IN_SMEM,
            cat, cat, cat, cat, narrow, narrow,
            *(pl.BlockSpec((None,) + a.shape[1:], lambda *_, n=n: (n, 0, 0, 0)) for a, n in zip(kv, kv_at)),
            layer_spec(w_own, layer), layer_spec(w_peer, layer),
            full, layer_spec(norms, layer),
        ],
        [
            narrow, narrow, full, full, full, row_spec(CHUNK, 128),
            pl.BlockSpec((1, heads, 128, 256), lambda i: (i, 0, 0, 0)),
        ],
        [
            shape((rows, half), BF16),
            shape((rows, half), BF16),
            shape((rows, width), BF16),
            shape((rows, width), BF16),
            shape((rows, width), BF16),
            shape((rows, 128), F32),
            shape((steps, heads, 128, 256), BF16),
        ],
        (steps,),
        "attend",
        [pltpu.VMEM((heads, 128, 256), F32)],
        after,
    )


def gelu_both(u):
    root = math.sqrt(2.0 / math.pi)
    a = root + (root * 0.044715) * (u * u)
    gate = 0.5 + 0.5 * jnp.tanh(u * a)
    act = u * gate
    return act, gate + (act - act * gate) * (6.0 * a - 4.0 * root)


def feed_kernel(
    x_ref, wio_ref, wip_ref, wbo_ref, wbp_ref, norm_ref,
    ho_ref, hp_ref, slope_ref, out_ref, xhat_ref, rstd_ref,
    acc,
):
    step, steps = pl.program_id(0), pl.num_programs(0)
    rows = x_ref.shape[0]

    def side(w_in, w_back, h_ref, base):
        for i in range(rows // CHUNK):
            at = slice(i * CHUNK, i * CHUNK + CHUNK)
            act, slope = gelu_both(dot(x_ref[at, :], w_in[...]))
            act = act.astype(BF16)
            h_ref[at, :] = act
            slope_ref[at, :] = slope.astype(BF16)
            acc[at, :] = base[at, :].astype(F32) + dot(act, w_back[...])

    @pl.when(step == 0)
    def _():
        side(wio_ref, wbo_ref, ho_ref, x_ref)

    @pl.when((step > 0) & (step < steps // 2))
    def _():
        side(wio_ref, wbo_ref, ho_ref, acc)

    @pl.when(step >= steps // 2)
    def _():
        side(wip_ref, wbp_ref, hp_ref, acc)

    @pl.when(step == steps - 1)
    def _():
        def part(i, _):
            at = pl.ds(pl.multiple_of(i * CHUNK, CHUNK), CHUNK)
            y, x_hat, rstd = norm_rows(acc[at, :], norm_ref[2:3], norm_ref[3:4])
            out_ref[at, :] = y.astype(out_ref.dtype)
            xhat_ref[at, :] = x_hat.astype(BF16)
            rstd_ref[at, :] = jnp.broadcast_to(rstd, (CHUNK, 128))
            return 0

        lax.fori_loop(0, rows // CHUNK, part, 0)


def ff_specs(layer, width, blocks):
    own = lambda j: jnp.minimum(j, blocks - 1)
    peer = lambda j: jnp.maximum(j - blocks, 0)
    w_in = [
        pl.BlockSpec((None, width, FF_BLOCK), lambda j, f=f: (layer, 0, f(j))) for f in (own, peer)
    ]
    w_back = [
        pl.BlockSpec((None, FF_BLOCK, width), lambda j, f=f: (layer, f(j), 0)) for f in (own, peer)
    ]
    return own, peer, w_in, w_back


def feed(x, wi_own, wi_peer, wb_own, wb_peer, layer, norms, dtype, after=()):
    rows, width = x.shape
    half = wi_own.shape[2]
    blocks = half // FF_BLOCK
    own, peer, w_in, w_back = ff_specs(layer, width, blocks)
    full = whole((rows, width))
    return run(
        feed_kernel,
        (x, wi_own, wi_peer, wb_own, wb_peer, norms),
        [full, *w_in, *w_back, layer_spec(norms, layer)],
        [
            pl.BlockSpec((rows, FF_BLOCK), lambda j: (0, own(j))),
            pl.BlockSpec((rows, FF_BLOCK), lambda j: (0, peer(j))),
            pl.BlockSpec((rows, FF_BLOCK), lambda j: (0, j)),
            full, full, whole((rows, 128)),
        ],
        [
            shape((rows, half), BF16),
            shape((rows, half), BF16),
            shape((rows, 2 * half), BF16),
            shape((rows, width), dtype),
            shape((rows, width), BF16),
            shape((rows, 128), F32),
        ],
        (2 * blocks,),
        "feed",
        [pltpu.VMEM((rows, width), F32)],
        after,
    )


def norm_back(y, x_hat, rstd, gain):
    scaled = y * gain
    mean = jnp.mean(scaled, axis=1, keepdims=True)
    along = jnp.mean(scaled * x_hat, axis=1, keepdims=True)
    gain_grad = jnp.sum(y * x_hat, axis=0, keepdims=True)
    shift_grad = jnp.sum(y, axis=0, keepdims=True)
    return (scaled - mean - x_hat * along) * rstd, gain_grad, shift_grad


def feed_back_kernel(
    up_ref, live_ref, xh2_ref, rs2_ref, xh1_ref, rs1_ref, slope_ref,
    wio_ref, wip_ref, wbo_ref, wbp_ref, norm_ref,
    gfb_ref, gho_ref, ghp_ref, ng_ref,
    acc,
):
    step, steps = pl.program_id(0), pl.num_programs(0)
    rows, width = up_ref.shape
    tiles = width // 128

    def chunk(i):
        return pl.ds(pl.multiple_of(i * CHUNK, CHUNK), CHUNK)

    def wide(ref, at):
        return jnp.concatenate([ref[at, :]] * tiles, axis=1)

    @pl.when(step == 0)
    def _():
        ng_ref[...] = jnp.zeros_like(ng_ref)

        def part(i, _):
            at = chunk(i)
            y = up_ref[at, :].astype(F32)
            if live_ref is not None:
                y = y * wide(live_ref, at)
            grad, gain_grad, shift_grad = norm_back(
                y, xh2_ref[at, :].astype(F32), wide(rs2_ref, at), norm_ref[2:3]
            )
            acc[at, :] = grad
            gfb_ref[0, at, :] = grad.astype(BF16)
            ng_ref[2:3] += gain_grad
            ng_ref[3:4] += shift_grad
            return 0

        lax.fori_loop(0, rows // CHUNK, part, 0)

    def side(w_in, w_back, gh_ref):
        for i in range(rows // CHUNK):
            at = slice(i * CHUNK, i * CHUNK + CHUNK)
            act = dot_nt(gfb_ref[0, at, :], w_back[...])
            gh = (act * slope_ref[at, :].astype(F32)).astype(BF16)
            gh_ref[at, :] = gh
            acc[at, :] += dot_nt(gh, w_in[...])

    @pl.when(step < steps // 2)
    def _():
        side(wio_ref, wbo_ref, gho_ref)

    @pl.when(step >= steps // 2)
    def _():
        side(wip_ref, wbp_ref, ghp_ref)

    @pl.when(step == steps - 1)
    def _():
        def part(i, _):
            at = chunk(i)
            grad, gain_grad, shift_grad = norm_back(
                acc[at, :], xh1_ref[at, :].astype(F32), wide(rs1_ref, at), norm_ref[0:1]
            )
            gfb_ref[1, at, :] = grad.astype(BF16)
            ng_ref[0:1] += gain_grad
            ng_ref[1:2] += shift_grad
            return 0

        lax.fori_loop(0, rows // CHUNK, part, 0)


def feed_back(
    up, live, xh2, rs2, xh1, rs1, slope, wi_own, wi_peer, wb_own, wb_peer, layer, norms, after=()
):
    rows, width = up.shape
    half = wi_own.shape[2]
    blocks = half // FF_BLOCK
    own, peer, w_in, w_back = ff_specs(layer, width, blocks)
    full, thin = whole((rows, width)), whole((rows, 128))
    if live is None:

        def kernel(up_ref, *refs):
            feed_back_kernel(up_ref, None, *refs)

        args, specs = (up,), [full]
    else:
        kernel, args, specs = feed_back_kernel, (up, live), [full, thin]
    return run(
        kernel,
        args + (xh2, rs2, xh1, rs1, slope, wi_own, wi_peer, wb_own, wb_peer, norms),
        specs
        + [
            full, thin, full, thin,
            pl.BlockSpec((rows, FF_BLOCK), lambda j: (0, j)),
            *w_in, *w_back, layer_spec(norms, layer),
        ],
        [
            whole((2, rows, width)),
            pl.BlockSpec((rows, FF_BLOCK), lambda j: (0, own(j))),
            pl.BlockSpec((rows, FF_BLOCK), lambda j: (0, peer(j))),
            whole((4, width)),
        ],
        [
            shape((2, rows, width), BF16),
            shape((rows, half), BF16),
            shape((rows, half), BF16),
            shape((4, width), F32),
        ],
        (2 * blocks,),
        "feed_back",
        [pltpu.VMEM((rows, width), F32)],
        after,
    )


def mix_back_kernel(
    gfb_ref, wo_ref, wp_ref, rden_ref, mo_ref, mp_ref, qo_ref, qp_ref, gx_ref, dkv_ref, total
):
    rows = gfb_ref.shape[0]
    half = mo_ref.shape[1]
    pairs = half // 128
    first = pl.program_id(0) == 0
    r = lax.broadcasted_iota(jnp.int32, (256, 128), 0) % 128
    c = lax.broadcasted_iota(jnp.int32, (256, 128), 1)
    spread_c = jnp.where((r < HEAD) == (c < HEAD), -1.0 / HEAD, 0.0).astype(BF16)
    gb = gfb_ref[...]
    for side, (w_ref, m_ref, q_ref) in enumerate(
        ((wo_ref, mo_ref, qo_ref), (wp_ref, mp_ref, qp_ref))
    ):
        gm = dot_nt(gb, w_ref[...])
        for pair in range(pairs):
            base = side * half + pair * 128
            rden = rden_ref[:, base : base + 128].astype(F32)
            g = gm[:, pair * 128 : pair * 128 + 128] * rden
            m = m_ref[:, pair * 128 : pair * 128 + 128].astype(F32)
            prod = jnp.where(rden < 1.0, g * m, 0.0)
            high = prod.astype(BF16)
            rest = (prod - high.astype(F32)).astype(BF16)
            minus_c = dot(jnp.concatenate([high, rest], axis=1), spread_c).astype(BF16)
            gx = jnp.concatenate([g.astype(BF16), minus_c], axis=1)
            gx_ref[:, 2 * base : 2 * base + 256] = gx
            part = pair_state(q_ref[:, pair * 256 : pair * 256 + 256], gx)
            at = side * pairs + pair
            total[at] = jnp.where(first, part, total[at] + part)

    @pl.when(pl.program_id(0) == pl.num_programs(0) - 1)
    def _():
        dkv_ref[...] = total[...].astype(BF16)


def mix_back(gfb, w_own, w_peer, layer, rden, m_own, m_peer, q_own, q_peer, after=()):
    _, rows, width = gfb.shape
    half = m_own.shape[1]
    heads = half // HEAD
    full, narrow, cat = (row_spec(CHUNK, n) for n in (width, half, heads * 128))
    return run(
        mix_back_kernel,
        (gfb, w_own, w_peer, rden, m_own, m_peer, q_own, q_peer),
        [
            pl.BlockSpec((None, CHUNK, width), lambda i: (1, i, 0)),
            layer_spec(w_own, layer), layer_spec(w_peer, layer),
            full, narrow, narrow, cat, cat,
        ],
        [row_spec(CHUNK, 2 * width), whole((heads, 128, 256))],
        [
            shape((rows, 2 * width), BF16),
            shape((heads, 128, 256), BF16),
        ],
        (rows // CHUNK,),
        "mix_back",
        [pltpu.VMEM((heads, 128, 256), F32)],
        after,
    )


def attend_back_kernel(
    here_ref, qo_ref, qp_ref, ko_ref, kp_ref, vo_ref, vp_ref, gx_ref, state_ref, dkv_ref,
    cos_ref, sin_ref,
    go_ref, gp_ref,
    dstate,
):
    rows = qo_ref.shape[0]
    half = vo_ref.shape[1]
    pairs = half // 128

    @pl.when(pl.program_id(0) == 0)
    def _():
        carry = here_ref[0, 7].astype(F32) * (1 - here_ref[0, 4]).astype(F32)
        for at in range(2 * pairs):
            dstate[at] = dkv_ref[(at + pairs) % (2 * pairs)].astype(F32) * carry

    low = low_lanes(rows)
    wide_low, state_low = wide_low_lanes(rows), wide_low_lanes(128)
    row = lax.broadcasted_iota(jnp.int32, (rows, rows), 0)
    col = lax.broadcasted_iota(jnp.int32, (rows, rows), 1)
    causal, anti = col <= row, row <= col
    cos, sin = cos_ref[...], sin_ref[...]
    trig = jnp.where(low, cos, sin), jnp.where(low, sin, cos)
    for side, (q_ref, k_ref, v_ref, out_ref) in enumerate(
        ((qo_ref, ko_ref, vo_ref, go_ref), (qp_ref, kp_ref, vp_ref, gp_ref))
    ):
        for pair in range(pairs):
            at = side * pairs + pair
            vext = vext_of(v_ref[:, pair * 128 : pair * 128 + 128])
            gx = gx_ref[:, at * 256 : at * 256 + 256]
            gext = [own_lanes(gx, wide_low, odd) for odd in (0, 1)]
            both = jnp.concatenate(gext, axis=0)
            ds_both = dot_nt(both, vext)
            q_far = dot_nt(both, state_ref[0, at])
            dst_both = dot_nt(vext, both)
            left_over = dstate[at].astype(BF16)
            back = [own_lanes(left_over, state_low, odd) for odd in (0, 1)]
            k_far = dot_nt(vext, jnp.concatenate(back, axis=0))
            dstate[at] += pair_state(q_ref[:, pair * 256 : pair * 256 + 256], gx)
            dq, dk, left, right = [], [], [], []
            for odd in (0, 1):
                head = 2 * pair + odd
                here = slice(odd * rows, odd * rows + rows)
                q = q_ref[:, head * 128 : head * 128 + 128]
                k = k_ref[:, head * 128 : head * 128 + 128]
                score_t = jnp.where(anti, dot_nt(k, q), 0.0).astype(BF16)
                ds = jnp.where(causal, ds_both[here], 0.0).astype(BF16)
                ds_t = jnp.where(anti, dst_both[:, here], 0.0).astype(BF16)
                q_grad = (dot(ds, k) + q_far[here]) * trig[odd]
                k_grad = (dot(ds_t, q) + k_far[:, odd * 128 : odd * 128 + 128]) * trig[odd]
                left += [score_t, k]
                right += [gext[odd][:, :128], back[odd][:, :128]]
                q_grad = q_grad + pltpu.roll(q_grad, HEAD, 1)
                k_grad = k_grad + pltpu.roll(k_grad, HEAD, 1)
                dq.append(jnp.where(q > 0, q_grad, 0.0))
                dk.append(jnp.where(k > 0, k_grad, 0.0))
            dv = dot(jnp.concatenate(left, axis=1), jnp.concatenate(right, axis=0))
            for kind, value in enumerate(
                (jnp.where(low, dq[0], dq[1]), jnp.where(low, dk[0], dk[1]), dv)
            ):
                base = kind * half + pair * 128
                out_ref[:, base : base + 128] = value.astype(BF16)


def attend_back_on_kernel(*refs):
    inputs, (wo_ref, wp_ref, first_ref), (go_ref, gp_ref, up_ref, dstate) = (
        refs[:12], refs[12:15], refs[15:],
    )
    attend_back_kernel(*inputs, go_ref, gp_ref, dstate)
    input_back_kernel(go_ref, gp_ref, wo_ref, wp_ref, first_ref, up_ref)


def attend_back(here, own, peer, gx, states, dkv, cos, sin, after=(), onward=None):
    rows = cos.shape[0]
    half = own[2].shape[1]
    heads = half // HEAD
    steps = rows // CHUNK
    back = lambda i: steps - 1 - i
    cat, narrow, trig = (row_spec(CHUNK, n, back) for n in (heads * 128, half, 128))
    args = (here, own[0], peer[0], own[1], peer[1], own[2], peer[2], gx, states, dkv, cos, sin)
    specs = [
        IN_SMEM,
        cat, cat, cat, cat, narrow, narrow,
        row_spec(CHUNK, heads * 256, back),
        pl.BlockSpec((1, heads, 128, 256), lambda i: (back(i), 0, 0, 0)),
        whole(dkv.shape), trig, trig,
    ]
    outs = [row_spec(CHUNK, 3 * half, back)] * 2
    shapes = [shape((rows, 3 * half), BF16)] * 2
    kernel = attend_back_kernel
    if onward is not None:
        w_own, w_peer, layer, gfb = onward
        kernel = attend_back_on_kernel
        width = gfb.shape[2]
        args += (w_own, w_peer, gfb)
        specs += [layer_spec(w_own, layer), layer_spec(w_peer, layer)]
        specs += [pl.BlockSpec((None, CHUNK, width), lambda i: (1, back(i), 0))]
        outs, shapes = outs + [row_spec(CHUNK, width, back)], shapes + [shape((rows, width), BF16)]
    return run(
        kernel, args, specs, outs, shapes, (steps,), "attend_back",
        [pltpu.VMEM((heads, 128, 256), F32)],
        after,
    )


def input_back_kernel(go_ref, gp_ref, wo_ref, wp_ref, first_ref, out_ref):
    half = wo_ref.shape[2]
    total = first_ref[...].astype(F32)
    for g_ref, w_ref in ((go_ref, wo_ref), (gp_ref, wp_ref)):
        for kind in range(3):
            total = total + dot_nt(g_ref[:, kind * half : kind * half + half], w_ref[kind])
    out_ref[...] = total.astype(out_ref.dtype)


def input_back(g_own, g_peer, w_own, w_peer, layer, gfb, after=()):
    _, rows, width = gfb.shape
    block = rows // 2
    third, full = row_spec(block, g_own.shape[1]), row_spec(block, width)
    return run(
        input_back_kernel,
        (g_own, g_peer, w_own, w_peer, gfb),
        [
            third, third, layer_spec(w_own, layer), layer_spec(w_peer, layer),
            pl.BlockSpec((None, block, width), lambda i: (1, i, 0)),
        ],
        full,
        shape((rows, width), F32),
        (rows // block,),
        "input_back",
        (),
        after,
    )


def weight_kernel(a_ref, b_ref, c_ref, d_ref, out_ref):
    out_ref[...] = (dot_tn(a_ref[...], b_ref[...]) + dot_tn(c_ref[...], d_ref[...])).astype(
        out_ref.dtype
    )


def weight_grad(a, b, c, d, block_m, block_n, name):
    rows, m = a.shape
    n = b.shape[1]
    left = pl.BlockSpec((rows, block_m), lambda i, j: (0, i))
    right = pl.BlockSpec((rows, block_n), lambda i, j: (0, j))
    return run(
        weight_kernel,
        (a, b, c, d),
        [left, right, left, right],
        pl.BlockSpec((block_m, block_n), lambda i, j: (i, j)),
        shape((m, n), BF16),
        (m // block_m, n // block_n),
        name,
    )


FF_ROWS = 448
Q_ROWS = 144
NORM_ROW = 408


def fold_lanes(values, width):
    pieces = [values[:, at : at + width] for at in range(0, values.shape[1], width)]
    return jnp.concatenate(pieces, axis=0) if len(pieces) > 1 else values


def blocks_of(index_ref, scr, rows, z_local, x_first, other, kept):
    x, y = index_ref[0, 0], index_ref[0, 1]
    if x_first:
        spot = other * 2 + (x if kept else 1 - x)
    else:
        spot = (y if kept else 1 - y) * 2 + other
    start = pl.multiple_of((z_local * 4 + spot) * rows, 8)
    return scr[pl.ds(start, rows), :]


def back_pack_kernel(index_ref, a_ref, b_ref, c_ref, d_ref, ka, sa, kb, sb, scr):
    rows = scr.shape[0] // 4
    scr[...] = dot_tn(a_ref[...], b_ref[...]) + dot_tn(c_ref[...], d_ref[...])
    z = pl.program_id(0)
    for x_first, (keep, send) in ((True, (ka, sa)), (False, (kb, sb))):

        @pl.when((z < 2) == x_first)
        def _():
            for other in range(2):
                for kept, out in ((True, keep), (False, send)):
                    value = blocks_of(index_ref, scr, rows, 0, x_first, other, kept)
                    out[0, other] = fold_lanes(value, out.shape[3]).astype(BF16)


def half_spec(array, at):
    return pl.BlockSpec((None,) + array.shape[1:], lambda *_: (at, 0, 0))


def back_pack(index, a, b, c, d, after=()):
    rows, m = a.shape
    n = b.shape[2]
    block = m // 4
    left = pl.BlockSpec((rows, block), lambda z: (0, z))
    buffer = shape((2, 2, FF_ROWS, n // 2), BF16)
    low = pl.BlockSpec((1, 2, block // 2, n // 2), lambda z: (jnp.minimum(z, 1), 0, 0, 0))
    high = pl.BlockSpec((1, 2, block // 2, n // 2), lambda z: (jnp.maximum(z - 2, 0), 0, 0, 0))
    return run(
        back_pack_kernel,
        (index, a, b, c, d),
        [IN_SMEM, left, half_spec(b, 0), left, half_spec(d, 0)],
        [low, low, high, high],
        [buffer] * 4,
        (4,),
        "back_grad",
        [pltpu.VMEM((block, n), F32)],
        after,
    )


def spread(index_ref, scr, rows, outs, tail=None):
    ka, sa, kb, sb = outs
    for x_first, keep, send in ((True, ka, sa), (False, kb, sb)):
        for z in range(2):
            z_local = z if x_first else z + 2
            for other in range(2):
                for kept, out in ((True, keep), (False, send)):
                    value = blocks_of(index_ref, scr, rows, z_local, x_first, other, kept)
                    if tail is not None:
                        x, y = index_ref[0, 0], index_ref[0, 1]
                        if x_first:
                            w = z_local * 4 + other * 2 + (x if kept else 1 - x)
                        else:
                            w = z_local * 4 + (y if kept else 1 - y) * 2 + other
                        value = jnp.concatenate([value, tail(w)], axis=0)
                    out[z, other] = fold_lanes(value, out.shape[3]).astype(BF16)


def in_pack_kernel(index_ref, a_ref, b_ref, c_ref, d_ref, _ka, _sa, _kb, _sb, ka, sa, kb, sb, scr):
    scr[...] = dot_tn(a_ref[...], b_ref[...]) + dot_tn(c_ref[...], d_ref[...])
    spread(index_ref, scr, scr.shape[0] // 16, (ka, sa, kb, sb))


def column_pack(index, a, b, c, d, buffers, block_n, lanes, block_rows, first_block, name, after=()):
    rows, m = a.shape
    n = b.shape[1]
    right = pl.BlockSpec((rows, block_n), lambda j: (0, j))
    out_rows = m // 16 * (block_n // lanes)
    out = pl.BlockSpec((2, 2, out_rows, lanes), lambda j: (0, 0, first_block + j, 0))
    specs = [IN_SMEM, whole(a.shape), right, whole(c.shape), right]
    scratch = [pltpu.VMEM((m, block_n), F32)]
    if buffers is None:

        def fresh(index_ref, a_ref, b_ref, c_ref, d_ref, *outs):
            in_pack_kernel(index_ref, a_ref, b_ref, c_ref, d_ref, *([None] * 4), *outs)

        return run(
            fresh, (index, a, b, c, d), specs, [out] * 4,
            [shape((2, 2, block_rows, lanes), BF16)] * 4, (n // block_n,), name, scratch, after,
        )
    return run(
        in_pack_kernel,
        (index, a, b, c, d, *buffers),
        specs + [pl.BlockSpec(memory_space=pl.ANY)] * 4,
        [out] * 4,
        [shape(buffer.shape, BF16) for buffer in buffers],
        (n // block_n,),
        name,
        scratch,
        after,
        {5 + i: i for i in range(4)},
    )


def out_pack_kernel(
    index_ref, a_ref, b_ref, c_ref, d_ref, norm_ref, norm_got_ref, _ka, _sa, _kb, _sb,
    ka, sa, kb, sb, scr,
):
    scr[...] = dot_tn(a_ref[...], b_ref[...]) + dot_tn(c_ref[...], d_ref[...])
    blank = jnp.zeros((8, scr.shape[1] - 128), F32)
    spread(
        index_ref, scr, scr.shape[0] // 16, (ka, sa, kb, sb),
        lambda w: jnp.concatenate([norm_ref[w] + norm_got_ref[w], blank], axis=1),
    )


def out_pack(index, a, b, c, d, norms, norms_got, buffers, after=()):
    m, n = a.shape[1], b.shape[2]
    block = 2 * (m // 16 + 8)
    out = pl.BlockSpec((2, 2, block, n // 2), lambda j: (0, 0, (FF_ROWS - block) // block, 0))
    return run(
        out_pack_kernel,
        (index, a, b, c, d, norms, norms_got, *buffers),
        [IN_SMEM, whole(a.shape), half_spec(b, 1), whole(c.shape), half_spec(d, 1)]
        + [whole(norms.shape)] * 2
        + [pl.BlockSpec(memory_space=pl.ANY)] * 4,
        [out] * 4,
        [shape(buffer.shape, BF16) for buffer in buffers],
        (1,),
        "out_grad",
        [pltpu.VMEM((m, n), F32)],
        after,
        {7 + i: i for i in range(4)},
    )


def swap(values, axis="narrow"):
    return lax.ppermute(values, axis, [(0, 1), (1, 0)])


def sum_of(a_ref, b_ref, *at):
    return (a_ref[at].astype(F32) + b_ref[at].astype(F32)).astype(BF16)


def fold_split_kernel(index_ref, ka, ga, kb, gb, ka_out, sa_out, kb_out, sb_out):
    x, y = index_ref[0, 0], index_ref[0, 1]
    ka_out[0] = sum_of(ka, ga, 0, y)
    sa_out[0] = sum_of(ka, ga, 0, 1 - y)
    kb_out[0] = sum_of(kb, gb, 0, x)
    sb_out[0] = sum_of(kb, gb, 0, 1 - x)


def fold_split(index, ka, ga, kb, gb, after=()):
    _, _, r, c = ka.shape
    return run(
        fold_split_kernel,
        (index, ka, ga, kb, gb),
        [IN_SMEM]
        + [pl.BlockSpec((1, 2, r, c), lambda z: (z, 0, 0, 0))] * 4,
        [pl.BlockSpec((1, r, c), lambda z: (z, 0, 0))] * 4,
        [shape((2, r, c), BF16)] * 4,
        (2,),
        "fold_split",
        (),
        after,
        weight=FOLD_WEIGHT,
    )


def fold_near_kernel(index_ref, *refs):
    z = index_ref[0, 2]
    keep, send = refs[-2:]
    for half in range(2):
        done = 0
        for at in range(0, len(refs) - 2, 4):
            k, g = refs[at + 2 * half], refs[at + 2 * half + 1]
            rows = slice(done, done + k.shape[1])
            done += k.shape[1]
            keep[half, rows] = sum_of(k, g, z)
            send[half, rows] = sum_of(k, g, 1 - z)


def fold_near(index, groups, after=()):
    arrays = [array for group in groups for array in group]
    rows, lanes = sum(group[0].shape[1] for group in groups), arrays[0].shape[2]
    return run(
        fold_near_kernel,
        (index, *arrays),
        [IN_SMEM] + [whole(array.shape) for array in arrays],
        [whole((2, rows, lanes))] * 2,
        [shape((2, rows, lanes), BF16)] * 2,
        (1,),
        "fold_near",
        (),
        after,
        weight=FOLD_WEIGHT,
    )


def fold_far_kernel(index_ref, k, g, keep, send):
    z = index_ref[0, 3]
    keep[...] = sum_of(k, g, z)
    send[...] = sum_of(k, g, 1 - z)


def fold_far(index, keep, got, after=()):
    return run(
        fold_far_kernel,
        (index, keep, got),
        [IN_SMEM] + [whole(keep.shape)] * 2,
        [whole(keep.shape[1:])] * 2,
        [shape(keep.shape[1:], BF16)] * 2,
        (1,),
        "fold_far",
        (),
        after,
        weight=FOLD_WEIGHT,
    )


def settle_kernel(norms, index_ref, k, g, out, squares):
    total = k[...].astype(F32) + g[...].astype(F32)
    out[...] = total
    if norms:
        row, lane = (lax.broadcasted_iota(jnp.int32, total.shape, n) for n in (0, 1))
        here = jnp.logical_and(row >= NORM_ROW, row < NORM_ROW + 8)
        other = jnp.logical_or(lane < index_ref[0, 4] * norms, lane >= (index_ref[0, 4] + 1) * norms)
        total = jnp.where(jnp.logical_and(here, other), 0.0, total)
    total = total * total
    part = total[:, :128] + total[:, 128:256] + total[:, 256:]
    squares[...] = jnp.sum(part.reshape(-1, 8, 128), axis=0)


def settle(index, keep, got, norms=0, after=()):
    return run(
        functools.partial(settle_kernel, norms),
        (index, keep, got),
        [IN_SMEM, whole(keep.shape), whole(keep.shape)],
        [whole(keep.shape), whole((8, 128))],
        [shape(keep.shape, F32), shape((8, 128), F32)],
        (1,),
        "settle",
        (),
        after,
    )


def shuffle(values, axis, bit):
    return lax.ppermute(values, axis, [(i, i ^ bit) for i in range(lax.axis_size(axis))])


def adamw(master, first, second, gradient, factor, step_rate, decay_rate):
    fix_one = 1.0 - BETA_ONE**STEP_NUMBER
    fix_two = 1.0 - BETA_TWO**STEP_NUMBER
    clipped = gradient * factor
    first = BETA_ONE * first + (1.0 - BETA_ONE) * clipped
    second = BETA_TWO * second + (1.0 - BETA_TWO) * clipped * clipped
    update = first / fix_one / (jnp.sqrt(second / fix_two) + ADAM_EPS)
    master = master - step_rate * (update + decay_rate * master)
    return (master, first, second)


def update_kernel(wide, sums_ref, index_ref, one_ref, ff_ref, q_ref, *refs):
    states, news, clip_ref = refs[:15], refs[15:30], refs[30]
    layer = pl.program_id(0)
    total = jnp.sum(jnp.sum(sums_ref[...], axis=0, keepdims=True), axis=1, keepdims=True)
    clip_norm = jnp.sqrt(total)
    factor = jnp.minimum(1.0, CLIP / clip_norm)
    clip_ref[...] = jnp.broadcast_to(clip_norm, clip_ref.shape)

    def kind(at, gradient, rate, decay):
        old = [ref[...] for ref in states[3 * at : 3 * at + 3]]
        for ref, value in zip(news[3 * at : 3 * at + 3], adamw(*old, gradient, factor, rate, decay)):
            ref[...] = value

    def all_kinds(ff, q):
        three, rows, half = news[0].shape
        kind(0, q.reshape(three, rows, half), LR_MATRIX, DECAY_MATRIX)
        kind(1, jnp.concatenate([ff[384:408], ff[416:440]], axis=1), LR_MATRIX, DECAY_MATRIX)
        kind(2, jnp.concatenate([ff[n : n + 48] for n in range(192, 384, 48)], axis=1), LR_MATRIX, DECAY_MATRIX)
        kind(3, jnp.concatenate([ff[:96], ff[96:192]], axis=1), LR_MATRIX, DECAY_MATRIX)

    @pl.when(layer == 0)
    def _():
        all_kinds(ff_ref[...], q_ref[...])
        part = states[12].shape[1]
        columns = ff_ref[NORM_ROW : NORM_ROW + 8, :128]
        mine = jnp.where(index_ref[0, 4] == 0, columns[:, :part], columns[:, part : 2 * part])
        kind(4, mine, LR_NORMS, 0.0)

    @pl.when(layer == 1)
    def _():
        all_kinds(one_ref[:FF_ROWS], one_ref[FF_ROWS:])


def update(sums, index, one, ff, q, states, wide):
    specs = [layer_at(state) for state in states[:12]] + [whole(state.shape) for state in states[12:]]
    *news, clip_norm = run(
        functools.partial(update_kernel, wide),
        (sums, index, one, ff, q, *states),
        [whole(sums.shape), IN_SMEM, whole(one.shape), whole(ff.shape), whole(q.shape)] + specs,
        specs + [whole((8, 128))],
        [shape(state.shape, F32) for state in states] + [shape((8, 128), F32)],
        (LAYERS,),
        "update",
    )
    return news, clip_norm[0, :1]


def layer_at(array):
    rest = array.shape[1:]
    return pl.BlockSpec((None,) + rest, lambda l: (l,) + (0,) * len(rest))


def shards(
    stream, seq_lengths, cotangent, w_qkv, w_out, w_in, w_back, norm_params,
    qkv_master, qkv_first, qkv_second, out_master, out_first, out_second,
    in_master, in_first, in_second, back_master, back_first, back_second,
    norm_master, norm_first, norm_second,
    wide_axes,
):
    rows, width = stream.shape
    half = w_qkv.shape[3]
    every = wide_axes + ("narrow",)
    wide = math.prod(lax.axis_size(axis) for axis in wide_axes)
    by_axes = len(wide_axes) == 3
    lengths = seq_lengths[0]
    core = lax.axis_index("narrow")
    z, y, x = (lax.axis_index(axis) for axis in wide_axes) if by_axes else (0, 0, 0)
    goes_on = (lengths[0] > rows).astype(jnp.int32)
    lane = lax.broadcasted_iota(jnp.int32, (1, 8), 1)
    here = jnp.zeros((1, 8), jnp.int32)
    for n, value in enumerate((x, y, z % 2, z // 2, core, lengths[0], lengths[1], goes_on)):
        here = jnp.where(lane == n, value, here)
    cos, sin, live = tables(here, rows)

    qkv = jnp.transpose(w_qkv, (0, 2, 1, 3))
    qkv_peer, out_peer = swap(qkv), swap(w_out)
    in_peer = swap(lax.optimization_barrier((w_in, cos, out_peer))[0])
    back_peer = None

    low = stream
    kept = []
    got = [None] * LAYERS
    for layer in range(LAYERS):
        last = layer == LAYERS - 1
        if layer == 0:
            *own, kv_own = project(low, (qkv,), layer, cos, sin)
            *peer, kv_peer = project(low, (qkv_peer,), layer, cos, sin)
            kv, kv_at = (swap(kv_peer), swap(kv_own)), (0, 0)
            back_peer = swap(lax.optimization_barrier((w_back, *kv))[0])
        else:
            *parts, kv = project(low, (qkv, qkv_peer), layer, cos, sin)
            own, peer = parts[:3], parts[3:]
            kv, kv_at = (swap(kv),) * 2, (0, 1)
        low_got = swap(low)
        m_own, m_peer, rden, ffn_in, xh1, rs1, states = attend(
            here, own, peer, kv, kv_at, w_out, out_peer, layer, low, norm_params
        )
        h_own, h_peer, slope, out, xh2, rs2 = feed(
            ffn_in, w_in, in_peer, w_back, back_peer, layer, norm_params, F32 if last else BF16,
            got[layer - 1] + (low_got,) if last else (),
        )
        got[layer] = (low_got, swap(m_peer), swap(ffn_in), swap(h_peer))
        kept.append((low, own, peer, m_own, m_peer, rden, ffn_in, xh1, rs1, states, h_own, slope, xh2, rs2))
        low = out

    up = cotangent
    norm_grads = [None] * LAYERS
    shares = [None] * LAYERS
    by_x, by_y = (lambda v: swap(v, "x")), (lambda v: swap(v, "y"))
    near, far = (lambda v: shuffle(v, "z", 1)), (lambda v: shuffle(v, "z", 2))
    after = got[LAYERS - 1][1:3]
    for layer in reversed(range(LAYERS)):
        (low, own, peer, m_own, m_peer, rden, ffn_in, xh1, rs1, states, h_own, slope, xh2, rs2) = (
            kept[layer]
        )
        low_got, m_got, ffn_got, h_got = got[layer]
        last = layer == 0
        gfb, gh_own, gh_peer, norm_grads[layer] = feed_back(
            up, None if last else live, xh2, rs2, xh1, rs1, slope, w_in, in_peer, w_back, back_peer,
            layer, norm_params, after,
        )
        gfb_got, gh_got = swap(gfb), swap(gh_peer)
        mix = (gfb, w_out, out_peer, layer, rden, m_own, m_peer, own[0], peer[0])
        back = (here, own, peer)
        norm_sum = jnp.stack(norm_grads) if last else None
        if not by_axes:
            back_grad = weight_grad(h_own, gfb[0], h_got, gfb_got[0], 512, width, "back_grad")
            in_grad = weight_grad(ffn_in, gh_own, ffn_got, gh_got, width, 512, "in_grad")
            out_grad = weight_grad(m_own, gfb[1], m_got, gfb_got[1], half, width, "out_grad")
            gx, dkv = mix_back(*mix)
            g_own, g_peer = attend_back(*back, gx, states, swap(dkv), cos, sin)
            up = input_back(g_own, g_peer, qkv, qkv_peer, layer, gfb)
            qkv_grad = weight_grad(low, g_own, low_got, swap(g_peer), width, half, "qkv_grad")
            shares[layer] = [
                lax.psum_scatter(g, wide_axes, scatter_dimension=0, tiled=True).astype(F32)
                for g in (qkv_grad, out_grad, in_grad, back_grad)
            ]
            shares[layer][0] = shares[layer][0].reshape(-1, 3, half)
            after = ()
            continue
        after = ()
        if last:
            norms = jnp.transpose(norm_sum.reshape(8, wide, width // wide), (1, 0, 2))
            norms = jnp.pad(norms, ((0, 0), (0, 0), (0, 128 - width // wide)))
            norms_got = swap(norms)
            ka, sa, kb, sb = fold_split(here, *q_first, (gfb,))
            q_second = (ka, by_y(sa), kb, by_x(sb))
            gx = None
            after = (ka,)
        else:
            norms = norms_got = jnp.zeros((wide, 8, 128), F32)
            gx, dkv = mix_back(*mix)
            after = (gx,)
        buffers = back_pack(here, h_own, gfb, h_got, gfb_got, after)
        after = ()
        if last:
            keep, send = fold_near(here, (ff_second, q_second), (buffers[0],))
            one_near = (keep, near(send))
            after = (keep,)
        buffers = column_pack(
            here, ffn_in, gh_own, ffn_got, gh_got, buffers, width, half, FF_ROWS, 2, "in_grad", after
        )
        ka, sa, kb, sb = out_pack(here, m_own, gfb, m_got, gfb_got, norms, norms_got, buffers)
        ff_first = (ka, by_x(sa), kb, by_y(sb))
        if last:
            keep, send = fold_far(here, *one_near, (ka,))
            one_far = (keep, far(send))
            gx, dkv = mix_back(*mix, (keep,))
            g_own, g_peer = attend_back(*back, gx, states, swap(dkv), cos, sin)
        else:
            g_own, g_peer, up = attend_back(
                *back, gx, states, swap(dkv), cos, sin, (ka,), (qkv, qkv_peer, layer, gfb)
            )
        g_got = swap(g_peer)
        ka, sa, kb, sb = fold_split(here, *ff_first, (g_own,))
        ff_second = (ka, by_y(sa), kb, by_x(sb))
        q_ka, q_sa, q_kb, q_sb = column_pack(
            here, low, g_own, low_got, g_got, None, half, half, Q_ROWS, 0, "qkv_grad", (ka,)
        )
        q_first = (q_ka, by_x(q_sa), q_kb, by_y(q_sb))
        after = (q_ka,)
        if not last:
            continue
        keep, send = fold_near(here, (ff_second,), (q_ka,))
        ff_near = (keep, near(send))
        up = input_back(g_own, g_peer, qkv, qkv_peer, layer, gfb, (keep,))
        ka, sa, kb, sb = fold_split(here, *q_first, (up,))
        q_second = (ka, by_y(sa), kb, by_x(sb))
        keep, send = fold_far(here, *ff_near, (ka,))
        ff_far = (keep, far(send))
        keep, send = fold_near(here, (q_second,), (keep,))
        q_near = (keep, near(send))
        one, one_squares = settle(here, *one_far, 0, (keep,))
        keep, send = fold_far(here, *q_near, (one,))
        q_far = (keep, far(send))
        ff, ff_squares = settle(here, *ff_far, width // wide // 2, (keep,))
        q, q_squares = settle(here, *q_far, 0, (ff,))

    count = wide * lax.axis_size("narrow")
    states = (
        qkv_master, qkv_first, qkv_second, out_master, out_first, out_second,
        in_master, in_first, in_second, back_master, back_first, back_second,
        norm_master, norm_first, norm_second,
    )
    exchange = lambda rows_in: lax.all_to_all(rows_in, every, 0, 0, tiled=True)
    if by_axes:
        squares = (one_squares + ff_squares + q_squares).sum(0, keepdims=True)
        sums = exchange(jnp.broadcast_to(squares, (count, 128)))
        flip = lambda array: jnp.transpose(array, (0, 2, 1, 3))
        states = tuple(flip(v) for v in states[:3]) + states[3:12] + tuple(
            v.reshape(8, -1) for v in states[12:]
        )
        new, clip_norm = update(sums, here, one, ff, q, states, wide)
        new = [flip(v) for v in new[:3]] + new[3:12] + [v.reshape(LAYERS, 4, -1) for v in new[12:]]
        return (out, up, *new, clip_norm)
    gradients = [jnp.stack([shares[l][kind] for l in range(LAYERS)]) for kind in range(4)]
    gradients.append(lax.psum_scatter(norm_sum, every, scatter_dimension=2, tiled=True))
    squares = sum(jnp.sum(g * g) for g in gradients)
    clip_norm = jnp.sqrt(exchange(jnp.broadcast_to(squares, (count, 128))).sum(0)[:1])
    factor = jnp.minimum(1.0, CLIP / clip_norm[0])
    new = []
    for kind, gradient in enumerate(gradients):
        rates = (LR_MATRIX, DECAY_MATRIX) if kind < 4 else (LR_NORMS, 0.0)
        new += adamw(*states[3 * kind : 3 * kind + 3], gradient, factor, *rates)
    return (out, up, *new, clip_norm)


def solution(mesh):
    wide_axes = ("wide",)
    if mesh.shape["wide"] == 16:
        wide_axes = ("z", "y", "x")
        mesh = Mesh(mesh.devices.reshape(4, 2, 2, 2), wide_axes + ("narrow",))
    rows = P(wide_axes + ("narrow",), None)
    qkv = P(None, wide_axes, None, "narrow")
    deep = P(None, ("narrow",) + wide_axes, None)
    in_part = P(None, wide_axes, "narrow")
    norm = P(None, None, wide_axes + ("narrow",))
    states = (qkv,) * 3 + (deep,) * 3 + (in_part,) * 3 + (deep,) * 3 + (norm,) * 3
    in_specs = (
        rows, P(wide_axes, None), rows,
        P(None, None, None, "narrow"), P(None, "narrow", None), P(None, None, "narrow"),
        P(None, "narrow", None), P(),
    ) + states
    out_specs = (rows, rows) + states + (P(),)
    return jax.shard_map(
        functools.partial(shards, wide_axes=wide_axes),
        mesh=mesh, in_specs=in_specs, out_specs=out_specs, check_vma=False,
    )
```

```python
import functools
import math

import jax
import jax.numpy as jnp
from jax import lax
from jax.experimental import pallas as pl
from jax.experimental.pallas import tpu as pltpu
from jax.sharding import Mesh
from jax.sharding import PartitionSpec as P

HEAD = 64
LAYERS = 2
CHUNK = 256
FF_BLOCK = 768
FF_CHUNK = 256
MIX_CHUNK = 512
VMEM = 64 * 1024 * 1024 - 128 * 1024
FOLD_WEIGHT = 1e12

EPS_NORM = 1e-05
CLIP = 1.0
BETA_ONE = 0.5
BETA_TWO = 0.5
ADAM_EPS = 1e-08
LR_MATRIX = 0.1
LR_NORMS = 0.5
DECAY_MATRIX = 0.1
STEP_NUMBER = 4.0

F32 = jnp.float32
BF16 = jnp.bfloat16


def run(
    kernel, args, in_specs, out_specs, out_shape, grid, name,
    scratch=(), after=(), aliases=None, weight=0, vmem=None,
):
    count, extra = len(args), len(after)

    def body(*refs):
        kernel(*refs[:count], *refs[count + extra :])

    return pl.pallas_call(
        body,
        grid=grid,
        in_specs=list(in_specs) + [pl.BlockSpec(memory_space=pl.ANY)] * extra,
        out_specs=out_specs,
        out_shape=out_shape,
        scratch_shapes=list(scratch),
        input_output_aliases=aliases or {},
        compiler_params=pltpu.CompilerParams(
            vmem_limit_bytes=vmem or VMEM, dimension_semantics=("arbitrary",) * len(grid)
        ),
        cost_estimate=pl.CostEstimate(
            flops=int(weight), bytes_accessed=int(weight), transcendentals=0
        ),
        name=name,
    )(*args, *after)


def dot(a, b):
    return jnp.dot(a, b, preferred_element_type=F32)


def dot_nt(a, b):
    return lax.dot_general(a, b, (((1,), (1,)), ((), ())), preferred_element_type=F32)


def dot_tn(a, b):
    return lax.dot_general(a, b, (((0,), (0,)), ((), ())), preferred_element_type=F32)


def low_lanes(rows):
    return lax.broadcasted_iota(jnp.int32, (rows, 128), 1) < HEAD


def shape(dims, dtype):
    return jax.ShapeDtypeStruct(dims, dtype)


IN_SMEM = pl.BlockSpec(memory_space=pltpu.SMEM)


ANY = pl.BlockSpec(memory_space=pl.ANY)


class Copies:
    def __init__(self, semaphores):
        self.semaphores = semaphores
        self.count = 0

    def start(self, source, target):
        copy = pltpu.make_async_copy(source, target, self.semaphores.at[self.count])
        self.count += 1
        copy.start()
        return copy


def whole(array_shape):
    return pl.BlockSpec(array_shape, lambda *_: (0,) * len(array_shape))


def row_spec(rows, cols, index=lambda i: i):
    return pl.BlockSpec((rows, cols), lambda i: (index(i), 0))


def layer_spec(array, layer):
    rest = array.shape[1:]
    return pl.BlockSpec((None,) + rest, lambda *_: (layer,) + (0,) * len(rest))


def wide_low_lanes(rows):
    return jnp.concatenate([low_lanes(rows)] * 2, axis=1)


def own_lanes(pair, wide_low, odd):
    zero = jnp.zeros_like(pair)
    return jnp.where(wide_low, zero, pair) if odd else jnp.where(wide_low, pair, zero)


def pair_state(features, right):
    both = dot_tn(features, right)
    return jnp.where(wide_low_lanes(128), both[:128], both[128:])


def vext_of(v_pair):
    return jnp.concatenate([v_pair, jnp.ones_like(v_pair)], axis=1)


def tables_kernel(here_ref, cos_ref, sin_ref, live_ref):
    rows = cos_ref.shape[0]
    core, first_len, second_len = lax.axis_index("narrow"), here_ref[0, 0], here_ref[0, 1]
    index = core * rows + lax.broadcasted_iota(jnp.int32, (rows, 128), 0)
    in_first = index < first_len
    in_second = jnp.logical_and(index >= first_len, index < first_len + second_len)
    live = jnp.where(jnp.logical_or(in_first, in_second), 1.0, 0.0)
    position = jnp.where(in_second, index - first_len, index).astype(F32)
    span = jnp.where(in_first, first_len, jnp.where(in_second, second_len, 1)).astype(F32)
    angle = jnp.where(live > 0.0, 0.5 * math.pi * position / span, 0.0)
    square = angle * angle
    cos = sin = jnp.zeros_like(angle)
    for n in range(7, -1, -1):
        cos = cos * square + (-1.0) ** n / math.factorial(2 * n)
        sin = sin * square + (-1.0) ** n / math.factorial(2 * n + 1)
    cos_ref[...] = cos * live
    sin_ref[...] = sin * angle * live
    live_ref[...] = live


def hands_on(lengths_ref, rows, core):
    goes_on = jnp.logical_and(lengths_ref[0, 0] > rows, lax.axis_index("narrow") == core)
    return jnp.where(goes_on, 1.0, 0.0)


def tables(here, rows):
    return run(
        tables_kernel, (here,), [IN_SMEM], [whole((rows, 128))] * 3,
        [shape((rows, 128), F32)] * 3, (1,), "tables",
    )


def project_kernel(x_ref, *refs):
    sides = (len(refs) - 3) // 4
    weights, (cos_ref, sin_ref) = refs[:sides], refs[sides : sides + 2]
    outs, kv_ref = refs[sides + 2 : -1], refs[-1]
    rows = x_ref.shape[0]
    x = x_ref[...]
    low = low_lanes(rows)
    cos, sin = cos_ref[...], sin_ref[...]
    first = pl.program_id(0) == 0

    def features(values, out_ref):
        for pair in range(values.shape[1] // 128):
            tile = jnp.maximum(values[:, pair * 128 : pair * 128 + 128], 0.0)
            along = tile * cos
            across = pltpu.roll(tile, HEAD, 1) * sin
            base = pair * 256
            out_ref[:, base : base + 128] = jnp.where(low, along, across).astype(BF16)
            out_ref[:, base + 128 : base + 256] = jnp.where(low, across, along).astype(BF16)

    for side in range(sides):
        w_ref = weights[side]
        q_ref, k_ref, v_ref = outs[3 * side : 3 * side + 3]
        other = sides - 1 - side
        v = dot(x, w_ref[2]).astype(BF16)
        v_ref[...] = v
        features(dot(x, w_ref[1]), k_ref)
        features(dot(x, w_ref[0]), q_ref)
        for pair in range(v.shape[1] // 128):
            part = pair_state(
                k_ref[:, pair * 256 : pair * 256 + 256],
                vext_of(v[:, pair * 128 : pair * 128 + 128]),
            )
            kv_ref[other, pair] = jnp.where(first, part, kv_ref[other, pair] + part)


def project(x, weights, layer, cos, sin, after=()):
    rows, width = x.shape
    half = weights[0].shape[3]
    heads = half // HEAD
    block = rows // 2
    cat = row_spec(block, heads * 128)
    return run(
        project_kernel,
        (x, *weights, cos, sin),
        [row_spec(block, width)]
        + [layer_spec(w, layer) for w in weights]
        + [row_spec(block, 128)] * 2,
        [cat, cat, row_spec(block, half)] * len(weights)
        + [whole((len(weights), heads // 2, 128, 256))],
        [
            shape((rows, heads * 128), BF16),
            shape((rows, heads * 128), BF16),
            shape((rows, half), BF16),
        ]
        * len(weights)
        + [shape((len(weights), heads // 2, 128, 256), F32)],
        (rows // block,),
        "project",
        (),
        after,
    )


def norm_rows(r, gain, shift):
    mean = jnp.mean(r, axis=1, keepdims=True)
    centered = r - mean
    var = jnp.mean(centered * centered, axis=1, keepdims=True)
    rstd = lax.rsqrt(var + EPS_NORM)
    x_hat = centered * rstd
    return x_hat * gain + shift, x_hat, rstd


def attend_kernel(
    here_ref, qo_ref, qp_ref, ko_ref, kp_ref, vo_ref, vp_ref, kvo_ref, kvp_ref, wo_ref, wp_ref,
    resid_ref, norm_ref,
    mo_ref, mp_ref, rden_ref, low_ref, xhat_ref, rstd_ref, state_out_ref,
    state,
):
    rows = qo_ref.shape[0]
    half = vo_ref.shape[1]
    pairs = half // 128

    @pl.when(pl.program_id(0) == 0)
    def _():
        carry = hands_on(here_ref, rows * pl.num_programs(0), 1)
        state[:pairs] = kvo_ref[...] * carry
        state[pairs:] = kvp_ref[...] * carry

    low = low_lanes(rows)
    row = lax.broadcasted_iota(jnp.int32, (rows, rows), 0)
    col = lax.broadcasted_iota(jnp.int32, (rows, rows), 1)
    causal = col <= row
    branch = None
    for side, (q_ref, k_ref, v_ref, m_ref, w_ref) in enumerate(
        ((qo_ref, ko_ref, vo_ref, mo_ref, wo_ref), (qp_ref, kp_ref, vp_ref, mp_ref, wp_ref))
    ):
        for pair in range(pairs):
            at = side * pairs + pair
            vext = vext_of(v_ref[:, pair * 128 : pair * 128 + 128])
            k_pair = k_ref[:, pair * 256 : pair * 256 + 256]
            q = [q_ref[:, n * 128 : n * 128 + 128] for n in (2 * pair, 2 * pair + 1)]
            kv = state[at]
            kv_low = kv.astype(BF16)
            state_out_ref[0, at] = kv_low
            far = dot(jnp.concatenate(q, axis=0), kv_low)
            sums = []
            for odd in (0, 1):
                scores = dot_nt(q[odd], k_pair[:, odd * 128 : odd * 128 + 128])
                scores = jnp.where(causal, scores, 0.0).astype(BF16)
                sums.append(dot(scores, vext) + far[odd * rows : odd * rows + rows])
            state[at] = kv + pair_state(k_pair, vext)
            num = jnp.where(low, sums[0][:, :128], sums[1][:, :128])
            den = jnp.where(low, sums[0][:, 128:], sums[1][:, 128:])
            rden = 1.0 / jnp.maximum(den, 1.0)
            base = side * half + pair * 128
            rden_low = jnp.where(den > 1.0, jnp.minimum(rden, 1.0 - 2.0**-8), 1.0)
            rden_ref[:, base : base + 128] = rden_low.astype(BF16)
            m_ref[:, pair * 128 : pair * 128 + 128] = (num * rden).astype(BF16)
        part = dot(m_ref[...], w_ref[...])
        branch = part if branch is None else branch + part
    y, x_hat, rstd = norm_rows(resid_ref[...].astype(F32) + branch, norm_ref[0:1], norm_ref[1:2])
    low_ref[...] = y.astype(BF16)
    xhat_ref[...] = x_hat.astype(BF16)
    rstd_ref[...] = jnp.broadcast_to(rstd, rstd_ref.shape)


def attend(here, own, peer, kv, kv_at, w_own, w_peer, layer, resid, norms, after=()):
    rows, width = resid.shape
    half = own[2].shape[1]
    heads = half // HEAD
    steps = rows // CHUNK
    cat, narrow = row_spec(CHUNK, heads * 128), row_spec(CHUNK, half)
    full = row_spec(CHUNK, width)
    return run(
        attend_kernel,
        (here, own[0], peer[0], own[1], peer[1], own[2], peer[2], *kv,
         w_own, w_peer, resid, norms),
        [
            IN_SMEM,
            cat, cat, cat, cat, narrow, narrow,
            *(pl.BlockSpec((None,) + a.shape[1:], lambda *_, n=n: (n, 0, 0, 0)) for a, n in zip(kv, kv_at)),
            layer_spec(w_own, layer), layer_spec(w_peer, layer),
            full, layer_spec(norms, layer),
        ],
        [
            narrow, narrow, full, full, full, row_spec(CHUNK, 128),
            pl.BlockSpec((1, heads, 128, 256), lambda i: (i, 0, 0, 0)),
        ],
        [
            shape((rows, half), BF16),
            shape((rows, half), BF16),
            shape((rows, width), BF16),
            shape((rows, width), BF16),
            shape((rows, width), BF16),
            shape((rows, 128), F32),
            shape((steps, heads, 128, 256), BF16),
        ],
        (steps,),
        "attend",
        [pltpu.VMEM((heads, 128, 256), F32)],
        after,
    )


def gelu_both(u):
    root = math.sqrt(2.0 / math.pi)
    a = root + (root * 0.044715) * (u * u)
    gate = 0.5 + 0.5 * jnp.tanh(u * a)
    act = u * gate
    return act, gate + (act - act * gate) * (6.0 * a - 4.0 * root)


def feed_kernel(
    layer,
    x_ref, wio_ref, wip_ref, wbo_ref, wbp_ref, norm_ref,
    ho_ref, hp_ref, slope_ref, out_ref, xhat_ref, rstd_ref,
    x, w_in, w_back, h, slope, acc, out, xhat, rstd, semaphores,
):
    rows = x.shape[0]
    blocks = w_in.shape[0] // 2
    width = FF_BLOCK
    copies = Copies(semaphores)
    waits = [copies.start(x_ref, x)]
    for n in range(2 * blocks):
        wi, wb = (wio_ref, wbo_ref) if n < blocks else (wip_ref, wbp_ref)
        at = pl.ds(n % blocks * width, width)
        waits.append(copies.start(wi.at[layer, :, at], w_in.at[n]))
        waits.append(copies.start(wb.at[layer, at, :], w_back.at[n]))
    waits.pop(0).wait()
    outgoing = []
    for n in range(2 * blocks):
        waits.pop(0).wait()
        waits.pop(0).wait()
        for i in range(rows // FF_CHUNK):
            at = slice(i * FF_CHUNK, i * FF_CHUNK + FF_CHUNK)
            act, deriv = gelu_both(dot(x[at, :], w_in[n]))
            act = act.astype(BF16)
            h[n, at, :] = act
            slope[n, at, :] = deriv.astype(BF16)
            base = x[at, :].astype(F32) if n == 0 else acc[at, :]
            total = base + dot(act, w_back[n])
            if n < 2 * blocks - 1:
                acc[at, :] = total
                continue
            y, x_hat, inverse = norm_rows(total, norm_ref[2:3], norm_ref[3:4])
            out[at, :] = y.astype(out.dtype)
            xhat[at, :] = x_hat.astype(BF16)
            rstd[at, :] = jnp.broadcast_to(inverse, (FF_CHUNK, 128))
            here = pl.ds(i * FF_CHUNK, FF_CHUNK)
            for source, target in ((out, out_ref), (xhat, xhat_ref), (rstd, rstd_ref)):
                outgoing.append(copies.start(source.at[here, :], target.at[here, :]))
        part = pl.ds(n % blocks * width, width)
        target = ho_ref if n < blocks else hp_ref
        outgoing.append(copies.start(h.at[n], target.at[:, part]))
        outgoing.append(copies.start(slope.at[n], slope_ref.at[:, pl.ds(n * width, width)]))
    for copy in outgoing:
        copy.wait()


def feed(x, wi_own, wi_peer, wb_own, wb_peer, layer, norms, dtype, after=()):
    rows, width = x.shape
    half = wi_own.shape[2]
    blocks = half // FF_BLOCK
    copies = 1 + 8 * blocks + 3 * (rows // FF_CHUNK)
    return run(
        functools.partial(feed_kernel, layer),
        (x, wi_own, wi_peer, wb_own, wb_peer, norms),
        [ANY] * 5 + [layer_spec(norms, layer)],
        [ANY] * 6,
        [
            shape((rows, half), BF16),
            shape((rows, half), BF16),
            shape((rows, 2 * half), BF16),
            shape((rows, width), dtype),
            shape((rows, width), BF16),
            shape((rows, 128), F32),
        ],
        (1,),
        "feed",
        [
            pltpu.VMEM((rows, width), BF16),
            pltpu.VMEM((2 * blocks, width, FF_BLOCK), BF16),
            pltpu.VMEM((2 * blocks, FF_BLOCK, width), BF16),
            pltpu.VMEM((2 * blocks, rows, FF_BLOCK), BF16),
            pltpu.VMEM((2 * blocks, rows, FF_BLOCK), BF16),
            pltpu.VMEM((rows, width), F32),
            pltpu.VMEM((rows, width), dtype),
            pltpu.VMEM((rows, width), BF16),
            pltpu.VMEM((rows, 128), F32),
            pltpu.SemaphoreType.DMA((copies,)),
        ],
        after,
    )


def feed_grid_kernel(
    x_ref, wio_ref, wip_ref, wbo_ref, wbp_ref, norm_ref,
    ho_ref, hp_ref, slope_ref, out_ref, xhat_ref, rstd_ref,
    acc,
):
    step, steps = pl.program_id(0), pl.num_programs(0)
    rows = x_ref.shape[0]

    def side(w_in, w_back, h_ref, base):
        for i in range(rows // CHUNK):
            at = slice(i * CHUNK, i * CHUNK + CHUNK)
            act, slope = gelu_both(dot(x_ref[at, :], w_in[...]))
            act = act.astype(BF16)
            h_ref[at, :] = act
            slope_ref[at, :] = slope.astype(BF16)
            acc[at, :] = base[at, :].astype(F32) + dot(act, w_back[...])

    @pl.when(step == 0)
    def _():
        side(wio_ref, wbo_ref, ho_ref, x_ref)

    @pl.when((step > 0) & (step < steps // 2))
    def _():
        side(wio_ref, wbo_ref, ho_ref, acc)

    @pl.when(step >= steps // 2)
    def _():
        side(wip_ref, wbp_ref, hp_ref, acc)

    @pl.when(step == steps - 1)
    def _():
        def part(i, _):
            at = pl.ds(pl.multiple_of(i * CHUNK, CHUNK), CHUNK)
            y, x_hat, rstd = norm_rows(acc[at, :], norm_ref[2:3], norm_ref[3:4])
            out_ref[at, :] = y.astype(out_ref.dtype)
            xhat_ref[at, :] = x_hat.astype(BF16)
            rstd_ref[at, :] = jnp.broadcast_to(rstd, (CHUNK, 128))
            return 0

        lax.fori_loop(0, rows // CHUNK, part, 0)


def ff_specs(layer, width, blocks):
    own = lambda j: jnp.minimum(j, blocks - 1)
    peer = lambda j: jnp.maximum(j - blocks, 0)
    w_in = [
        pl.BlockSpec((None, width, FF_BLOCK), lambda j, f=f: (layer, 0, f(j))) for f in (own, peer)
    ]
    w_back = [
        pl.BlockSpec((None, FF_BLOCK, width), lambda j, f=f: (layer, f(j), 0)) for f in (own, peer)
    ]
    return own, peer, w_in, w_back


def feed_grid(x, wi_own, wi_peer, wb_own, wb_peer, layer, norms, dtype, after=()):
    rows, width = x.shape
    half = wi_own.shape[2]
    blocks = half // FF_BLOCK
    own, peer, w_in, w_back = ff_specs(layer, width, blocks)
    full = whole((rows, width))
    return run(
        feed_grid_kernel,
        (x, wi_own, wi_peer, wb_own, wb_peer, norms),
        [full, *w_in, *w_back, layer_spec(norms, layer)],
        [
            pl.BlockSpec((rows, FF_BLOCK), lambda j: (0, own(j))),
            pl.BlockSpec((rows, FF_BLOCK), lambda j: (0, peer(j))),
            pl.BlockSpec((rows, FF_BLOCK), lambda j: (0, j)),
            full, full, whole((rows, 128)),
        ],
        [
            shape((rows, half), BF16),
            shape((rows, half), BF16),
            shape((rows, 2 * half), BF16),
            shape((rows, width), dtype),
            shape((rows, width), BF16),
            shape((rows, 128), F32),
        ],
        (2 * blocks,),
        "feed",
        [pltpu.VMEM((rows, width), F32)],
        after,
    )


def norm_back(y, x_hat, rstd, gain):
    scaled = y * gain
    mean = jnp.mean(scaled, axis=1, keepdims=True)
    along = jnp.mean(scaled * x_hat, axis=1, keepdims=True)
    gain_grad = jnp.sum(y * x_hat, axis=0, keepdims=True)
    shift_grad = jnp.sum(y, axis=0, keepdims=True)
    return (scaled - mean - x_hat * along) * rstd, gain_grad, shift_grad


def feed_back_kernel(
    layer, masked, *refs,
):
    count = 12 if masked else 11
    up_ref, *refs_in = refs[:count]
    live_ref = refs_in.pop(0) if masked else None
    xh2_ref, rs2_ref, xh1_ref, rs1_ref, slope_ref, wio_ref, wip_ref, wbo_ref, wbp_ref, norm_ref = refs_in
    gfb_ref, gho_ref, ghp_ref, ng_ref = refs[count : count + 4]
    up, live, xh2, rs2, xh1, rs1, slope, w_in, w_back, gfb, gh, acc, semaphores = refs[count + 4 :]
    rows, width = up.shape
    blocks = w_in.shape[0] // 2
    copies = Copies(semaphores)
    chunks = [pl.ds(i * FF_CHUNK, FF_CHUNK) for i in range(rows // FF_CHUNK)]

    def wide(value):
        return jnp.concatenate([value] * (width // 128), axis=1)

    first = []
    for at in chunks:
        pairs = [(up_ref, up), (xh2_ref, xh2), (rs2_ref, rs2)]
        if masked:
            pairs.append((live_ref, live))
        first.append([copies.start(source.at[at, :], target.at[at, :]) for source, target in pairs])
    waits = []
    for n in range(2 * blocks):
        wi, wb = (wio_ref, wbo_ref) if n < blocks else (wip_ref, wbp_ref)
        at = pl.ds(n % blocks * FF_BLOCK, FF_BLOCK)
        waits.append(copies.start(wb.at[layer, at, :], w_back.at[n]))
        waits.append(copies.start(slope_ref.at[:, pl.ds(n * FF_BLOCK, FF_BLOCK)], slope.at[n]))
        waits.append(copies.start(wi.at[layer, :, at], w_in.at[n]))
    late = [copies.start(xh1_ref, xh1), copies.start(rs1_ref, rs1)]
    sums = [None] * 4

    def add(kind, value):
        sums[kind] = value if sums[kind] is None else sums[kind] + value

    outgoing = []
    for at, arrivals in zip(chunks, first):
        for copy in arrivals:
            copy.wait()
        y = up[at, :].astype(F32)
        if masked:
            y = y * wide(live[at, :])
        grad, gain_grad, shift_grad = norm_back(
            y, xh2[at, :].astype(F32), wide(rs2[at, :]), norm_ref[2:3]
        )
        acc[at, :] = grad
        gfb[0, at, :] = grad.astype(BF16)
        add(2, gain_grad)
        add(3, shift_grad)
    outgoing.append(copies.start(gfb.at[0], gfb_ref.at[0]))
    for n in range(2 * blocks):
        for _ in range(3):
            waits.pop(0).wait()
        if n == 2 * blocks - 1:
            for copy in late:
                copy.wait()
        for at in chunks:
            act = dot_nt(gfb[0, at, :], w_back[n])
            gh_part = (act * slope[n, at, :].astype(F32)).astype(BF16)
            gh[n, at, :] = gh_part
            total = acc[at, :] + dot_nt(gh_part, w_in[n])
            if n < 2 * blocks - 1:
                acc[at, :] = total
                continue
            grad, gain_grad, shift_grad = norm_back(
                total, xh1[at, :].astype(F32), wide(rs1[at, :]), norm_ref[0:1]
            )
            gfb[1, at, :] = grad.astype(BF16)
            outgoing.append(copies.start(gfb.at[1, at, :], gfb_ref.at[1, at, :]))
            add(0, gain_grad)
            add(1, shift_grad)
        target = gho_ref if n < blocks else ghp_ref
        part = pl.ds(n % blocks * FF_BLOCK, FF_BLOCK)
        outgoing.append(copies.start(gh.at[n], target.at[:, part]))
    ng_ref[...] = jnp.concatenate(sums, axis=0)
    for copy in outgoing:
        copy.wait()


def feed_back(
    up, live, xh2, rs2, xh1, rs1, slope, wi_own, wi_peer, wb_own, wb_peer, layer, norms, after=()
):
    rows, width = up.shape
    half = wi_own.shape[2]
    blocks = half // FF_BLOCK
    chunks = rows // FF_CHUNK
    masked = live is not None
    args = (up,) + ((live,) if masked else ())
    args += (xh2, rs2, xh1, rs1, slope, wi_own, wi_peer, wb_own, wb_peer, norms)
    thin = pltpu.VMEM((rows, 128), F32)
    full = pltpu.VMEM((rows, width), BF16)
    return run(
        functools.partial(feed_back_kernel, layer, masked),
        args,
        [ANY] * (len(args) - 1) + [layer_spec(norms, layer)],
        [ANY] * 3 + [whole((4, width))],
        [
            shape((2, rows, width), BF16),
            shape((rows, half), BF16),
            shape((rows, half), BF16),
            shape((4, width), F32),
        ],
        (1,),
        "feed_back",
        [
            pltpu.VMEM((rows, width), up.dtype), thin if masked else pltpu.VMEM((8, 128), F32),
            full, thin, full, thin,
            pltpu.VMEM((2 * blocks, rows, FF_BLOCK), BF16),
            pltpu.VMEM((2 * blocks, width, FF_BLOCK), BF16),
            pltpu.VMEM((2 * blocks, FF_BLOCK, width), BF16),
            pltpu.VMEM((2, rows, width), BF16),
            pltpu.VMEM((2 * blocks, rows, FF_BLOCK), BF16),
            pltpu.VMEM((rows, width), F32),
            pltpu.SemaphoreType.DMA((5 * chunks + 8 * blocks + 3,)),
        ],
        after,
    )


def mix_back_kernel(
    layer,
    gfb_ref, wo_ref, wp_ref, rden_ref, mo_ref, mp_ref, qo_ref, qp_ref,
    gx_ref, dkv_ref,
    gb, w, rden, m, q, gx_out, semaphores,
):
    rows = MIX_CHUNK
    total_rows, half = m.shape[1:]
    pairs = half // 128
    copies = Copies(semaphores)
    arrivals, leaving = [], []
    for n in range(total_rows // rows):
        at = pl.ds(n * rows, rows)
        part = [copies.start(gfb_ref.at[1, at, :], gb.at[at, :])]
        if n == 0:
            part += [copies.start(ref.at[layer], w.at[n]) for n, ref in enumerate((wo_ref, wp_ref))]
        part.append(copies.start(rden_ref.at[at, :], rden.at[at, :]))
        for side, (m_in, q_in) in enumerate(((mo_ref, qo_ref), (mp_ref, qp_ref))):
            part.append(copies.start(m_in.at[at, :], m.at[side, at, :]))
            part.append(copies.start(q_in.at[at, :], q.at[side, at, :]))
        arrivals.append(part)
    r = lax.broadcasted_iota(jnp.int32, (256, 128), 0) % 128
    c = lax.broadcasted_iota(jnp.int32, (256, 128), 1)
    spread_c = jnp.where((r < HEAD) == (c < HEAD), -1.0 / HEAD, 0.0).astype(BF16)
    totals = [None] * (2 * pairs)
    for n in range(total_rows // rows):
        at = slice(n * rows, n * rows + rows)
        for copy in arrivals[n]:
            copy.wait()
        for side in range(2):
            gm = dot_nt(gb[at, :], w[side])
            for pair in range(pairs):
                base = side * half + pair * 128
                inverse = rden[at, base : base + 128].astype(F32)
                g = gm[:, pair * 128 : pair * 128 + 128] * inverse
                mixed = m[side, at, pair * 128 : pair * 128 + 128].astype(F32)
                prod = jnp.where(inverse < 1.0, g * mixed, 0.0)
                high = prod.astype(BF16)
                rest = (prod - high.astype(F32)).astype(BF16)
                minus_c = dot(jnp.concatenate([high, rest], axis=1), spread_c).astype(BF16)
                gx = jnp.concatenate([g.astype(BF16), minus_c], axis=1)
                gx_out[at, 2 * base : 2 * base + 256] = gx
        here = pl.ds(n * rows, rows)
        leaving.append(copies.start(gx_out.at[here, :], gx_ref.at[here, :]))
    for side in range(2):
        for pair in range(pairs):
            wide = 2 * (side * half + pair * 128)
            state = pair_state(
                q[side, :, pair * 256 : pair * 256 + 256], gx_out[:, wide : wide + 256]
            )
            dkv_ref[side * pairs + pair] = state.astype(BF16)
    for copy in leaving:
        copy.wait()


def mix_back(gfb, w_own, w_peer, layer, rden, m_own, m_peer, q_own, q_peer, after=()):
    _, rows, width = gfb.shape
    half = m_own.shape[1]
    heads = half // HEAD
    steps = rows // MIX_CHUNK
    return run(
        functools.partial(mix_back_kernel, layer),
        (gfb, w_own, w_peer, rden, m_own, m_peer, q_own, q_peer),
        [ANY] * 8,
        [ANY, whole((heads, 128, 256))],
        [
            shape((rows, 2 * width), BF16),
            shape((heads, 128, 256), BF16),
        ],
        (1,),
        "mix_back",
        [
            pltpu.VMEM((rows, width), BF16),
            pltpu.VMEM((2, half, width), BF16),
            pltpu.VMEM((rows, width), BF16),
            pltpu.VMEM((2, rows, half), BF16),
            pltpu.VMEM((2, rows, heads * 128), BF16),
            pltpu.VMEM((rows, 2 * width), BF16),
            pltpu.SemaphoreType.DMA((7 * steps + 2,)),
        ],
        after,
    )


def attend_back_kernel(
    here_ref, qo_ref, qp_ref, ko_ref, kp_ref, vo_ref, vp_ref, gx_ref, state_ref, dkv_ref,
    cos_ref, sin_ref,
    go_ref, gp_ref,
    dstate,
):
    rows = qo_ref.shape[0]
    half = vo_ref.shape[1]
    pairs = half // 128

    @pl.when(pl.program_id(0) == 0)
    def _():
        carry = hands_on(here_ref, rows * pl.num_programs(0), 0)
        for at in range(2 * pairs):
            dstate[at] = dkv_ref[(at + pairs) % (2 * pairs)].astype(F32) * carry

    low = low_lanes(rows)
    wide_low, state_low = wide_low_lanes(rows), wide_low_lanes(128)
    row = lax.broadcasted_iota(jnp.int32, (rows, rows), 0)
    col = lax.broadcasted_iota(jnp.int32, (rows, rows), 1)
    causal, anti = col <= row, row <= col
    cos, sin = cos_ref[...], sin_ref[...]
    trig = jnp.where(low, cos, sin), jnp.where(low, sin, cos)
    for side, (q_ref, k_ref, v_ref, out_ref) in enumerate(
        ((qo_ref, ko_ref, vo_ref, go_ref), (qp_ref, kp_ref, vp_ref, gp_ref))
    ):
        for pair in range(pairs):
            at = side * pairs + pair
            vext = vext_of(v_ref[:, pair * 128 : pair * 128 + 128])
            gx = gx_ref[:, at * 256 : at * 256 + 256]
            gext = [own_lanes(gx, wide_low, odd) for odd in (0, 1)]
            both = jnp.concatenate(gext, axis=0)
            ds_both = dot_nt(both, vext)
            q_far = dot_nt(both, state_ref[0, at])
            dst_both = dot_nt(vext, both)
            left_over = dstate[at].astype(BF16)
            back = [own_lanes(left_over, state_low, odd) for odd in (0, 1)]
            k_far = dot_nt(vext, jnp.concatenate(back, axis=0))
            dstate[at] += pair_state(q_ref[:, pair * 256 : pair * 256 + 256], gx)
            dq, dk, left, right = [], [], [], []
            for odd in (0, 1):
                head = 2 * pair + odd
                here = slice(odd * rows, odd * rows + rows)
                q = q_ref[:, head * 128 : head * 128 + 128]
                k = k_ref[:, head * 128 : head * 128 + 128]
                score_t = jnp.where(anti, dot_nt(k, q), 0.0).astype(BF16)
                ds = jnp.where(causal, ds_both[here], 0.0).astype(BF16)
                ds_t = jnp.where(anti, dst_both[:, here], 0.0).astype(BF16)
                q_grad = (dot(ds, k) + q_far[here]) * trig[odd]
                k_grad = (dot(ds_t, q) + k_far[:, odd * 128 : odd * 128 + 128]) * trig[odd]
                left += [score_t, k]
                right += [gext[odd][:, :128], back[odd][:, :128]]
                q_grad = q_grad + pltpu.roll(q_grad, HEAD, 1)
                k_grad = k_grad + pltpu.roll(k_grad, HEAD, 1)
                dq.append(jnp.where(q > 0, q_grad, 0.0))
                dk.append(jnp.where(k > 0, k_grad, 0.0))
            dv = dot(jnp.concatenate(left, axis=1), jnp.concatenate(right, axis=0))
            for kind, value in enumerate(
                (jnp.where(low, dq[0], dq[1]), jnp.where(low, dk[0], dk[1]), dv)
            ):
                base = kind * half + pair * 128
                out_ref[:, base : base + 128] = value.astype(BF16)


def attend_back_on_kernel(*refs):
    inputs, (wo_ref, wp_ref, first_ref), (go_ref, gp_ref, up_ref, dstate) = (
        refs[:12], refs[12:15], refs[15:],
    )
    attend_back_kernel(*inputs, go_ref, gp_ref, dstate)
    half = wo_ref.shape[2]
    total = first_ref[...].astype(F32)
    for g_ref, w_ref in ((go_ref, wo_ref), (gp_ref, wp_ref)):
        for kind in range(3):
            total = total + dot_nt(g_ref[:, kind * half : kind * half + half], w_ref[kind])
    up_ref[...] = total.astype(up_ref.dtype)


def attend_back(here, own, peer, gx, states, dkv, cos, sin, after=(), onward=None):
    rows = cos.shape[0]
    half = own[2].shape[1]
    heads = half // HEAD
    steps = rows // CHUNK
    back = lambda i: steps - 1 - i
    cat, narrow, trig = (row_spec(CHUNK, n, back) for n in (heads * 128, half, 128))
    args = (here, own[0], peer[0], own[1], peer[1], own[2], peer[2], gx, states, dkv, cos, sin)
    specs = [
        IN_SMEM,
        cat, cat, cat, cat, narrow, narrow,
        row_spec(CHUNK, heads * 256, back),
        pl.BlockSpec((1, heads, 128, 256), lambda i: (back(i), 0, 0, 0)),
        whole(dkv.shape), trig, trig,
    ]
    outs = [row_spec(CHUNK, 3 * half, back)] * 2
    shapes = [shape((rows, 3 * half), BF16)] * 2
    kernel = attend_back_kernel
    if onward is not None:
        w_own, w_peer, layer, gfb = onward
        kernel = attend_back_on_kernel
        width = gfb.shape[2]
        args += (w_own, w_peer, gfb)
        specs += [layer_spec(w_own, layer), layer_spec(w_peer, layer)]
        specs += [pl.BlockSpec((None, CHUNK, width), lambda i: (1, back(i), 0))]
        outs, shapes = outs + [row_spec(CHUNK, width, back)], shapes + [shape((rows, width), BF16)]
    return run(
        kernel, args, specs, outs, shapes, (steps,), "attend_back",
        [pltpu.VMEM((heads, 128, 256), F32)],
        after,
    )


def input_back_kernel(go_ref, gp_ref, wo_ref, wp_ref, first_ref, out_ref):
    half = wo_ref.shape[2]
    total = first_ref[...].astype(F32)
    for g_ref, w_ref in ((go_ref, wo_ref), (gp_ref, wp_ref)):
        for kind in range(3):
            total = total + dot_nt(g_ref[:, kind * half : kind * half + half], w_ref[kind])
    out_ref[...] = total.astype(out_ref.dtype)


def input_back(g_own, g_peer, w_own, w_peer, layer, gfb, after=()):
    _, rows, width = gfb.shape
    block = rows // 2
    third, full = row_spec(block, g_own.shape[1]), row_spec(block, width)
    return run(
        input_back_kernel,
        (g_own, g_peer, w_own, w_peer, gfb),
        [
            third, third, layer_spec(w_own, layer), layer_spec(w_peer, layer),
            pl.BlockSpec((None, block, width), lambda i: (1, i, 0)),
        ],
        full,
        shape((rows, width), F32),
        (rows // block,),
        "input_back",
        (),
        after,
    )


def weight_kernel(a_ref, b_ref, c_ref, d_ref, out_ref):
    out_ref[...] = (dot_tn(a_ref[...], b_ref[...]) + dot_tn(c_ref[...], d_ref[...])).astype(
        out_ref.dtype
    )


def weight_grad(a, b, c, d, block_m, block_n, name):
    rows, m = a.shape
    n = b.shape[1]
    left = pl.BlockSpec((rows, block_m), lambda i, j: (0, i))
    right = pl.BlockSpec((rows, block_n), lambda i, j: (0, j))
    return run(
        weight_kernel,
        (a, b, c, d),
        [left, right, left, right],
        pl.BlockSpec((block_m, block_n), lambda i, j: (i, j)),
        shape((m, n), BF16),
        (m // block_m, n // block_n),
        name,
    )


FF_ROWS = 448
NORM_ROW = 408


def fold_lanes(values, width):
    pieces = [values[:, at : at + width] for at in range(0, values.shape[1], width)]
    return jnp.concatenate(pieces, axis=0) if len(pieces) > 1 else values


def blocks_of(scr, rows, z_local, x_first, other, kept):
    x, y = lax.axis_index("x"), lax.axis_index("y")
    if x_first:
        spot = other * 2 + (x if kept else 1 - x)
    else:
        spot = (y if kept else 1 - y) * 2 + other
    start = pl.multiple_of((z_local * 4 + spot) * rows, 8)
    return scr[pl.ds(start, rows), :]


def spread(scr, rows, outs):
    ka, sa, kb, sb = outs
    for x_first, keep, send in ((True, ka, sa), (False, kb, sb)):
        for z in range(2):
            z_local = z if x_first else z + 2
            for other in range(2):
                for kept, out in ((True, keep), (False, send)):
                    value = blocks_of(scr, rows, z_local, x_first, other, kept)
                    out[z, other] = value.astype(BF16)


def q_pack_kernel(
    a_ref, b_ref, c_ref, d_ref, ka_ref, sa_ref, kb_ref, sb_ref, left, right, out, scr, semaphores
):
    parts, _, lanes = right.shape
    rows, m = a_ref.shape
    block = m // 16
    outs = (ka_ref, sa_ref, kb_ref, sb_ref)
    copies = Copies(semaphores)
    first = [
        copies.start(ref, left.at[pl.ds(side * rows, rows), :])
        for side, ref in enumerate((a_ref, c_ref))
    ]
    arrivals = [
        [
            copies.start(ref.at[:, pl.ds(n * lanes, lanes)], right.at[n, pl.ds(side * rows, rows), :])
            for side, ref in enumerate((b_ref, d_ref))
        ]
        for n in range(parts)
    ]
    leaving = []
    for n in range(parts):
        for copy in (first if n == 0 else []) + arrivals[n]:
            copy.wait()
        scr[n % 2] = dot_tn(left[...], right[n])
        here = slice(n * block, n * block + block)
        spread(scr.at[n % 2], block, [out.at[which, :, :, here, :] for which in range(4)])
        for which in range(4):
            at = pl.ds(n * block, block)
            leaving.append(copies.start(out.at[which, :, :, at, :], outs[which].at[:, :, at, :]))
    for copy in leaving:
        copy.wait()


def q_pack(a, b, c, d, lanes, after=()):
    rows, m = a.shape
    parts = b.shape[1] // lanes
    buffer = (2, 2, m // 16 * parts, lanes)
    return run(
        q_pack_kernel,
        (a, b, c, d),
        [ANY] * 4,
        [ANY] * 4,
        [shape(buffer, BF16)] * 4,
        (1,),
        "qkv_grad",
        [
            pltpu.VMEM((2 * rows, m), BF16),
            pltpu.VMEM((parts, 2 * rows, lanes), BF16),
            pltpu.VMEM((4,) + buffer, BF16),
            pltpu.VMEM((2, m, lanes), F32),
            pltpu.SemaphoreType.DMA((2 + 6 * parts,)),
        ],
        after,
    )


def pack_kernel(
    index_ref, ho_ref, gfb_ref, hg_ref, gfbg_ref, fi_ref, gho_ref, fg_ref, ghg_ref, mo_ref, mg_ref,
    norm_ref, norm_got_ref,
    ka_ref, sa_ref, kb_ref, sb_ref,
    h, gfb, f, gh, m, out, scr, semaphores,
):
    x, y = lax.axis_index("x"), lax.axis_index("y")
    outs = (ka_ref, sa_ref, kb_ref, sb_ref)
    lanes = out.shape[4]
    block = h.shape[2]
    columns = gh.shape[2]
    copies = Copies(semaphores)
    start = copies.start

    def both(sources, target, *at):
        rows = sources[0].shape[0]
        return [
            start(source, target.at[(*at, pl.ds(side * rows, rows))])
            for side, source in enumerate(sources)
        ]

    back_first = both((gfb_ref.at[0], gfbg_ref.at[0]), gfb, 0)
    back_parts = [
        both((ho_ref.at[:, pl.ds(n * block, block)], hg_ref.at[:, pl.ds(n * block, block)]), h, n)
        for n in range(4)
    ]
    in_first = both((fi_ref, fg_ref), f)
    in_parts = [
        both((gho_ref.at[:, pl.ds(n * columns, columns)], ghg_ref.at[:, pl.ds(n * columns, columns)]), gh, n)
        for n in range(2)
    ]
    out_parts = both((mo_ref, mg_ref), m) + both((gfb_ref.at[1], gfbg_ref.at[1]), gfb, 1)
    outgoing = []

    def wait(parts):
        for copy in parts:
            copy.wait()

    def place(slot, base, z, rows, at, tail=None):
        x_first = z < 2
        for other in range(2):
            for kept in (True, False):
                if x_first:
                    spot = other * 2 + (x if kept else 1 - x)
                else:
                    spot = (y if kept else 1 - y) * 2 + other
                value = scr[slot, pl.ds(pl.multiple_of(base + spot * rows, 8), rows), :]
                if tail is not None:
                    value = jnp.concatenate([value, tail(z * 4 + spot)], axis=0)
                value = fold_lanes(value, lanes).astype(BF16)
                which = (0 if x_first else 2) + (0 if kept else 1)
                out[which, z % 2, other, at : at + value.shape[0], :] = value

    wait(back_first)
    for z in range(4):
        wait(back_parts[z])
        scr[z % 2, :block, :] = dot_tn(h[z], gfb[0])
        place(z % 2, 0, z, block // 4, 0)
        for which in (0, 1) if z < 2 else (2, 3):
            rows = pl.ds(0, block // 2)
            outgoing.append(
                start(out.at[which, z % 2, :, rows, :], outs[which].at[z % 2, :, rows, :])
            )
    wait(in_first)
    at = block // 2
    for n in range(2):
        wait(in_parts[n])
        scr[n] = dot_tn(f[...], gh[n])
        rows = scr.shape[1] // 16
        for z in range(4):
            place(n, z * 4 * rows, z, rows, at)
        here = pl.ds(at, 2 * rows)
        at += 2 * rows
        for which in range(4):
            outgoing.append(start(out.at[which, :, :, here, :], outs[which].at[:, :, here, :]))
    wait(out_parts)
    scr[0, :block, :] = dot_tn(m[...], gfb[1])
    blank = jnp.zeros((8, scr.shape[2] - 128), F32)
    tail = lambda w: jnp.concatenate([norm_ref[w] + norm_got_ref[w], blank], axis=1)
    for z in range(4):
        place(0, z * (block // 4), z, block // 16, at, tail)
    here = pl.ds(at, 2 * (block // 16 + 8))
    for which in range(4):
        outgoing.append(start(out.at[which, :, :, here, :], outs[which].at[:, :, here, :]))
    for copy in outgoing:
        copy.wait()


def pack(index, h_own, gfb, h_got, gfb_got, ffn_in, gh_own, ffn_got, gh_got, m_own, m_got, norms, norms_got, after=()):
    rows, hidden = h_own.shape
    width = ffn_in.shape[1]
    half = m_own.shape[1]
    return run(
        pack_kernel,
        (index, h_own, gfb, h_got, gfb_got, ffn_in, gh_own, ffn_got, gh_got, m_own, m_got, norms, norms_got),
        [IN_SMEM] + [ANY] * 10 + [whole(norms.shape)] * 2,
        [ANY] * 4,
        [shape((2, 2, FF_ROWS, half), BF16)] * 4,
        (1,),
        "pack",
        [
            pltpu.VMEM((4, 2 * rows, hidden // 4), BF16),
            pltpu.VMEM((2, 2 * rows, width), BF16),
            pltpu.VMEM((2 * rows, width), BF16),
            pltpu.VMEM((2, 2 * rows, hidden // 2), BF16),
            pltpu.VMEM((2 * rows, half), BF16),
            pltpu.VMEM((4, 2, 2, FF_ROWS, half), BF16),
            pltpu.VMEM((2, width, width), F32),
            pltpu.SemaphoreType.DMA((40,)),
        ],
        after,
    )


def swap(values, axis="narrow"):
    return lax.ppermute(values, axis, [(0, 1), (1, 0)])


def sum_of(a_ref, b_ref, *at):
    return (a_ref[at].astype(F32) + b_ref[at].astype(F32)).astype(BF16)


def fold_split_kernel(index_ref, ka, ga, kb, gb, ka_out, sa_out, kb_out, sb_out):
    x, y = lax.axis_index("x"), lax.axis_index("y")
    ka_out[0] = sum_of(ka, ga, 0, y)
    sa_out[0] = sum_of(ka, ga, 0, 1 - y)
    kb_out[0] = sum_of(kb, gb, 0, x)
    sb_out[0] = sum_of(kb, gb, 0, 1 - x)


def fold_split(index, ka, ga, kb, gb, after=()):
    _, _, r, c = ka.shape
    return run(
        fold_split_kernel,
        (index, ka, ga, kb, gb),
        [IN_SMEM]
        + [pl.BlockSpec((1, 2, r, c), lambda z: (z, 0, 0, 0))] * 4,
        [pl.BlockSpec((1, r, c), lambda z: (z, 0, 0))] * 4,
        [shape((2, r, c), BF16)] * 4,
        (2,),
        "fold_split",
        (),
        after,
        weight=FOLD_WEIGHT,
    )


def fold_near_kernel(index_ref, *refs):
    z = lax.axis_index("z") % 2
    keep, send = refs[-2:]
    for half in range(2):
        done = 0
        for at in range(0, len(refs) - 2, 4):
            k, g = refs[at + 2 * half], refs[at + 2 * half + 1]
            rows = slice(done, done + k.shape[1])
            done += k.shape[1]
            keep[half, rows] = sum_of(k, g, z)
            send[half, rows] = sum_of(k, g, 1 - z)


def fold_near(index, groups, after=()):
    arrays = [array for group in groups for array in group]
    rows, lanes = sum(group[0].shape[1] for group in groups), arrays[0].shape[2]
    return run(
        fold_near_kernel,
        (index, *arrays),
        [IN_SMEM] + [whole(array.shape) for array in arrays],
        [whole((2, rows, lanes))] * 2,
        [shape((2, rows, lanes), BF16)] * 2,
        (1,),
        "fold_near",
        (),
        after,
        weight=FOLD_WEIGHT,
    )


def fold_far_kernel(index_ref, k, g, keep, send):
    z = lax.axis_index("z") // 2
    keep[...] = sum_of(k, g, z)
    send[...] = sum_of(k, g, 1 - z)


def fold_far(index, keep, got, after=()):
    return run(
        fold_far_kernel,
        (index, keep, got),
        [IN_SMEM] + [whole(keep.shape)] * 2,
        [whole(keep.shape[1:])] * 2,
        [shape(keep.shape[1:], BF16)] * 2,
        (1,),
        "fold_far",
        (),
        after,
        weight=FOLD_WEIGHT,
    )


def settle_kernel(norms, index_ref, k, g, out, squares):
    total = k[...].astype(F32) + g[...].astype(F32)
    out[...] = total
    if norms:
        row, lane = (lax.broadcasted_iota(jnp.int32, total.shape, n) for n in (0, 1))
        here = jnp.logical_and(row >= NORM_ROW, row < NORM_ROW + 8)
        other = jnp.logical_or(lane < lax.axis_index("narrow") * norms, lane >= (lax.axis_index("narrow") + 1) * norms)
        total = jnp.where(jnp.logical_and(here, other), 0.0, total)
    total = total * total
    part = total[:, :128] + total[:, 128:256] + total[:, 256:]
    squares[...] = jnp.sum(part.reshape(-1, 8, 128), axis=0)


def settle(index, keep, got, norms=0, after=()):
    return run(
        functools.partial(settle_kernel, norms),
        (index, keep, got),
        [IN_SMEM, whole(keep.shape), whole(keep.shape)],
        [whole(keep.shape), whole((8, 128))],
        [shape(keep.shape, F32), shape((8, 128), F32)],
        (1,),
        "settle",
        (),
        after,
    )


def shuffle(values, axis, bit):
    return lax.ppermute(values, axis, [(i, i ^ bit) for i in range(lax.axis_size(axis))])


def adamw(master, first, second, gradient, factor, step_rate, decay_rate):
    fix_one = 1.0 - BETA_ONE**STEP_NUMBER
    fix_two = 1.0 - BETA_TWO**STEP_NUMBER
    clipped = gradient * factor
    first = BETA_ONE * first + (1.0 - BETA_ONE) * clipped
    second = BETA_TWO * second + (1.0 - BETA_TWO) * clipped * clipped
    update = first / fix_one / (jnp.sqrt(second / fix_two) + ADAM_EPS)
    master = master - step_rate * (update + decay_rate * master)
    return (master, first, second)


def update_kernel(wide, sums_ref, index_ref, one_ref, ff_ref, q_ref, *refs):
    states, news, clip_ref = refs[:15], refs[15:30], refs[30]
    layer = pl.program_id(0)
    total = jnp.sum(jnp.sum(sums_ref[...], axis=0, keepdims=True), axis=1, keepdims=True)
    clip_norm = jnp.sqrt(total)
    factor = jnp.minimum(1.0, CLIP / clip_norm)
    clip_ref[0] = clip_norm[0, 0]

    def kind(at, gradient, rate, decay):
        old = [ref[...] for ref in states[3 * at : 3 * at + 3]]
        for ref, value in zip(news[3 * at : 3 * at + 3], adamw(*old, gradient, factor, rate, decay)):
            ref[...] = value

    def all_kinds(ff, q):
        three, rows, half = news[0].shape
        kind(0, q.reshape(three, rows, half), LR_MATRIX, DECAY_MATRIX)
        kind(1, jnp.concatenate([ff[384:408], ff[416:440]], axis=1), LR_MATRIX, DECAY_MATRIX)
        kind(2, jnp.concatenate([ff[n : n + 48] for n in range(192, 384, 48)], axis=1), LR_MATRIX, DECAY_MATRIX)
        kind(3, jnp.concatenate([ff[:96], ff[96:192]], axis=1), LR_MATRIX, DECAY_MATRIX)

    @pl.when(layer == 0)
    def _():
        all_kinds(ff_ref[...], q_ref[...])
        part = states[12].shape[1]
        columns = ff_ref[NORM_ROW : NORM_ROW + 8, :128]
        mine = jnp.where(lax.axis_index("narrow") == 0, columns[:, :part], columns[:, part : 2 * part])
        kind(4, mine, LR_NORMS, 0.0)

    @pl.when(layer == 1)
    def _():
        all_kinds(one_ref[:FF_ROWS], one_ref[FF_ROWS:])


def update(sums, index, one, ff, q, states, wide):
    specs = [layer_at(state) for state in states[:12]] + [whole(state.shape) for state in states[12:]]
    *news, clip_norm = run(
        functools.partial(update_kernel, wide),
        (sums, index, one, ff, q, *states),
        [whole(sums.shape), IN_SMEM, whole(one.shape), whole(ff.shape), whole(q.shape)] + specs,
        specs + [IN_SMEM],
        [shape(state.shape, F32) for state in states] + [shape((1,), F32)],
        (LAYERS,),
        "update",
    )
    return news, clip_norm


def layer_at(array):
    rest = array.shape[1:]
    return pl.BlockSpec((None,) + rest, lambda l: (l,) + (0,) * len(rest))


def shards(
    stream, seq_lengths, cotangent, w_qkv, w_out, w_in, w_back, norm_params,
    qkv_master, qkv_first, qkv_second, out_master, out_first, out_second,
    in_master, in_first, in_second, back_master, back_first, back_second,
    norm_master, norm_first, norm_second,
    wide_axes,
):
    rows, width = stream.shape
    half = w_qkv.shape[3]
    every = wide_axes + ("narrow",)
    wide = math.prod(lax.axis_size(axis) for axis in wide_axes)
    by_axes = len(wide_axes) == 3
    here = seq_lengths
    cos, sin, live = tables(here, rows)

    qkv = jnp.transpose(w_qkv, (0, 2, 1, 3))
    qkv_peer, out_peer = swap(qkv), swap(w_out)
    in_peer = swap(lax.optimization_barrier((w_in, cos, out_peer))[0])
    back_peer = None

    low = stream
    kept = []
    got = [None] * LAYERS
    for layer in range(LAYERS):
        last = layer == LAYERS - 1
        if layer == 0:
            *own, kv_own = project(low, (qkv,), layer, cos, sin)
            *peer, kv_peer = project(low, (qkv_peer,), layer, cos, sin)
            kv, kv_at = (swap(kv_peer), swap(kv_own)), (0, 0)
            back_peer = swap(lax.optimization_barrier((w_back, *kv))[0])
        else:
            *parts, kv = project(low, (qkv, qkv_peer), layer, cos, sin)
            own, peer = parts[:3], parts[3:]
            kv, kv_at = (swap(kv),) * 2, (0, 1)
        low_got = swap(low)
        m_own, m_peer, rden, ffn_in, xh1, rs1, states = attend(
            here, own, peer, kv, kv_at, w_out, out_peer, layer, low, norm_params
        )
        h_own, h_peer, slope, out, xh2, rs2 = (feed if last else feed_grid)(
            ffn_in, w_in, in_peer, w_back, back_peer, layer, norm_params, F32 if last else BF16,
            got[layer - 1] + (low_got,) if last else (),
        )
        got[layer] = (low_got, swap(m_peer), swap(ffn_in), swap(h_peer))
        kept.append((low, own, peer, m_own, m_peer, rden, ffn_in, xh1, rs1, states, h_own, slope, xh2, rs2))
        low = out

    up = cotangent
    norm_grads = [None] * LAYERS
    shares = [None] * LAYERS
    by_x, by_y = (lambda v: swap(v, "x")), (lambda v: swap(v, "y"))
    near, far = (lambda v: shuffle(v, "z", 1)), (lambda v: shuffle(v, "z", 2))
    after = got[LAYERS - 1][1:3]
    for layer in reversed(range(LAYERS)):
        (low, own, peer, m_own, m_peer, rden, ffn_in, xh1, rs1, states, h_own, slope, xh2, rs2) = (
            kept[layer]
        )
        low_got, m_got, ffn_got, h_got = got[layer]
        last = layer == 0
        gfb, gh_own, gh_peer, norm_grads[layer] = feed_back(
            up, None if last else live, xh2, rs2, xh1, rs1, slope, w_in, in_peer, w_back, back_peer,
            layer, norm_params, after,
        )
        gfb_got, gh_got = swap(gfb), swap(gh_peer)
        mix = (gfb, w_out, out_peer, layer, rden, m_own, m_peer, own[0], peer[0])
        back = (here, own, peer)
        norm_sum = jnp.stack(norm_grads) if last else None
        if not by_axes:
            back_grad = weight_grad(h_own, gfb[0], h_got, gfb_got[0], 512, width, "back_grad")
            in_grad = weight_grad(ffn_in, gh_own, ffn_got, gh_got, width, 512, "in_grad")
            out_grad = weight_grad(m_own, gfb[1], m_got, gfb_got[1], half, width, "out_grad")
            gx, dkv = mix_back(*mix)
            g_own, g_peer = attend_back(*back, gx, states, swap(dkv), cos, sin)
            up = input_back(g_own, g_peer, qkv, qkv_peer, layer, gfb)
            qkv_grad = weight_grad(low, g_own, low_got, swap(g_peer), width, half, "qkv_grad")
            shares[layer] = [
                lax.psum_scatter(g, wide_axes, scatter_dimension=0, tiled=True).astype(F32)
                for g in (qkv_grad, out_grad, in_grad, back_grad)
            ]
            shares[layer][0] = shares[layer][0].reshape(-1, 3, half)
            after = ()
            continue
        if last:
            norms = jnp.transpose(norm_sum.reshape(8, wide, width // wide), (1, 0, 2))
            norms = jnp.pad(norms, ((0, 0), (0, 0), (0, 128 - width // wide)))
            norms_got = swap(norms)
            ka, sa, kb, sb = fold_split(here, *q_first, (gfb,))
            keep, send = fold_near(here, (ff_second, (ka, by_y(sa), kb, by_x(sb))))
            one_near = (keep, near(send))
            after = (keep,)
        else:
            norms = norms_got = jnp.zeros((wide, 8, 128), F32)
            gx, dkv = mix_back(*mix, (h_got,))
            after = (gx,)
        ka, sa, kb, sb = pack(
            here, h_own, gfb, h_got, gfb_got, ffn_in, gh_own, ffn_got, gh_got, m_own, m_got,
            norms, norms_got, after,
        )
        ff_first = (ka, by_x(sa), kb, by_y(sb))
        if last:
            keep, send = fold_far(here, *one_near, (ka,))
            one_far = (keep, far(send))
            gx, dkv = mix_back(*mix, (keep,))
            g_own, g_peer = attend_back(*back, gx, states, swap(dkv), cos, sin)
        else:
            g_own, g_peer, up = attend_back(
                *back, gx, states, swap(dkv), cos, sin, (ka,), (qkv, qkv_peer, layer, gfb)
            )
        g_got = swap(g_peer)
        ka, sa, kb, sb = fold_split(here, *ff_first, (g_own,))
        ff_second = (ka, by_y(sa), kb, by_x(sb))
        q_ka, q_sa, q_kb, q_sb = q_pack(low, g_own, low_got, g_got, half, (ka,))
        q_first = (q_ka, by_x(q_sa), q_kb, by_y(q_sb))
        after = (q_ka,)
        if not last:
            continue
        keep, send = fold_near(here, (ff_second,), (q_ka,))
        ff_near = (keep, near(send))
        up = input_back(g_own, g_peer, qkv, qkv_peer, layer, gfb, (keep,))
        ka, sa, kb, sb = fold_split(here, *q_first, (up,))
        q_second = (ka, by_y(sa), kb, by_x(sb))
        keep, send = fold_far(here, *ff_near, (ka,))
        ff_far = (keep, far(send))
        keep, send = fold_near(here, (q_second,), (keep,))
        q_near = (keep, near(send))
        one, one_squares = settle(here, *one_far, 0, (keep,))
        keep, send = fold_far(here, *q_near, (one,))
        q_far = (keep, far(send))
        ff, ff_squares = settle(here, *ff_far, width // wide // 2, (keep,))
        q, q_squares = settle(here, *q_far, 0, (ff,))

    count = wide * lax.axis_size("narrow")
    states = (
        qkv_master, qkv_first, qkv_second, out_master, out_first, out_second,
        in_master, in_first, in_second, back_master, back_first, back_second,
        norm_master, norm_first, norm_second,
    )
    exchange = lambda rows_in: lax.all_to_all(rows_in, every, 0, 0, tiled=True)
    if by_axes:
        squares = (one_squares + ff_squares + q_squares).sum(0, keepdims=True)
        sums = exchange(jnp.broadcast_to(squares, (count, 128)))
        flip = lambda array: jnp.transpose(array, (0, 2, 1, 3))
        states = tuple(flip(v) for v in states[:3]) + states[3:12] + tuple(
            v.reshape(8, -1) for v in states[12:]
        )
        new, clip_norm = update(sums, here, one, ff, q, states, wide)
        new = [flip(v) for v in new[:3]] + new[3:12] + [v.reshape(LAYERS, 4, -1) for v in new[12:]]
        return (out, up, *new, clip_norm)
    gradients = [jnp.stack([shares[l][kind] for l in range(LAYERS)]) for kind in range(4)]
    gradients.append(lax.psum_scatter(norm_sum, every, scatter_dimension=2, tiled=True))
    squares = sum(jnp.sum(g * g) for g in gradients)
    clip_norm = jnp.sqrt(exchange(jnp.broadcast_to(squares, (count, 128))).sum(0)[:1])
    factor = jnp.minimum(1.0, CLIP / clip_norm[0])
    new = []
    for kind, gradient in enumerate(gradients):
        rates = (LR_MATRIX, DECAY_MATRIX) if kind < 4 else (LR_NORMS, 0.0)
        new += adamw(*states[3 * kind : 3 * kind + 3], gradient, factor, *rates)
    return (out, up, *new, clip_norm)


def solution(mesh):
    wide_axes = ("wide",)
    if mesh.shape["wide"] == 16:
        wide_axes = ("z", "y", "x")
        mesh = Mesh(mesh.devices.reshape(4, 2, 2, 2), wide_axes + ("narrow",))
    rows = P(wide_axes + ("narrow",), None)
    qkv = P(None, wide_axes, None, "narrow")
    deep = P(None, ("narrow",) + wide_axes, None)
    in_part = P(None, wide_axes, "narrow")
    norm = P(None, None, wide_axes + ("narrow",))
    states = (qkv,) * 3 + (deep,) * 3 + (in_part,) * 3 + (deep,) * 3 + (norm,) * 3
    in_specs = (
        rows, P(wide_axes, None), rows,
        P(None, None, None, "narrow"), P(None, "narrow", None), P(None, None, "narrow"),
        P(None, "narrow", None), P(),
    ) + states
    out_specs = (rows, rows) + states + (P(),)
    return jax.shard_map(
        functools.partial(shards, wide_axes=wide_axes),
        mesh=mesh, in_specs=in_specs, out_specs=out_specs, check_vma=False,
    )
```

```python
import functools
import math

import jax
import jax.numpy as jnp
from jax import lax
from jax.experimental import pallas as pl
from jax.experimental.pallas import tpu as pltpu
from jax.sharding import Mesh
from jax.sharding import PartitionSpec as P

HEAD = 64
LAYERS = 2
CHUNK = 256
FF_BLOCK = 768
FF_CHUNK = 256
MIX_CHUNK = 512
VMEM = 64 * 1024 * 1024 - 128 * 1024
FOLD_WEIGHT = 1e12

EPS_NORM = 1e-05
CLIP = 1.0
BETA_ONE = 0.5
BETA_TWO = 0.5
ADAM_EPS = 1e-08
LR_MATRIX = 0.1
LR_NORMS = 0.5
DECAY_MATRIX = 0.1
STEP_NUMBER = 4.0

F32 = jnp.float32
BF16 = jnp.bfloat16


def run(
    kernel, args, in_specs, out_specs, out_shape, grid, name,
    scratch=(), after=(), aliases=None, weight=0, vmem=None,
):
    count, extra = len(args), len(after)

    def body(*refs):
        kernel(*refs[:count], *refs[count + extra :])

    return pl.pallas_call(
        body,
        grid=grid,
        in_specs=list(in_specs) + [pl.BlockSpec(memory_space=pl.ANY)] * extra,
        out_specs=out_specs,
        out_shape=out_shape,
        scratch_shapes=list(scratch),
        input_output_aliases=aliases or {},
        compiler_params=pltpu.CompilerParams(
            vmem_limit_bytes=vmem or VMEM, dimension_semantics=("arbitrary",) * len(grid)
        ),
        cost_estimate=pl.CostEstimate(
            flops=int(weight), bytes_accessed=int(weight), transcendentals=0
        ),
        name=name,
    )(*args, *after)


def dot(a, b):
    return jnp.dot(a, b, preferred_element_type=F32)


def dot_nt(a, b):
    return lax.dot_general(a, b, (((1,), (1,)), ((), ())), preferred_element_type=F32)


def dot_tn(a, b):
    return lax.dot_general(a, b, (((0,), (0,)), ((), ())), preferred_element_type=F32)


def low_lanes(rows):
    return lax.broadcasted_iota(jnp.int32, (rows, 128), 1) < HEAD


def shape(dims, dtype):
    return jax.ShapeDtypeStruct(dims, dtype)


IN_SMEM = pl.BlockSpec(memory_space=pltpu.SMEM)


ANY = pl.BlockSpec(memory_space=pl.ANY)


class Copies:
    def __init__(self, semaphores):
        self.semaphores = semaphores
        self.count = 0

    def start(self, source, target):
        copy = pltpu.make_async_copy(source, target, self.semaphores.at[self.count])
        self.count += 1
        copy.start()
        return copy


def whole(array_shape):
    return pl.BlockSpec(array_shape, lambda *_: (0,) * len(array_shape))


def row_spec(rows, cols, index=lambda i: i):
    return pl.BlockSpec((rows, cols), lambda i: (index(i), 0))


def layer_spec(array, layer):
    rest = array.shape[1:]
    return pl.BlockSpec((None,) + rest, lambda *_: (layer,) + (0,) * len(rest))


def wide_low_lanes(rows):
    return jnp.concatenate([low_lanes(rows)] * 2, axis=1)


def own_lanes(pair, wide_low, odd):
    zero = jnp.zeros_like(pair)
    return jnp.where(wide_low, zero, pair) if odd else jnp.where(wide_low, pair, zero)


def pair_state(features, right):
    both = dot_tn(features, right)
    return jnp.where(wide_low_lanes(128), both[:128], both[128:])


def vext_of(v_pair):
    return jnp.concatenate([v_pair, jnp.ones_like(v_pair)], axis=1)


def tables_kernel(here_ref, cos_ref, sin_ref, live_ref):
    rows = cos_ref.shape[0]
    core, first_len, second_len = lax.axis_index("narrow"), here_ref[0, 0], here_ref[0, 1]
    index = core * rows + lax.broadcasted_iota(jnp.int32, (rows, 128), 0)
    in_first = index < first_len
    in_second = jnp.logical_and(index >= first_len, index < first_len + second_len)
    live = jnp.where(jnp.logical_or(in_first, in_second), 1.0, 0.0)
    position = jnp.where(in_second, index - first_len, index).astype(F32)
    span = jnp.where(in_first, first_len, jnp.where(in_second, second_len, 1)).astype(F32)
    angle = jnp.where(live > 0.0, 0.5 * math.pi * position / span, 0.0)
    square = angle * angle
    cos = sin = jnp.zeros_like(angle)
    for n in range(7, -1, -1):
        cos = cos * square + (-1.0) ** n / math.factorial(2 * n)
        sin = sin * square + (-1.0) ** n / math.factorial(2 * n + 1)
    cos_ref[...] = cos * live
    sin_ref[...] = sin * angle * live
    live_ref[...] = live


def hands_on(lengths_ref, rows, core):
    goes_on = jnp.logical_and(lengths_ref[0, 0] > rows, lax.axis_index("narrow") == core)
    return jnp.where(goes_on, 1.0, 0.0)


def tables(here, rows):
    return run(
        tables_kernel, (here,), [IN_SMEM], [whole((rows, 128))] * 3,
        [shape((rows, 128), F32)] * 3, (1,), "tables",
    )


def project_kernel(x_ref, *refs):
    sides = (len(refs) - 3) // 4
    weights, (cos_ref, sin_ref) = refs[:sides], refs[sides : sides + 2]
    outs, kv_ref = refs[sides + 2 : -1], refs[-1]
    rows = x_ref.shape[0]
    x = x_ref[...]
    low = low_lanes(rows)
    cos, sin = cos_ref[...], sin_ref[...]
    first = pl.program_id(0) == 0

    def features(values, out_ref):
        for pair in range(values.shape[1] // 128):
            tile = jnp.maximum(values[:, pair * 128 : pair * 128 + 128], 0.0)
            along = tile * cos
            across = pltpu.roll(tile, HEAD, 1) * sin
            base = pair * 256
            out_ref[:, base : base + 128] = jnp.where(low, along, across).astype(BF16)
            out_ref[:, base + 128 : base + 256] = jnp.where(low, across, along).astype(BF16)

    for side in range(sides):
        w_ref = weights[side]
        q_ref, k_ref, v_ref = outs[3 * side : 3 * side + 3]
        other = sides - 1 - side
        v = dot(x, w_ref[2]).astype(BF16)
        v_ref[...] = v
        features(dot(x, w_ref[1]), k_ref)
        features(dot(x, w_ref[0]), q_ref)
        for pair in range(v.shape[1] // 128):
            part = pair_state(
                k_ref[:, pair * 256 : pair * 256 + 256],
                vext_of(v[:, pair * 128 : pair * 128 + 128]),
            )
            kv_ref[other, pair] = jnp.where(first, part, kv_ref[other, pair] + part)


def project(x, weights, layer, cos, sin, after=()):
    rows, width = x.shape
    half = weights[0].shape[3]
    heads = half // HEAD
    block = rows // 2
    cat = row_spec(block, heads * 128)
    return run(
        project_kernel,
        (x, *weights, cos, sin),
        [row_spec(block, width)]
        + [layer_spec(w, layer) for w in weights]
        + [row_spec(block, 128)] * 2,
        [cat, cat, row_spec(block, half)] * len(weights)
        + [whole((len(weights), heads // 2, 128, 256))],
        [
            shape((rows, heads * 128), BF16),
            shape((rows, heads * 128), BF16),
            shape((rows, half), BF16),
        ]
        * len(weights)
        + [shape((len(weights), heads // 2, 128, 256), F32)],
        (rows // block,),
        "project",
        (),
        after,
    )


def norm_rows(r, gain, shift):
    mean = jnp.mean(r, axis=1, keepdims=True)
    centered = r - mean
    var = jnp.mean(centered * centered, axis=1, keepdims=True)
    rstd = lax.rsqrt(var + EPS_NORM)
    x_hat = centered * rstd
    return x_hat * gain + shift, x_hat, rstd


def attend_kernel(
    here_ref, qo_ref, qp_ref, ko_ref, kp_ref, vo_ref, vp_ref, kvo_ref, kvp_ref, wo_ref, wp_ref,
    resid_ref, norm_ref,
    mo_ref, mp_ref, rden_ref, low_ref, xhat_ref, rstd_ref, state_out_ref,
    state,
):
    rows = qo_ref.shape[0]
    half = vo_ref.shape[1]
    pairs = half // 128

    @pl.when(pl.program_id(0) == 0)
    def _():
        carry = hands_on(here_ref, rows * pl.num_programs(0), 1)
        state[:pairs] = kvo_ref[...] * carry
        state[pairs:] = kvp_ref[...] * carry

    low = low_lanes(rows)
    row = lax.broadcasted_iota(jnp.int32, (rows, rows), 0)
    col = lax.broadcasted_iota(jnp.int32, (rows, rows), 1)
    causal = col <= row
    branch = None
    for side, (q_ref, k_ref, v_ref, m_ref, w_ref) in enumerate(
        ((qo_ref, ko_ref, vo_ref, mo_ref, wo_ref), (qp_ref, kp_ref, vp_ref, mp_ref, wp_ref))
    ):
        for pair in range(pairs):
            at = side * pairs + pair
            vext = vext_of(v_ref[:, pair * 128 : pair * 128 + 128])
            k_pair = k_ref[:, pair * 256 : pair * 256 + 256]
            q = [q_ref[:, n * 128 : n * 128 + 128] for n in (2 * pair, 2 * pair + 1)]
            kv = state[at]
            kv_low = kv.astype(BF16)
            state_out_ref[0, at] = kv_low
            far = dot(jnp.concatenate(q, axis=0), kv_low)
            sums = []
            for odd in (0, 1):
                scores = dot_nt(q[odd], k_pair[:, odd * 128 : odd * 128 + 128])
                scores = jnp.where(causal, scores, 0.0).astype(BF16)
                sums.append(dot(scores, vext) + far[odd * rows : odd * rows + rows])
            state[at] = kv + pair_state(k_pair, vext)
            num = jnp.where(low, sums[0][:, :128], sums[1][:, :128])
            den = jnp.where(low, sums[0][:, 128:], sums[1][:, 128:])
            rden = 1.0 / jnp.maximum(den, 1.0)
            base = side * half + pair * 128
            rden_low = jnp.where(den > 1.0, jnp.minimum(rden, 1.0 - 2.0**-8), 1.0)
            rden_ref[:, base : base + 128] = rden_low.astype(BF16)
            m_ref[:, pair * 128 : pair * 128 + 128] = (num * rden).astype(BF16)
        part = dot(m_ref[...], w_ref[...])
        branch = part if branch is None else branch + part
    y, x_hat, rstd = norm_rows(resid_ref[...].astype(F32) + branch, norm_ref[0:1], norm_ref[1:2])
    low_ref[...] = y.astype(BF16)
    xhat_ref[...] = x_hat.astype(BF16)
    rstd_ref[...] = jnp.broadcast_to(rstd, rstd_ref.shape)


def attend(here, own, peer, kv, kv_at, w_own, w_peer, layer, resid, norms, after=()):
    rows, width = resid.shape
    half = own[2].shape[1]
    heads = half // HEAD
    steps = rows // CHUNK
    cat, narrow = row_spec(CHUNK, heads * 128), row_spec(CHUNK, half)
    full = row_spec(CHUNK, width)
    return run(
        attend_kernel,
        (here, own[0], peer[0], own[1], peer[1], own[2], peer[2], *kv,
         w_own, w_peer, resid, norms),
        [
            IN_SMEM,
            cat, cat, cat, cat, narrow, narrow,
            *(pl.BlockSpec((None,) + a.shape[1:], lambda *_, n=n: (n, 0, 0, 0)) for a, n in zip(kv, kv_at)),
            layer_spec(w_own, layer), layer_spec(w_peer, layer),
            full, layer_spec(norms, layer),
        ],
        [
            narrow, narrow, full, full, full, row_spec(CHUNK, 128),
            pl.BlockSpec((1, heads, 128, 256), lambda i: (i, 0, 0, 0)),
        ],
        [
            shape((rows, half), BF16),
            shape((rows, half), BF16),
            shape((rows, width), BF16),
            shape((rows, width), BF16),
            shape((rows, width), BF16),
            shape((rows, 128), F32),
            shape((steps, heads, 128, 256), BF16),
        ],
        (steps,),
        "attend",
        [pltpu.VMEM((heads, 128, 256), F32)],
        after,
    )


def gelu_both(u):
    root = math.sqrt(2.0 / math.pi)
    a = root + (root * 0.044715) * (u * u)
    gate = 0.5 + 0.5 * jnp.tanh(u * a)
    act = u * gate
    return act, gate + (act - act * gate) * (6.0 * a - 4.0 * root)


def feed_kernel(
    layer,
    x_ref, wio_ref, wip_ref, wbo_ref, wbp_ref, norm_ref,
    ho_ref, hp_ref, slope_ref, out_ref, xhat_ref, rstd_ref,
    x, w_in, w_back, h, slope, acc, out, xhat, rstd, semaphores,
):
    rows = x.shape[0]
    blocks = w_in.shape[0] // 2
    width = FF_BLOCK
    copies = Copies(semaphores)
    waits = [copies.start(x_ref, x)]
    for n in range(2 * blocks):
        wi, wb = (wio_ref, wbo_ref) if n < blocks else (wip_ref, wbp_ref)
        at = pl.ds(n % blocks * width, width)
        waits.append(copies.start(wi.at[layer, :, at], w_in.at[n]))
        waits.append(copies.start(wb.at[layer, at, :], w_back.at[n]))
    waits.pop(0).wait()
    outgoing = []
    for n in range(2 * blocks):
        waits.pop(0).wait()
        waits.pop(0).wait()
        for i in range(rows // FF_CHUNK):
            at = slice(i * FF_CHUNK, i * FF_CHUNK + FF_CHUNK)
            act, deriv = gelu_both(dot(x[at, :], w_in[n]))
            act = act.astype(BF16)
            h[n, at, :] = act
            slope[n, at, :] = deriv.astype(BF16)
            base = x[at, :].astype(F32) if n == 0 else acc[at, :]
            total = base + dot(act, w_back[n])
            if n < 2 * blocks - 1:
                acc[at, :] = total
                continue
            y, x_hat, inverse = norm_rows(total, norm_ref[2:3], norm_ref[3:4])
            out[at, :] = y.astype(out.dtype)
            xhat[at, :] = x_hat.astype(BF16)
            rstd[at, :] = jnp.broadcast_to(inverse, (FF_CHUNK, 128))
            here = pl.ds(i * FF_CHUNK, FF_CHUNK)
            for source, target in ((out, out_ref), (xhat, xhat_ref), (rstd, rstd_ref)):
                outgoing.append(copies.start(source.at[here, :], target.at[here, :]))
        part = pl.ds(n % blocks * width, width)
        target = ho_ref if n < blocks else hp_ref
        outgoing.append(copies.start(h.at[n], target.at[:, part]))
        outgoing.append(copies.start(slope.at[n], slope_ref.at[:, pl.ds(n * width, width)]))
    for copy in outgoing:
        copy.wait()


def feed(x, wi_own, wi_peer, wb_own, wb_peer, layer, norms, dtype, after=()):
    rows, width = x.shape
    half = wi_own.shape[2]
    blocks = half // FF_BLOCK
    copies = 1 + 8 * blocks + 3 * (rows // FF_CHUNK)
    return run(
        functools.partial(feed_kernel, layer),
        (x, wi_own, wi_peer, wb_own, wb_peer, norms),
        [ANY] * 5 + [layer_spec(norms, layer)],
        [ANY] * 6,
        [
            shape((rows, half), BF16),
            shape((rows, half), BF16),
            shape((rows, 2 * half), BF16),
            shape((rows, width), dtype),
            shape((rows, width), BF16),
            shape((rows, 128), F32),
        ],
        (1,),
        "feed",
        [
            pltpu.VMEM((rows, width), BF16),
            pltpu.VMEM((2 * blocks, width, FF_BLOCK), BF16),
            pltpu.VMEM((2 * blocks, FF_BLOCK, width), BF16),
            pltpu.VMEM((2 * blocks, rows, FF_BLOCK), BF16),
            pltpu.VMEM((2 * blocks, rows, FF_BLOCK), BF16),
            pltpu.VMEM((rows, width), F32),
            pltpu.VMEM((rows, width), dtype),
            pltpu.VMEM((rows, width), BF16),
            pltpu.VMEM((rows, 128), F32),
            pltpu.SemaphoreType.DMA((copies,)),
        ],
        after,
    )


def feed_grid_kernel(
    x_ref, wio_ref, wip_ref, wbo_ref, wbp_ref, norm_ref,
    ho_ref, hp_ref, slope_ref, out_ref, xhat_ref, rstd_ref,
    acc,
):
    step, steps = pl.program_id(0), pl.num_programs(0)
    rows = x_ref.shape[0]

    def side(w_in, w_back, h_ref, base):
        for i in range(rows // CHUNK):
            at = slice(i * CHUNK, i * CHUNK + CHUNK)
            act, slope = gelu_both(dot(x_ref[at, :], w_in[...]))
            act = act.astype(BF16)
            h_ref[at, :] = act
            slope_ref[at, :] = slope.astype(BF16)
            acc[at, :] = base[at, :].astype(F32) + dot(act, w_back[...])

    @pl.when(step == 0)
    def _():
        side(wio_ref, wbo_ref, ho_ref, x_ref)

    @pl.when((step > 0) & (step < steps // 2))
    def _():
        side(wio_ref, wbo_ref, ho_ref, acc)

    @pl.when(step >= steps // 2)
    def _():
        side(wip_ref, wbp_ref, hp_ref, acc)

    @pl.when(step == steps - 1)
    def _():
        def part(i, _):
            at = pl.ds(pl.multiple_of(i * CHUNK, CHUNK), CHUNK)
            y, x_hat, rstd = norm_rows(acc[at, :], norm_ref[2:3], norm_ref[3:4])
            out_ref[at, :] = y.astype(out_ref.dtype)
            xhat_ref[at, :] = x_hat.astype(BF16)
            rstd_ref[at, :] = jnp.broadcast_to(rstd, (CHUNK, 128))
            return 0

        lax.fori_loop(0, rows // CHUNK, part, 0)


def ff_specs(layer, width, blocks):
    own = lambda j: jnp.minimum(j, blocks - 1)
    peer = lambda j: jnp.maximum(j - blocks, 0)
    w_in = [
        pl.BlockSpec((None, width, FF_BLOCK), lambda j, f=f: (layer, 0, f(j))) for f in (own, peer)
    ]
    w_back = [
        pl.BlockSpec((None, FF_BLOCK, width), lambda j, f=f: (layer, f(j), 0)) for f in (own, peer)
    ]
    return own, peer, w_in, w_back


def feed_grid(x, wi_own, wi_peer, wb_own, wb_peer, layer, norms, dtype, after=()):
    rows, width = x.shape
    half = wi_own.shape[2]
    blocks = half // FF_BLOCK
    own, peer, w_in, w_back = ff_specs(layer, width, blocks)
    full = whole((rows, width))
    return run(
        feed_grid_kernel,
        (x, wi_own, wi_peer, wb_own, wb_peer, norms),
        [full, *w_in, *w_back, layer_spec(norms, layer)],
        [
            pl.BlockSpec((rows, FF_BLOCK), lambda j: (0, own(j))),
            pl.BlockSpec((rows, FF_BLOCK), lambda j: (0, peer(j))),
            pl.BlockSpec((rows, FF_BLOCK), lambda j: (0, j)),
            full, full, whole((rows, 128)),
        ],
        [
            shape((rows, half), BF16),
            shape((rows, half), BF16),
            shape((rows, 2 * half), BF16),
            shape((rows, width), dtype),
            shape((rows, width), BF16),
            shape((rows, 128), F32),
        ],
        (2 * blocks,),
        "feed",
        [pltpu.VMEM((rows, width), F32)],
        after,
    )


def norm_back(y, x_hat, rstd, gain):
    scaled = y * gain
    mean = jnp.mean(scaled, axis=1, keepdims=True)
    along = jnp.mean(scaled * x_hat, axis=1, keepdims=True)
    gain_grad = jnp.sum(y * x_hat, axis=0, keepdims=True)
    shift_grad = jnp.sum(y, axis=0, keepdims=True)
    return (scaled - mean - x_hat * along) * rstd, gain_grad, shift_grad


def feed_back_kernel(
    layer, masked, *refs,
):
    count = 12 if masked else 11
    up_ref, *refs_in = refs[:count]
    live_ref = refs_in.pop(0) if masked else None
    xh2_ref, rs2_ref, xh1_ref, rs1_ref, slope_ref, wio_ref, wip_ref, wbo_ref, wbp_ref, norm_ref = refs_in
    gfb_ref, gho_ref, ghp_ref, ng_ref = refs[count : count + 4]
    up, live, xh2, rs2, xh1, rs1, slope, w_in, w_back, gfb, gh, acc, semaphores = refs[count + 4 :]
    rows, width = up.shape
    blocks = w_in.shape[0] // 2
    copies = Copies(semaphores)
    chunks = [pl.ds(i * FF_CHUNK, FF_CHUNK) for i in range(rows // FF_CHUNK)]

    def wide(value):
        return jnp.concatenate([value] * (width // 128), axis=1)

    first = []
    for at in chunks:
        pairs = [(up_ref, up), (xh2_ref, xh2), (rs2_ref, rs2)]
        if masked:
            pairs.append((live_ref, live))
        first.append([copies.start(source.at[at, :], target.at[at, :]) for source, target in pairs])
    waits = []
    for n in range(2 * blocks):
        wi, wb = (wio_ref, wbo_ref) if n < blocks else (wip_ref, wbp_ref)
        at = pl.ds(n % blocks * FF_BLOCK, FF_BLOCK)
        waits.append(copies.start(wb.at[layer, at, :], w_back.at[n]))
        waits.append(copies.start(slope_ref.at[:, pl.ds(n * FF_BLOCK, FF_BLOCK)], slope.at[n]))
        waits.append(copies.start(wi.at[layer, :, at], w_in.at[n]))
    late = [copies.start(xh1_ref, xh1), copies.start(rs1_ref, rs1)]
    sums = [None] * 4

    def add(kind, value):
        sums[kind] = value if sums[kind] is None else sums[kind] + value

    outgoing = []
    for at, arrivals in zip(chunks, first):
        for copy in arrivals:
            copy.wait()
        y = up[at, :].astype(F32)
        if masked:
            y = y * wide(live[at, :])
        grad, gain_grad, shift_grad = norm_back(
            y, xh2[at, :].astype(F32), wide(rs2[at, :]), norm_ref[2:3]
        )
        acc[at, :] = grad
        gfb[0, at, :] = grad.astype(BF16)
        add(2, gain_grad)
        add(3, shift_grad)
    outgoing.append(copies.start(gfb.at[0], gfb_ref.at[0]))
    for n in range(2 * blocks):
        for _ in range(3):
            waits.pop(0).wait()
        if n == 2 * blocks - 1:
            for copy in late:
                copy.wait()
        for at in chunks:
            act = dot_nt(gfb[0, at, :], w_back[n])
            gh_part = (act * slope[n, at, :].astype(F32)).astype(BF16)
            gh[n, at, :] = gh_part
            total = acc[at, :] + dot_nt(gh_part, w_in[n])
            if n < 2 * blocks - 1:
                acc[at, :] = total
                continue
            grad, gain_grad, shift_grad = norm_back(
                total, xh1[at, :].astype(F32), wide(rs1[at, :]), norm_ref[0:1]
            )
            gfb[1, at, :] = grad.astype(BF16)
            outgoing.append(copies.start(gfb.at[1, at, :], gfb_ref.at[1, at, :]))
            add(0, gain_grad)
            add(1, shift_grad)
        target = gho_ref if n < blocks else ghp_ref
        part = pl.ds(n % blocks * FF_BLOCK, FF_BLOCK)
        outgoing.append(copies.start(gh.at[n], target.at[:, part]))
    ng_ref[...] = jnp.concatenate(sums, axis=0)
    for copy in outgoing:
        copy.wait()


def feed_back(
    up, live, xh2, rs2, xh1, rs1, slope, wi_own, wi_peer, wb_own, wb_peer, layer, norms, after=()
):
    rows, width = up.shape
    half = wi_own.shape[2]
    blocks = half // FF_BLOCK
    chunks = rows // FF_CHUNK
    masked = live is not None
    args = (up,) + ((live,) if masked else ())
    args += (xh2, rs2, xh1, rs1, slope, wi_own, wi_peer, wb_own, wb_peer, norms)
    thin = pltpu.VMEM((rows, 128), F32)
    full = pltpu.VMEM((rows, width), BF16)
    return run(
        functools.partial(feed_back_kernel, layer, masked),
        args,
        [ANY] * (len(args) - 1) + [layer_spec(norms, layer)],
        [ANY] * 3 + [whole((4, width))],
        [
            shape((2, rows, width), BF16),
            shape((rows, half), BF16),
            shape((rows, half), BF16),
            shape((4, width), F32),
        ],
        (1,),
        "feed_back",
        [
            pltpu.VMEM((rows, width), up.dtype), thin if masked else pltpu.VMEM((8, 128), F32),
            full, thin, full, thin,
            pltpu.VMEM((2 * blocks, rows, FF_BLOCK), BF16),
            pltpu.VMEM((2 * blocks, width, FF_BLOCK), BF16),
            pltpu.VMEM((2 * blocks, FF_BLOCK, width), BF16),
            pltpu.VMEM((2, rows, width), BF16),
            pltpu.VMEM((2 * blocks, rows, FF_BLOCK), BF16),
            pltpu.VMEM((rows, width), F32),
            pltpu.SemaphoreType.DMA((5 * chunks + 8 * blocks + 3,)),
        ],
        after,
    )


def mix_back_kernel(
    layer,
    gfb_ref, wo_ref, wp_ref, rden_ref, mo_ref, mp_ref, qo_ref, qp_ref,
    gx_ref, dkv_ref,
    gb, w, rden, m, q, gx_out, semaphores,
):
    rows = MIX_CHUNK
    total_rows, half = m.shape[1:]
    pairs = half // 128
    copies = Copies(semaphores)
    arrivals, leaving = [], []
    for n in range(total_rows // rows):
        at = pl.ds(n * rows, rows)
        part = [copies.start(gfb_ref.at[1, at, :], gb.at[at, :])]
        if n == 0:
            part += [copies.start(ref.at[layer], w.at[n]) for n, ref in enumerate((wo_ref, wp_ref))]
        part.append(copies.start(rden_ref.at[at, :], rden.at[at, :]))
        for side, (m_in, q_in) in enumerate(((mo_ref, qo_ref), (mp_ref, qp_ref))):
            part.append(copies.start(m_in.at[at, :], m.at[side, at, :]))
            part.append(copies.start(q_in.at[at, :], q.at[side, at, :]))
        arrivals.append(part)
    r = lax.broadcasted_iota(jnp.int32, (256, 128), 0) % 128
    c = lax.broadcasted_iota(jnp.int32, (256, 128), 1)
    spread_c = jnp.where((r < HEAD) == (c < HEAD), -1.0 / HEAD, 0.0).astype(BF16)
    totals = [None] * (2 * pairs)
    for n in range(total_rows // rows):
        at = slice(n * rows, n * rows + rows)
        for copy in arrivals[n]:
            copy.wait()
        for side in range(2):
            gm = dot_nt(gb[at, :], w[side])
            for pair in range(pairs):
                base = side * half + pair * 128
                inverse = rden[at, base : base + 128].astype(F32)
                g = gm[:, pair * 128 : pair * 128 + 128] * inverse
                mixed = m[side, at, pair * 128 : pair * 128 + 128].astype(F32)
                prod = jnp.where(inverse < 1.0, g * mixed, 0.0)
                high = prod.astype(BF16)
                rest = (prod - high.astype(F32)).astype(BF16)
                minus_c = dot(jnp.concatenate([high, rest], axis=1), spread_c).astype(BF16)
                gx = jnp.concatenate([g.astype(BF16), minus_c], axis=1)
                gx_out[at, 2 * base : 2 * base + 256] = gx
        here = pl.ds(n * rows, rows)
        leaving.append(copies.start(gx_out.at[here, :], gx_ref.at[here, :]))
    for side in range(2):
        for pair in range(pairs):
            wide = 2 * (side * half + pair * 128)
            state = pair_state(
                q[side, :, pair * 256 : pair * 256 + 256], gx_out[:, wide : wide + 256]
            )
            dkv_ref[side * pairs + pair] = state.astype(BF16)
    for copy in leaving:
        copy.wait()


def mix_back(gfb, w_own, w_peer, layer, rden, m_own, m_peer, q_own, q_peer, after=()):
    _, rows, width = gfb.shape
    half = m_own.shape[1]
    heads = half // HEAD
    steps = rows // MIX_CHUNK
    return run(
        functools.partial(mix_back_kernel, layer),
        (gfb, w_own, w_peer, rden, m_own, m_peer, q_own, q_peer),
        [ANY] * 8,
        [ANY, whole((heads, 128, 256))],
        [
            shape((rows, 2 * width), BF16),
            shape((heads, 128, 256), BF16),
        ],
        (1,),
        "mix_back",
        [
            pltpu.VMEM((rows, width), BF16),
            pltpu.VMEM((2, half, width), BF16),
            pltpu.VMEM((rows, width), BF16),
            pltpu.VMEM((2, rows, half), BF16),
            pltpu.VMEM((2, rows, heads * 128), BF16),
            pltpu.VMEM((rows, 2 * width), BF16),
            pltpu.SemaphoreType.DMA((7 * steps + 2,)),
        ],
        after,
    )


def attend_back_kernel(
    here_ref, qo_ref, qp_ref, ko_ref, kp_ref, vo_ref, vp_ref, gx_ref, state_ref, dkv_ref,
    cos_ref, sin_ref,
    go_ref, gpq_ref, gpk_ref, gpv_ref,
    dstate,
):
    rows = qo_ref.shape[0]
    half = vo_ref.shape[1]
    pairs = half // 128

    @pl.when(pl.program_id(0) == 0)
    def _():
        carry = hands_on(here_ref, rows * pl.num_programs(0), 0)
        for at in range(2 * pairs):
            dstate[at] = dkv_ref[(at + pairs) % (2 * pairs)].astype(F32) * carry

    low = low_lanes(rows)
    wide_low, state_low = wide_low_lanes(rows), wide_low_lanes(128)
    row = lax.broadcasted_iota(jnp.int32, (rows, rows), 0)
    col = lax.broadcasted_iota(jnp.int32, (rows, rows), 1)
    causal, anti = col <= row, row <= col
    cos, sin = cos_ref[...], sin_ref[...]
    trig = jnp.where(low, cos, sin), jnp.where(low, sin, cos)
    for side, (q_ref, k_ref, v_ref) in enumerate(
        ((qo_ref, ko_ref, vo_ref), (qp_ref, kp_ref, vp_ref))
    ):
        for pair in range(pairs):
            at = side * pairs + pair
            vext = vext_of(v_ref[:, pair * 128 : pair * 128 + 128])
            gx = gx_ref[:, at * 256 : at * 256 + 256]
            gext = [own_lanes(gx, wide_low, odd) for odd in (0, 1)]
            both = jnp.concatenate(gext, axis=0)
            ds_both = dot_nt(both, vext)
            q_far = dot_nt(both, state_ref[0, at])
            dst_both = dot_nt(vext, both)
            left_over = dstate[at].astype(BF16)
            back = [own_lanes(left_over, state_low, odd) for odd in (0, 1)]
            k_far = dot_nt(vext, jnp.concatenate(back, axis=0))
            dstate[at] += pair_state(q_ref[:, pair * 256 : pair * 256 + 256], gx)
            dq, dk, left, right = [], [], [], []
            for odd in (0, 1):
                head = 2 * pair + odd
                here = slice(odd * rows, odd * rows + rows)
                q = q_ref[:, head * 128 : head * 128 + 128]
                k = k_ref[:, head * 128 : head * 128 + 128]
                score_t = jnp.where(anti, dot_nt(k, q), 0.0).astype(BF16)
                ds = jnp.where(causal, ds_both[here], 0.0).astype(BF16)
                ds_t = jnp.where(anti, dst_both[:, here], 0.0).astype(BF16)
                q_grad = (dot(ds, k) + q_far[here]) * trig[odd]
                k_grad = (dot(ds_t, q) + k_far[:, odd * 128 : odd * 128 + 128]) * trig[odd]
                left += [score_t, k]
                right += [gext[odd][:, :128], back[odd][:, :128]]
                q_grad = q_grad + pltpu.roll(q_grad, HEAD, 1)
                k_grad = k_grad + pltpu.roll(k_grad, HEAD, 1)
                dq.append(jnp.where(q > 0, q_grad, 0.0))
                dk.append(jnp.where(k > 0, k_grad, 0.0))
            dv = dot(jnp.concatenate(left, axis=1), jnp.concatenate(right, axis=0))
            for kind, value in enumerate(
                (jnp.where(low, dq[0], dq[1]), jnp.where(low, dk[0], dk[1]), dv)
            ):
                if side == 0:
                    base = kind * half + pair * 128
                    go_ref[:, base : base + 128] = value.astype(BF16)
                else:
                    out_ref = (gpq_ref, gpk_ref, gpv_ref)[kind]
                    out_ref[:, pair * 128 : pair * 128 + 128] = value.astype(BF16)


def attend_back_on_kernel(layer, *refs):
    inputs, (wo_ref, wp_ref, gfb_ref), (go_ref, *gp_refs, up_ref), scratch = (
        refs[:12], refs[12:15], refs[15:20], refs[20:],
    )
    dstate, g, w, gb, up, semaphores = scratch
    step, steps = pl.program_id(0), pl.num_programs(0)
    rows, third = go_ref.shape[0], wo_ref.shape[3]
    total = gb.shape[0]
    pieces = [
        (ref.at[layer, kind], w.at[side, :, pl.ds(kind * third, third)])
        for side, ref in enumerate((wo_ref, wp_ref))
        for kind in range(3)
    ] + [(gfb_ref.at[1], gb)]
    copies = [pltpu.make_async_copy(*piece, semaphores.at[n]) for n, piece in enumerate(pieces)]

    @pl.when(step == 0)
    def _():
        for copy in copies:
            copy.start()

    attend_back_kernel(*inputs, go_ref, *gp_refs, dstate)
    at = pl.ds(pl.multiple_of((steps - 1 - step) * rows, rows), rows)
    g[0, at, :] = go_ref[...]
    for kind, gp_ref in enumerate(gp_refs):
        g[1, at, kind * third : kind * third + third] = gp_ref[...]

    @pl.when(step == steps - 1)
    def _():
        for copy in copies:
            copy.wait()
        leaving = []
        for n in range(2):
            part = slice(n * total // 2, (n + 1) * total // 2)
            value = gb[part, :].astype(F32)
            value = value + dot_nt(g[0, part, :], w[0]) + dot_nt(g[1, part, :], w[1])
            up[part, :] = value.astype(BF16)
            here = pl.ds(n * total // 2, total // 2)
            copy = pltpu.make_async_copy(up.at[here, :], up_ref.at[here, :], semaphores.at[7 + n])
            copy.start()
            leaving.append(copy)
        for copy in leaving:
            copy.wait()


def attend_back(here, own, peer, gx, states, dkv, cos, sin, after=(), onward=None):
    rows = cos.shape[0]
    half = own[2].shape[1]
    heads = half // HEAD
    steps = rows // CHUNK
    back = lambda i: steps - 1 - i
    cat, narrow, trig = (row_spec(CHUNK, n, back) for n in (heads * 128, half, 128))
    args = (here, own[0], peer[0], own[1], peer[1], own[2], peer[2], gx, states, dkv, cos, sin)
    specs = [
        IN_SMEM,
        cat, cat, cat, cat, narrow, narrow,
        row_spec(CHUNK, heads * 256, back),
        pl.BlockSpec((1, heads, 128, 256), lambda i: (back(i), 0, 0, 0)),
        whole(dkv.shape), trig, trig,
    ]
    outs = [row_spec(CHUNK, 3 * half, back)] + [row_spec(CHUNK, half, back)] * 3
    shapes = [shape((rows, 3 * half), BF16)] + [shape((rows, half), BF16)] * 3
    kernel = attend_back_kernel
    scratch = [pltpu.VMEM((heads, 128, 256), F32)]
    if onward is not None:
        w_own, w_peer, layer, gfb = onward
        kernel = functools.partial(attend_back_on_kernel, layer)
        width = gfb.shape[2]
        args += (w_own, w_peer, gfb)
        specs += [ANY] * 3
        outs, shapes = outs + [ANY], shapes + [shape((rows, width), BF16)]
        scratch += [
            pltpu.VMEM((2, rows, 3 * half), BF16),
            pltpu.VMEM((2, width, 3 * half), BF16),
            pltpu.VMEM((rows, width), BF16),
            pltpu.VMEM((rows, width), BF16),
            pltpu.SemaphoreType.DMA((9,)),
        ]
    return run(
        kernel, args, specs, outs, shapes, (steps,), "attend_back", scratch, after,
    )


def input_back_kernel(go_ref, gpq_ref, gpk_ref, gpv_ref, wo_ref, wp_ref, first_ref, out_ref):
    half = wo_ref.shape[2]
    total = first_ref[...].astype(F32)
    for kind, gp_ref in enumerate((gpq_ref, gpk_ref, gpv_ref)):
        total = total + dot_nt(go_ref[:, kind * half : kind * half + half], wo_ref[kind])
        total = total + dot_nt(gp_ref[...], wp_ref[kind])
    out_ref[...] = total.astype(out_ref.dtype)


def input_back(g_own, g_peer, w_own, w_peer, layer, gfb, after=()):
    _, rows, width = gfb.shape
    block = rows // 2
    third, full = row_spec(block, g_own.shape[1] // 3), row_spec(block, width)
    return run(
        input_back_kernel,
        (g_own, *g_peer, w_own, w_peer, gfb),
        [
            row_spec(block, g_own.shape[1]), third, third, third, layer_spec(w_own, layer), layer_spec(w_peer, layer),
            pl.BlockSpec((None, block, width), lambda i: (1, i, 0)),
        ],
        full,
        shape((rows, width), F32),
        (rows // block,),
        "input_back",
        (),
        after,
    )


def weight_kernel(a_ref, b_ref, c_ref, d_ref, out_ref):
    out_ref[...] = (dot_tn(a_ref[...], b_ref[...]) + dot_tn(c_ref[...], d_ref[...])).astype(
        out_ref.dtype
    )


def weight_grad(a, b, c, d, block_m, block_n, name):
    rows, m = a.shape
    n = b.shape[1]
    left = pl.BlockSpec((rows, block_m), lambda i, j: (0, i))
    right = pl.BlockSpec((rows, block_n), lambda i, j: (0, j))
    return run(
        weight_kernel,
        (a, b, c, d),
        [left, right, left, right],
        pl.BlockSpec((block_m, block_n), lambda i, j: (i, j)),
        shape((m, n), BF16),
        (m // block_m, n // block_n),
        name,
    )


FF_ROWS = 448
NORM_ROW = 408


def fold_lanes(values, width):
    pieces = [values[:, at : at + width] for at in range(0, values.shape[1], width)]
    return jnp.concatenate(pieces, axis=0) if len(pieces) > 1 else values


def blocks_of(scr, rows, z_local, x_first, other, kept):
    x, y = lax.axis_index("x"), lax.axis_index("y")
    if x_first:
        spot = other * 2 + (x if kept else 1 - x)
    else:
        spot = (y if kept else 1 - y) * 2 + other
    start = pl.multiple_of((z_local * 4 + spot) * rows, 8)
    return scr[pl.ds(start, rows), :]


def spread(scr, rows, outs):
    ka, sa, kb, sb = outs
    for x_first, keep, send in ((True, ka, sa), (False, kb, sb)):
        for z in range(2):
            z_local = z if x_first else z + 2
            for other in range(2):
                for kept, out in ((True, keep), (False, send)):
                    value = blocks_of(scr, rows, z_local, x_first, other, kept)
                    out[z, other] = value.astype(BF16)


def q_pack_kernel(
    a_ref, b_ref, c_ref, d0_ref, d1_ref, d2_ref,
    ka_ref, sa_ref, kb_ref, sb_ref,
    left, right, out, scr, semaphores,
):
    parts, _, lanes = right.shape
    rows, m = a_ref.shape
    block = m // 16
    outs = (ka_ref, sa_ref, kb_ref, sb_ref)
    copies = Copies(semaphores)
    first = [
        copies.start(ref, left.at[pl.ds(side * rows, rows), :])
        for side, ref in enumerate((a_ref, c_ref))
    ]
    arrivals = [
        [
            copies.start(b_ref.at[:, pl.ds(n * lanes, lanes)], right.at[n, pl.ds(0, rows), :]),
            copies.start(d_ref, right.at[n, pl.ds(rows, rows), :]),
        ]
        for n, d_ref in enumerate((d0_ref, d1_ref, d2_ref))
    ]
    leaving = []
    for n in range(parts):
        for copy in (first if n == 0 else []) + arrivals[n]:
            copy.wait()
        scr[n % 2] = dot_tn(left[...], right[n])
        here = slice(n * block, n * block + block)
        spread(scr.at[n % 2], block, [out.at[which, :, :, here, :] for which in range(4)])
        for which in range(4):
            at = pl.ds(n * block, block)
            leaving.append(copies.start(out.at[which, :, :, at, :], outs[which].at[:, :, at, :]))
    for copy in leaving:
        copy.wait()


def q_pack(a, b, c, d, lanes, after=()):
    rows, m = a.shape
    parts = b.shape[1] // lanes
    buffer = (2, 2, m // 16 * parts, lanes)
    return run(
        q_pack_kernel,
        (a, b, c, *d),
        [ANY] * 6,
        [ANY] * 4,
        [shape(buffer, BF16)] * 4,
        (1,),
        "qkv_grad",
        [
            pltpu.VMEM((2 * rows, m), BF16),
            pltpu.VMEM((parts, 2 * rows, lanes), BF16),
            pltpu.VMEM((4,) + buffer, BF16),
            pltpu.VMEM((2, m, lanes), F32),
            pltpu.SemaphoreType.DMA((2 + 6 * parts,)),
        ],
        after,
    )


def pack_kernel(
    index_ref, ho_ref, gfb_ref, hg_ref, gfbg_ref, fi_ref, gho_ref, fg_ref, ghg_ref, mo_ref, mg_ref,
    norm_ref, norm_got_ref,
    ka_ref, sa_ref, kb_ref, sb_ref,
    h, gfb, f, gh, m, out, scr, semaphores,
):
    x, y = lax.axis_index("x"), lax.axis_index("y")
    outs = (ka_ref, sa_ref, kb_ref, sb_ref)
    lanes = out.shape[4]
    block = h.shape[2]
    columns = gh.shape[2]
    copies = Copies(semaphores)
    start = copies.start

    def both(sources, target, *at):
        rows = sources[0].shape[0]
        return [
            start(source, target.at[(*at, pl.ds(side * rows, rows))])
            for side, source in enumerate(sources)
        ]

    back_first = both((gfb_ref.at[0], gfbg_ref.at[0]), gfb, 0)
    back_parts = [
        both((ho_ref.at[:, pl.ds(n * block, block)], hg_ref.at[:, pl.ds(n * block, block)]), h, n)
        for n in range(4)
    ]
    in_first = both((fi_ref, fg_ref), f)
    in_parts = [
        both((gho_ref.at[:, pl.ds(n * columns, columns)], ghg_ref.at[:, pl.ds(n * columns, columns)]), gh, n)
        for n in range(2)
    ]
    out_parts = both((mo_ref, mg_ref), m) + both((gfb_ref.at[1], gfbg_ref.at[1]), gfb, 1)
    outgoing = []

    def wait(parts):
        for copy in parts:
            copy.wait()

    def place(slot, base, z, rows, at, tail=None):
        x_first = z < 2
        for other in range(2):
            for kept in (True, False):
                if x_first:
                    spot = other * 2 + (x if kept else 1 - x)
                else:
                    spot = (y if kept else 1 - y) * 2 + other
                value = scr[slot, pl.ds(pl.multiple_of(base + spot * rows, 8), rows), :]
                if tail is not None:
                    value = jnp.concatenate([value, tail(z * 4 + spot)], axis=0)
                value = fold_lanes(value, lanes).astype(BF16)
                which = (0 if x_first else 2) + (0 if kept else 1)
                out[which, z % 2, other, at : at + value.shape[0], :] = value

    wait(back_first)
    for z in range(4):
        wait(back_parts[z])
        scr[z % 2, :block, :] = dot_tn(h[z], gfb[0])
        place(z % 2, 0, z, block // 4, 0)
        for which in (0, 1) if z < 2 else (2, 3):
            rows = pl.ds(0, block // 2)
            outgoing.append(
                start(out.at[which, z % 2, :, rows, :], outs[which].at[z % 2, :, rows, :])
            )
    wait(in_first)
    at = block // 2
    for n in range(2):
        wait(in_parts[n])
        scr[n] = dot_tn(f[...], gh[n])
        rows = scr.shape[1] // 16
        for z in range(4):
            place(n, z * 4 * rows, z, rows, at)
        here = pl.ds(at, 2 * rows)
        at += 2 * rows
        for which in range(4):
            outgoing.append(start(out.at[which, :, :, here, :], outs[which].at[:, :, here, :]))
    wait(out_parts)
    scr[0, :block, :] = dot_tn(m[...], gfb[1])
    blank = jnp.zeros((8, scr.shape[2] - 128), F32)
    tail = lambda w: jnp.concatenate([norm_ref[w] + norm_got_ref[w], blank], axis=1)
    for z in range(4):
        place(0, z * (block // 4), z, block // 16, at, tail)
    here = pl.ds(at, 2 * (block // 16 + 8))
    for which in range(4):
        outgoing.append(start(out.at[which, :, :, here, :], outs[which].at[:, :, here, :]))
    for copy in outgoing:
        copy.wait()


def pack(index, h_own, gfb, h_got, gfb_got, ffn_in, gh_own, ffn_got, gh_got, m_own, m_got, norms, norms_got, after=()):
    rows, hidden = h_own.shape
    width = ffn_in.shape[1]
    half = m_own.shape[1]
    return run(
        pack_kernel,
        (index, h_own, gfb, h_got, gfb_got, ffn_in, gh_own, ffn_got, gh_got, m_own, m_got, norms, norms_got),
        [IN_SMEM] + [ANY] * 10 + [whole(norms.shape)] * 2,
        [ANY] * 4,
        [shape((2, 2, FF_ROWS, half), BF16)] * 4,
        (1,),
        "pack",
        [
            pltpu.VMEM((4, 2 * rows, hidden // 4), BF16),
            pltpu.VMEM((2, 2 * rows, width), BF16),
            pltpu.VMEM((2 * rows, width), BF16),
            pltpu.VMEM((2, 2 * rows, hidden // 2), BF16),
            pltpu.VMEM((2 * rows, half), BF16),
            pltpu.VMEM((4, 2, 2, FF_ROWS, half), BF16),
            pltpu.VMEM((2, width, width), F32),
            pltpu.SemaphoreType.DMA((40,)),
        ],
        after,
    )


def swap(values, axis="narrow"):
    return lax.ppermute(values, axis, [(0, 1), (1, 0)])


def sum_of(a_ref, b_ref, *at):
    return (a_ref[at].astype(F32) + b_ref[at].astype(F32)).astype(BF16)


def fold_split_kernel(ka, ga, kb, gb, sa_ref, sb_ref, held, out, semaphores):
    other = 1 - lax.axis_index("y"), 1 - lax.axis_index("x")
    copies = Copies(semaphores)
    arrivals = {}
    for z in range(2):
        for which, (k, g) in enumerate(((ka, ga), (kb, gb))):
            arrivals[which, z] = [
                copies.start(ref.at[z, other[which]], held.at[which, n, z])
                for n, ref in enumerate((k, g))
            ]
    leaving = []
    for (which, z), pair in arrivals.items():
        for copy in pair:
            copy.wait()
        out[which, z] = sum_of(held.at[which, 0], held.at[which, 1], z)
        leaving.append(copies.start(out.at[which, z], (sa_ref, sb_ref)[which].at[z]))
    for copy in leaving:
        copy.wait()


def fold_split(ka, ga, kb, gb, after=()):
    _, _, r, c = ka.shape
    return run(
        fold_split_kernel,
        (ka, ga, kb, gb),
        [ANY] * 4,
        [ANY] * 2,
        [shape((2, r, c), BF16)] * 2,
        (1,),
        "fold_split",
        [
            pltpu.VMEM((2, 2, 2, r, c), BF16),
            pltpu.VMEM((2, 2, r, c), BF16),
            pltpu.SemaphoreType.DMA((12,)),
        ],
        after,
        weight=FOLD_WEIGHT,
    )


def fold_near_kernel(groups, *refs):
    inputs, (keep_ref, send_ref, *held, out, semaphores) = refs[: 6 * groups], refs[6 * groups :]
    mine = lax.axis_index("y"), lax.axis_index("x")
    z_mine = lax.axis_index("z") % 2
    copies = Copies(semaphores)
    arrivals = []
    for group in range(groups):
        arrays = inputs[6 * group : 6 * group + 6]
        for which in range(2):
            k, g, got = arrays[3 * which : 3 * which + 3]
            place = held[group]
            arrivals.append(
                [copies.start(ref.at[z, mine[which]], place.at[which, n, z]) for z in range(2) for n, ref in enumerate((k, g))]
                + [copies.start(got, place.at[which, 2])]
            )
    leaving = []
    done = 0
    for group in range(groups):
        rows = held[group].shape[3]
        here = pl.ds(done, rows)
        for which in range(2):
            for copy in arrivals[2 * group + which]:
                copy.wait()
            for n, (target, z) in enumerate(((send_ref, 1 - z_mine), (keep_ref, z_mine))):
                total = sum(held[group][which, m, z].astype(F32) for m in range(3))
                out[n, which, done : done + rows, :] = total.astype(BF16)
                leaving.append(copies.start(out.at[n, which, here, :], target.at[which, here, :]))
        done += rows
    for copy in leaving:
        copy.wait()


def fold_near(groups, after=()):
    arrays = [array for group in groups for array in group]
    rows, lanes = sum(group[0].shape[2] for group in groups), arrays[0].shape[3]
    return run(
        functools.partial(fold_near_kernel, len(groups)),
        arrays,
        [ANY] * len(arrays),
        [ANY] * 2,
        [shape((2, rows, lanes), BF16)] * 2,
        (1,),
        "fold_near",
        [pltpu.VMEM((2, 3, 2) + group[0].shape[2:], BF16) for group in groups]
        + [pltpu.VMEM((2, 2, rows, lanes), BF16), pltpu.SemaphoreType.DMA((14 * len(groups),))],
        after,
        weight=FOLD_WEIGHT,
    )


def fold_far_kernel(index_ref, k, g, keep, send):
    z = lax.axis_index("z") // 2
    keep[...] = sum_of(k, g, z)
    send[...] = sum_of(k, g, 1 - z)


def fold_far(index, keep, got, after=(), weight=FOLD_WEIGHT):
    return run(
        fold_far_kernel,
        (index, keep, got),
        [IN_SMEM] + [whole(keep.shape)] * 2,
        [whole(keep.shape[1:])] * 2,
        [shape(keep.shape[1:], BF16)] * 2,
        (1,),
        "fold_far",
        (),
        after,
        weight=weight,
    )


def settle_kernel(norms, *refs):
    out, squares = refs[-2:]
    done = 0
    parts = 0.0
    for at in range(0, len(refs) - 2, 2):
        total = refs[at][...].astype(F32) + refs[at + 1][...].astype(F32)
        out[done : done + total.shape[0], :] = total
        if norms and done == 0:
            core = lax.axis_index("narrow")
            row, lane = (lax.broadcasted_iota(jnp.int32, total.shape, n) for n in (0, 1))
            shared = jnp.logical_and(row >= NORM_ROW, row < NORM_ROW + 8)
            other = jnp.logical_or(lane < core * norms, lane >= (core + 1) * norms)
            total = jnp.where(jnp.logical_and(shared, other), 0.0, total)
        done += total.shape[0]
        total = total * total
        part = total[:, :128] + total[:, 128:256] + total[:, 256:]
        parts = parts + jnp.sum(part.reshape(-1, 8, 128), axis=0)
    squares[...] = parts


def settle(pairs, norms=0, after=()):
    arrays = [array for pair in pairs for array in pair]
    rows, lanes = sum(pair[0].shape[0] for pair in pairs), arrays[0].shape[1]
    return run(
        functools.partial(settle_kernel, norms),
        arrays,
        [whole(array.shape) for array in arrays],
        [whole((rows, lanes)), whole((8, 128))],
        [shape((rows, lanes), F32), shape((8, 128), F32)],
        (1,),
        "settle",
        (),
        after,
    )


def shuffle(values, axis, bit):
    return lax.ppermute(values, axis, [(i, i ^ bit) for i in range(lax.axis_size(axis))])


def adamw(master, first, second, gradient, factor, step_rate, decay_rate):
    fix_one = 1.0 - BETA_ONE**STEP_NUMBER
    fix_two = 1.0 - BETA_TWO**STEP_NUMBER
    clipped = gradient * factor
    first = BETA_ONE * first + (1.0 - BETA_ONE) * clipped
    second = BETA_TWO * second + (1.0 - BETA_TWO) * clipped * clipped
    update = first / fix_one / (jnp.sqrt(second / fix_two) + ADAM_EPS)
    master = master - step_rate * (update + decay_rate * master)
    return (master, first, second)


def update_kernel(sums_ref, zero_ref, one_ref, *refs):
    states, news, clip_ref = refs[:15], refs[15:30], refs[30]
    layer = pl.program_id(0)
    total = jnp.sum(jnp.sum(sums_ref[...], axis=0, keepdims=True), axis=1, keepdims=True)
    clip_norm = jnp.sqrt(total)
    factor = jnp.minimum(1.0, CLIP / clip_norm)
    clip_ref[0] = clip_norm[0, 0]

    def kind(at, gradient, rate, decay):
        old = [ref[...] for ref in states[3 * at : 3 * at + 3]]
        for ref, value in zip(news[3 * at : 3 * at + 3], adamw(*old, gradient, factor, rate, decay)):
            ref[...] = value

    def all_kinds(grads):
        kind(0, grads[FF_ROWS:].reshape(news[0].shape), LR_MATRIX, DECAY_MATRIX)
        kind(1, jnp.concatenate([grads[384:408], grads[416:440]], axis=1), LR_MATRIX, DECAY_MATRIX)
        parts = [grads[at : at + 48] for at in range(192, 384, 48)]
        kind(2, jnp.concatenate(parts, axis=1), LR_MATRIX, DECAY_MATRIX)
        kind(3, jnp.concatenate([grads[:96], grads[96:192]], axis=1), LR_MATRIX, DECAY_MATRIX)

    @pl.when(layer == 0)
    def _():
        all_kinds(zero_ref[...])
        part = states[12].shape[1]
        columns = zero_ref[NORM_ROW : NORM_ROW + 8, :128]
        mine = jnp.where(lax.axis_index("narrow") == 0, columns[:, :part], columns[:, part : 2 * part])
        kind(4, mine, LR_NORMS, 0.0)

    @pl.when(layer == 1)
    def _():
        all_kinds(one_ref[...])


def update(sums, zero, one, states):
    specs = [layer_at(state) for state in states[:12]] + [whole(state.shape) for state in states[12:]]
    *news, clip_norm = run(
        update_kernel,
        (sums, zero, one, *states),
        [whole(sums.shape), whole(zero.shape), whole(one.shape)] + specs,
        specs + [IN_SMEM],
        [shape(state.shape, F32) for state in states] + [shape((1,), F32)],
        (LAYERS,),
        "update",
    )
    return news, clip_norm


def layer_at(array):
    rest = array.shape[1:]
    return pl.BlockSpec((None,) + rest, lambda l: (l,) + (0,) * len(rest))


def shards(
    stream, seq_lengths, cotangent, w_qkv, w_out, w_in, w_back, norm_params,
    qkv_master, qkv_first, qkv_second, out_master, out_first, out_second,
    in_master, in_first, in_second, back_master, back_first, back_second,
    norm_master, norm_first, norm_second,
    wide_axes,
):
    rows, width = stream.shape
    half = w_qkv.shape[3]
    every = wide_axes + ("narrow",)
    wide = math.prod(lax.axis_size(axis) for axis in wide_axes)
    by_axes = len(wide_axes) == 3
    here = seq_lengths
    cos, sin, live = tables(here, rows)

    qkv = jnp.transpose(w_qkv, (0, 2, 1, 3))
    qkv_peer, out_peer = swap(qkv), swap(w_out)
    in_peer = swap(lax.optimization_barrier((w_in, cos, out_peer))[0])
    back_peer = None

    low = stream
    kept = []
    got = [None] * LAYERS
    for layer in range(LAYERS):
        last = layer == LAYERS - 1
        if layer == 0:
            *own, kv_own = project(low, (qkv,), layer, cos, sin)
            *peer, kv_peer = project(low, (qkv_peer,), layer, cos, sin)
            kv, kv_at = (swap(kv_peer), swap(kv_own)), (0, 0)
            back_peer = swap(lax.optimization_barrier((w_back, *kv))[0])
        else:
            *parts, kv = project(low, (qkv, qkv_peer), layer, cos, sin)
            own, peer = parts[:3], parts[3:]
            kv, kv_at = (swap(kv),) * 2, (0, 1)
        low_got = swap(low)
        m_own, m_peer, rden, ffn_in, xh1, rs1, states = attend(
            here, own, peer, kv, kv_at, w_out, out_peer, layer, low, norm_params
        )
        h_own, h_peer, slope, out, xh2, rs2 = (feed if last else feed_grid)(
            ffn_in, w_in, in_peer, w_back, back_peer, layer, norm_params, F32 if last else BF16,
            got[layer - 1] + (low_got,) if last else (),
        )
        got[layer] = (low_got, swap(m_peer), swap(ffn_in), swap(h_peer))
        kept.append((low, own, peer, m_own, m_peer, rden, ffn_in, xh1, rs1, states, h_own, slope, xh2, rs2))
        low = out

    up = cotangent
    norm_grads = [None] * LAYERS
    shares = [None] * LAYERS
    by_x, by_y = (lambda v: swap(v, "x")), (lambda v: swap(v, "y"))
    near, far = (lambda v: shuffle(v, "z", 1)), (lambda v: shuffle(v, "z", 2))
    after = got[LAYERS - 1][1:3]
    for layer in reversed(range(LAYERS)):
        (low, own, peer, m_own, m_peer, rden, ffn_in, xh1, rs1, states, h_own, slope, xh2, rs2) = (
            kept[layer]
        )
        low_got, m_got, ffn_got, h_got = got[layer]
        last = layer == 0
        gfb, gh_own, gh_peer, norm_grads[layer] = feed_back(
            up, None if last else live, xh2, rs2, xh1, rs1, slope, w_in, in_peer, w_back, back_peer,
            layer, norm_params, after,
        )
        gfb_got, gh_got = swap(gfb), swap(gh_peer)
        mix = (gfb, w_out, out_peer, layer, rden, m_own, m_peer, own[0], peer[0])
        back = (here, own, peer)
        norm_sum = jnp.stack(norm_grads) if last else None
        if not by_axes:
            back_grad = weight_grad(h_own, gfb[0], h_got, gfb_got[0], 512, width, "back_grad")
            in_grad = weight_grad(ffn_in, gh_own, ffn_got, gh_got, width, 512, "in_grad")
            out_grad = weight_grad(m_own, gfb[1], m_got, gfb_got[1], half, width, "out_grad")
            gx, dkv = mix_back(*mix)
            g_own, *g_peer = attend_back(*back, gx, states, swap(dkv), cos, sin)
            up = input_back(g_own, g_peer, qkv, qkv_peer, layer, gfb)
            g_got = jnp.concatenate([swap(g) for g in g_peer], axis=1)
            qkv_grad = weight_grad(low, g_own, low_got, g_got, width, half, "qkv_grad")
            shares[layer] = [
                lax.psum_scatter(g, wide_axes, scatter_dimension=0, tiled=True).astype(F32)
                for g in (qkv_grad, out_grad, in_grad, back_grad)
            ]
            shares[layer][0] = shares[layer][0].reshape(-1, 3, half)
            after = ()
            continue
        if last:
            norms = jnp.transpose(norm_sum.reshape(8, wide, width // wide), (1, 0, 2))
            norms = jnp.pad(norms, ((0, 0), (0, 0), (0, 128 - width // wide)))
            norms_got = swap(norms)
            sa, sb = fold_split(*q_first, (gfb,))
            q_second = q_first[:2] + (by_y(sa),) + q_first[2:] + (by_x(sb),)
            after = (sa,)
        else:
            norms = norms_got = jnp.zeros((wide, 8, 128), F32)
            after = (h_got,)
        gx, dkv = mix_back(*mix, after)
        dkv_got = swap(dkv)
        ka, sa, kb, sb = pack(
            here, h_own, gfb, h_got, gfb_got, ffn_in, gh_own, ffn_got, gh_got, m_own, m_got,
            norms, norms_got, (dkv_got,),
        )
        ff_first = (ka, by_x(sa), kb, by_y(sb))
        if last:
            keep, send = fold_near((ff_second, q_second), (ka,))
            one_near = (keep, near(send))
            g_own, *g_peer = attend_back(*back, gx, states, dkv_got, cos, sin, (keep,))
            keep, send = fold_far(here, *one_near, (g_own,), 0)
            one_far = (keep, far(send))
            after = (keep,)
        else:
            g_own, *g_peer, up = attend_back(
                *back, gx, states, dkv_got, cos, sin, (ka,), (qkv, qkv_peer, layer, gfb)
            )
            after = (g_own,)
        g_got = [swap(g) for g in g_peer]
        if last:
            sa, sb = fold_split(*ff_first, after)
            ff_second = ff_first[:2] + (by_y(sa),) + ff_first[2:] + (by_x(sb),)
            after = (sa,)
        q_ka, q_sa, q_kb, q_sb = q_pack(low, g_own, low_got, g_got, half, after)
        q_first = (q_ka, by_x(q_sa), q_kb, by_y(q_sb))
        if not last:
            sa, sb = fold_split(*ff_first, (q_ka,))
            ff_second = ff_first[:2] + (by_y(sa),) + ff_first[2:] + (by_x(sb),)
            after = (sa,)
            continue
        keep, send = fold_near((ff_second,), (q_ka,))
        ff_near = (keep, near(send))
        up = input_back(g_own, g_peer, qkv, qkv_peer, layer, gfb, (keep,))
        sa, sb = fold_split(*q_first, (up,))
        q_second = q_first[:2] + (by_y(sa),) + q_first[2:] + (by_x(sb),)
        ff_keep, ff_send = fold_far(here, *ff_near, (sa,))
        one, one_squares = settle((one_far,), 0, (ff_keep,))
        keep, send = fold_near((q_second,), (one,))
        q_near = (keep, near(send))
        ff_far = (ff_keep, far(ff_send))
        keep, send = fold_far(here, *q_near, (), 0)
        zero, zero_squares = settle((ff_far, (keep, far(send))), width // wide // 2)

    count = wide * lax.axis_size("narrow")
    states = (
        qkv_master, qkv_first, qkv_second, out_master, out_first, out_second,
        in_master, in_first, in_second, back_master, back_first, back_second,
        norm_master, norm_first, norm_second,
    )
    exchange = lambda rows_in: lax.all_to_all(rows_in, every, 0, 0, tiled=True)
    if by_axes:
        squares = (one_squares + zero_squares).sum(0, keepdims=True)
        sums = exchange(jnp.broadcast_to(squares, (count, 128)))
        flip = lambda array: jnp.transpose(array, (0, 2, 1, 3))
        states = tuple(flip(v) for v in states[:3]) + states[3:12] + tuple(
            v.reshape(8, -1) for v in states[12:]
        )
        new, clip_norm = update(sums, zero, one, states)
        new = [flip(v) for v in new[:3]] + new[3:12] + [v.reshape(LAYERS, 4, -1) for v in new[12:]]
        return (out, up, *new, clip_norm)
    gradients = [jnp.stack([shares[l][kind] for l in range(LAYERS)]) for kind in range(4)]
    gradients.append(lax.psum_scatter(norm_sum, every, scatter_dimension=2, tiled=True))
    squares = sum(jnp.sum(g * g) for g in gradients)
    clip_norm = jnp.sqrt(exchange(jnp.broadcast_to(squares, (count, 128))).sum(0)[:1])
    factor = jnp.minimum(1.0, CLIP / clip_norm[0])
    new = []
    for kind, gradient in enumerate(gradients):
        rates = (LR_MATRIX, DECAY_MATRIX) if kind < 4 else (LR_NORMS, 0.0)
        new += adamw(*states[3 * kind : 3 * kind + 3], gradient, factor, *rates)
    return (out, up, *new, clip_norm)


def solution(mesh):
    wide_axes = ("wide",)
    if mesh.shape["wide"] == 16:
        wide_axes = ("z", "y", "x")
        mesh = Mesh(mesh.devices.reshape(4, 2, 2, 2), wide_axes + ("narrow",))
    rows = P(wide_axes + ("narrow",), None)
    qkv = P(None, wide_axes, None, "narrow")
    deep = P(None, ("narrow",) + wide_axes, None)
    in_part = P(None, wide_axes, "narrow")
    norm = P(None, None, wide_axes + ("narrow",))
    states = (qkv,) * 3 + (deep,) * 3 + (in_part,) * 3 + (deep,) * 3 + (norm,) * 3
    in_specs = (
        rows, P(wide_axes, None), rows,
        P(None, None, None, "narrow"), P(None, "narrow", None), P(None, None, "narrow"),
        P(None, "narrow", None), P(),
    ) + states
    out_specs = (rows, rows) + states + (P(),)
    return jax.shard_map(
        functools.partial(shards, wide_axes=wide_axes),
        mesh=mesh, in_specs=in_specs, out_specs=out_specs, check_vma=False,
    )
```

```python
import functools
import math

import jax
import jax.numpy as jnp
from jax import lax
from jax.experimental import pallas as pl
from jax.experimental.pallas import tpu as pltpu
from jax.sharding import Mesh
from jax.sharding import PartitionSpec as P

HEAD = 64
LAYERS = 2
CHUNK = 256
FF_BLOCK = 768
FF_CHUNK = 256
MIX_CHUNK = 512
VMEM = 64 * 1024 * 1024 - 128 * 1024
FOLD_WEIGHT = 1e12

EPS_NORM = 1e-05
CLIP = 1.0
BETA_ONE = 0.5
BETA_TWO = 0.5
ADAM_EPS = 1e-08
LR_MATRIX = 0.1
LR_NORMS = 0.5
DECAY_MATRIX = 0.1
STEP_NUMBER = 4.0

F32 = jnp.float32
BF16 = jnp.bfloat16


def run(
    kernel, args, in_specs, out_specs, out_shape, grid, name,
    scratch=(), after=(), aliases=None, weight=0, vmem=None,
):
    count, extra = len(args), len(after)

    def body(*refs):
        kernel(*refs[:count], *refs[count + extra :])

    return pl.pallas_call(
        body,
        grid=grid,
        in_specs=list(in_specs) + [pl.BlockSpec(memory_space=pl.ANY)] * extra,
        out_specs=out_specs,
        out_shape=out_shape,
        scratch_shapes=list(scratch),
        input_output_aliases=aliases or {},
        compiler_params=pltpu.CompilerParams(
            vmem_limit_bytes=vmem or VMEM, dimension_semantics=("arbitrary",) * len(grid)
        ),
        cost_estimate=pl.CostEstimate(
            flops=int(weight), bytes_accessed=int(weight), transcendentals=0
        ),
        name=name,
    )(*args, *after)


def dot(a, b):
    return jnp.dot(a, b, preferred_element_type=F32)


def dot_nt(a, b):
    return lax.dot_general(a, b, (((1,), (1,)), ((), ())), preferred_element_type=F32)


def dot_tn(a, b):
    return lax.dot_general(a, b, (((0,), (0,)), ((), ())), preferred_element_type=F32)


def low_lanes(rows):
    return lax.broadcasted_iota(jnp.int32, (rows, 128), 1) < HEAD


def shape(dims, dtype):
    return jax.ShapeDtypeStruct(dims, dtype)


IN_SMEM = pl.BlockSpec(memory_space=pltpu.SMEM)


ANY = pl.BlockSpec(memory_space=pl.ANY)


class Copies:
    def __init__(self, semaphores):
        self.semaphores = semaphores
        self.count = 0

    def start(self, source, target):
        copy = pltpu.make_async_copy(source, target, self.semaphores.at[self.count])
        self.count += 1
        copy.start()
        return copy


def whole(array_shape):
    return pl.BlockSpec(array_shape, lambda *_: (0,) * len(array_shape))


def row_spec(rows, cols, index=lambda i: i):
    return pl.BlockSpec((rows, cols), lambda i: (index(i), 0))


def layer_spec(array, layer):
    rest = array.shape[1:]
    return pl.BlockSpec((None,) + rest, lambda *_: (layer,) + (0,) * len(rest))


def wide_low_lanes(rows):
    return jnp.concatenate([low_lanes(rows)] * 2, axis=1)


def own_lanes(pair, wide_low, odd):
    zero = jnp.zeros_like(pair)
    return jnp.where(wide_low, zero, pair) if odd else jnp.where(wide_low, pair, zero)


def pair_state(features, right):
    both = dot_tn(features, right)
    return jnp.where(wide_low_lanes(128), both[:128], both[128:])


def vext_of(v_pair):
    return jnp.concatenate([v_pair, jnp.ones_like(v_pair)], axis=1)


def tables_kernel(here_ref, cos_ref, sin_ref, live_ref):
    rows = cos_ref.shape[0]
    core, first_len, second_len = lax.axis_index("narrow"), here_ref[0, 0], here_ref[0, 1]
    index = core * rows + lax.broadcasted_iota(jnp.int32, (rows, 128), 0)
    in_first = index < first_len
    in_second = jnp.logical_and(index >= first_len, index < first_len + second_len)
    live = jnp.where(jnp.logical_or(in_first, in_second), 1.0, 0.0)
    position = jnp.where(in_second, index - first_len, index).astype(F32)
    span = jnp.where(in_first, first_len, jnp.where(in_second, second_len, 1)).astype(F32)
    angle = jnp.where(live > 0.0, 0.5 * math.pi * position / span, 0.0)
    square = angle * angle
    cos = sin = jnp.zeros_like(angle)
    for n in range(7, -1, -1):
        cos = cos * square + (-1.0) ** n / math.factorial(2 * n)
        sin = sin * square + (-1.0) ** n / math.factorial(2 * n + 1)
    cos_ref[...] = cos * live
    sin_ref[...] = sin * angle * live
    live_ref[...] = live


def hands_on(lengths_ref, rows, core):
    goes_on = jnp.logical_and(lengths_ref[0, 0] > rows, lax.axis_index("narrow") == core)
    return jnp.where(goes_on, 1.0, 0.0)


def tables(here, rows):
    return run(
        tables_kernel, (here,), [IN_SMEM], [whole((rows, 128))] * 3,
        [shape((rows, 128), F32)] * 3, (1,), "tables",
    )


def project_kernel(x_ref, *refs):
    sides = (len(refs) - 3) // 4
    weights, (cos_ref, sin_ref) = refs[:sides], refs[sides : sides + 2]
    outs, kv_ref = refs[sides + 2 : -1], refs[-1]
    rows = x_ref.shape[0]
    x = x_ref[...]
    low = low_lanes(rows)
    cos, sin = cos_ref[...], sin_ref[...]
    first = pl.program_id(0) == 0

    def features(values, out_ref):
        for pair in range(values.shape[1] // 128):
            tile = jnp.maximum(values[:, pair * 128 : pair * 128 + 128], 0.0)
            along = tile * cos
            across = pltpu.roll(tile, HEAD, 1) * sin
            base = pair * 256
            out_ref[:, base : base + 128] = jnp.where(low, along, across).astype(BF16)
            out_ref[:, base + 128 : base + 256] = jnp.where(low, across, along).astype(BF16)

    for side in range(sides):
        w_ref = weights[side]
        q_ref, k_ref, v_ref = outs[3 * side : 3 * side + 3]
        other = sides - 1 - side
        v = dot(x, w_ref[2]).astype(BF16)
        v_ref[...] = v
        features(dot(x, w_ref[1]), k_ref)
        features(dot(x, w_ref[0]), q_ref)
        for pair in range(v.shape[1] // 128):
            part = pair_state(
                k_ref[:, pair * 256 : pair * 256 + 256],
                vext_of(v[:, pair * 128 : pair * 128 + 128]),
            )
            kv_ref[other, pair] = jnp.where(first, part, kv_ref[other, pair] + part)


def project(x, weights, layer, cos, sin, after=()):
    rows, width = x.shape
    half = weights[0].shape[3]
    heads = half // HEAD
    block = rows // 2
    cat = row_spec(block, heads * 128)
    return run(
        project_kernel,
        (x, *weights, cos, sin),
        [row_spec(block, width)]
        + [layer_spec(w, layer) for w in weights]
        + [row_spec(block, 128)] * 2,
        [cat, cat, row_spec(block, half)] * len(weights)
        + [whole((len(weights), heads // 2, 128, 256))],
        [
            shape((rows, heads * 128), BF16),
            shape((rows, heads * 128), BF16),
            shape((rows, half), BF16),
        ]
        * len(weights)
        + [shape((len(weights), heads // 2, 128, 256), F32)],
        (rows // block,),
        "project",
        (),
        after,
    )


def norm_rows(r, gain, shift):
    mean = jnp.mean(r, axis=1, keepdims=True)
    centered = r - mean
    var = jnp.mean(centered * centered, axis=1, keepdims=True)
    rstd = lax.rsqrt(var + EPS_NORM)
    x_hat = centered * rstd
    return x_hat * gain + shift, x_hat, rstd


def attend_kernel(
    here_ref, qo_ref, qp_ref, ko_ref, kp_ref, vo_ref, vp_ref, kvo_ref, kvp_ref, wo_ref, wp_ref,
    resid_ref, norm_ref,
    mo_ref, mp_ref, rden_ref, low_ref, xhat_ref, rstd_ref, state_out_ref,
    state,
):
    rows = qo_ref.shape[0]
    half = vo_ref.shape[1]
    pairs = half // 128

    @pl.when(pl.program_id(0) == 0)
    def _():
        carry = hands_on(here_ref, rows * pl.num_programs(0), 1)
        state[:pairs] = kvo_ref[...] * carry
        state[pairs:] = kvp_ref[...] * carry

    low = low_lanes(rows)
    row = lax.broadcasted_iota(jnp.int32, (rows, rows), 0)
    col = lax.broadcasted_iota(jnp.int32, (rows, rows), 1)
    causal = col <= row
    branch = None
    for side, (q_ref, k_ref, v_ref, m_ref, w_ref) in enumerate(
        ((qo_ref, ko_ref, vo_ref, mo_ref, wo_ref), (qp_ref, kp_ref, vp_ref, mp_ref, wp_ref))
    ):
        for pair in range(pairs):
            at = side * pairs + pair
            vext = vext_of(v_ref[:, pair * 128 : pair * 128 + 128])
            k_pair = k_ref[:, pair * 256 : pair * 256 + 256]
            q = [q_ref[:, n * 128 : n * 128 + 128] for n in (2 * pair, 2 * pair + 1)]
            kv = state[at]
            kv_low = kv.astype(BF16)
            state_out_ref[0, at] = kv_low
            far = dot(jnp.concatenate(q, axis=0), kv_low)
            sums = []
            for odd in (0, 1):
                scores = dot_nt(q[odd], k_pair[:, odd * 128 : odd * 128 + 128])
                scores = jnp.where(causal, scores, 0.0).astype(BF16)
                sums.append(dot(scores, vext) + far[odd * rows : odd * rows + rows])
            state[at] = kv + pair_state(k_pair, vext)
            num = jnp.where(low, sums[0][:, :128], sums[1][:, :128])
            den = jnp.where(low, sums[0][:, 128:], sums[1][:, 128:])
            rden = 1.0 / jnp.maximum(den, 1.0)
            base = side * half + pair * 128
            rden_low = jnp.where(den > 1.0, jnp.minimum(rden, 1.0 - 2.0**-8), 1.0)
            rden_ref[:, base : base + 128] = rden_low.astype(BF16)
            m_ref[:, pair * 128 : pair * 128 + 128] = (num * rden).astype(BF16)
        part = dot(m_ref[...], w_ref[...])
        branch = part if branch is None else branch + part
    y, x_hat, rstd = norm_rows(resid_ref[...].astype(F32) + branch, norm_ref[0:1], norm_ref[1:2])
    low_ref[...] = y.astype(BF16)
    xhat_ref[...] = x_hat.astype(BF16)
    rstd_ref[...] = jnp.broadcast_to(rstd, rstd_ref.shape)


def attend(here, own, peer, kv, kv_at, w_own, w_peer, layer, resid, norms, after=()):
    rows, width = resid.shape
    half = own[2].shape[1]
    heads = half // HEAD
    steps = rows // CHUNK
    cat, narrow = row_spec(CHUNK, heads * 128), row_spec(CHUNK, half)
    full = row_spec(CHUNK, width)
    return run(
        attend_kernel,
        (here, own[0], peer[0], own[1], peer[1], own[2], peer[2], *kv,
         w_own, w_peer, resid, norms),
        [
            IN_SMEM,
            cat, cat, cat, cat, narrow, narrow,
            *(pl.BlockSpec((None,) + a.shape[1:], lambda *_, n=n: (n, 0, 0, 0)) for a, n in zip(kv, kv_at)),
            layer_spec(w_own, layer), layer_spec(w_peer, layer),
            full, layer_spec(norms, layer),
        ],
        [
            narrow, narrow, full, full, full, row_spec(CHUNK, 128),
            pl.BlockSpec((1, heads, 128, 256), lambda i: (i, 0, 0, 0)),
        ],
        [
            shape((rows, half), BF16),
            shape((rows, half), BF16),
            shape((rows, width), BF16),
            shape((rows, width), BF16),
            shape((rows, width), BF16),
            shape((rows, 128), F32),
            shape((steps, heads, 128, 256), BF16),
        ],
        (steps,),
        "attend",
        [pltpu.VMEM((heads, 128, 256), F32)],
        after,
    )


def gelu_both(u):
    root = math.sqrt(2.0 / math.pi)
    a = root + (root * 0.044715) * (u * u)
    gate = 0.5 + 0.5 * jnp.tanh(u * a)
    act = u * gate
    return act, gate + (act - act * gate) * (6.0 * a - 4.0 * root)


def feed_kernel(
    layer,
    x_ref, wio_ref, wip_ref, wbo_ref, wbp_ref, norm_ref,
    ho_ref, hp_ref, slope_ref, out_ref, xhat_ref, rstd_ref,
    x, w_in, w_back, h, slope, acc, out, xhat, rstd, semaphores,
):
    rows = x.shape[0]
    blocks = w_in.shape[0] // 2
    width = FF_BLOCK
    copies = Copies(semaphores)
    waits = [copies.start(x_ref, x)]
    for n in range(2 * blocks):
        wi, wb = (wio_ref, wbo_ref) if n < blocks else (wip_ref, wbp_ref)
        at = pl.ds(n % blocks * width, width)
        waits.append(copies.start(wi.at[layer, :, at], w_in.at[n]))
        waits.append(copies.start(wb.at[layer, at, :], w_back.at[n]))
    waits.pop(0).wait()
    outgoing = []
    for n in range(2 * blocks):
        waits.pop(0).wait()
        waits.pop(0).wait()
        for i in range(rows // FF_CHUNK):
            at = slice(i * FF_CHUNK, i * FF_CHUNK + FF_CHUNK)
            act, deriv = gelu_both(dot(x[at, :], w_in[n]))
            act = act.astype(BF16)
            h[n, at, :] = act
            slope[n, at, :] = deriv.astype(BF16)
            base = x[at, :].astype(F32) if n == 0 else acc[at, :]
            total = base + dot(act, w_back[n])
            if n < 2 * blocks - 1:
                acc[at, :] = total
                continue
            y, x_hat, inverse = norm_rows(total, norm_ref[2:3], norm_ref[3:4])
            out[at, :] = y.astype(out.dtype)
            xhat[at, :] = x_hat.astype(BF16)
            rstd[at, :] = jnp.broadcast_to(inverse, (FF_CHUNK, 128))
            here = pl.ds(i * FF_CHUNK, FF_CHUNK)
            for source, target in ((out, out_ref), (xhat, xhat_ref), (rstd, rstd_ref)):
                outgoing.append(copies.start(source.at[here, :], target.at[here, :]))
        part = pl.ds(n % blocks * width, width)
        target = ho_ref if n < blocks else hp_ref
        outgoing.append(copies.start(h.at[n], target.at[:, part]))
        outgoing.append(copies.start(slope.at[n], slope_ref.at[:, pl.ds(n * width, width)]))
    for copy in outgoing:
        copy.wait()


def feed(x, wi_own, wi_peer, wb_own, wb_peer, layer, norms, dtype, after=()):
    rows, width = x.shape
    half = wi_own.shape[2]
    blocks = half // FF_BLOCK
    copies = 1 + 8 * blocks + 3 * (rows // FF_CHUNK)
    return run(
        functools.partial(feed_kernel, layer),
        (x, wi_own, wi_peer, wb_own, wb_peer, norms),
        [ANY] * 5 + [layer_spec(norms, layer)],
        [ANY] * 6,
        [
            shape((rows, half), BF16),
            shape((rows, half), BF16),
            shape((rows, 2 * half), BF16),
            shape((rows, width), dtype),
            shape((rows, width), BF16),
            shape((rows, 128), F32),
        ],
        (1,),
        "feed",
        [
            pltpu.VMEM((rows, width), BF16),
            pltpu.VMEM((2 * blocks, width, FF_BLOCK), BF16),
            pltpu.VMEM((2 * blocks, FF_BLOCK, width), BF16),
            pltpu.VMEM((2 * blocks, rows, FF_BLOCK), BF16),
            pltpu.VMEM((2 * blocks, rows, FF_BLOCK), BF16),
            pltpu.VMEM((rows, width), F32),
            pltpu.VMEM((rows, width), dtype),
            pltpu.VMEM((rows, width), BF16),
            pltpu.VMEM((rows, 128), F32),
            pltpu.SemaphoreType.DMA((copies,)),
        ],
        after,
    )


def feed_grid_kernel(
    x_ref, wio_ref, wip_ref, wbo_ref, wbp_ref, norm_ref,
    ho_ref, hp_ref, slope_ref, out_ref, xhat_ref, rstd_ref,
    acc,
):
    step, steps = pl.program_id(0), pl.num_programs(0)
    rows = x_ref.shape[0]

    def side(w_in, w_back, h_ref, base):
        for i in range(rows // CHUNK):
            at = slice(i * CHUNK, i * CHUNK + CHUNK)
            act, slope = gelu_both(dot(x_ref[at, :], w_in[...]))
            act = act.astype(BF16)
            h_ref[at, :] = act
            slope_ref[at, :] = slope.astype(BF16)
            acc[at, :] = base[at, :].astype(F32) + dot(act, w_back[...])

    @pl.when(step == 0)
    def _():
        side(wio_ref, wbo_ref, ho_ref, x_ref)

    @pl.when((step > 0) & (step < steps // 2))
    def _():
        side(wio_ref, wbo_ref, ho_ref, acc)

    @pl.when(step >= steps // 2)
    def _():
        side(wip_ref, wbp_ref, hp_ref, acc)

    @pl.when(step == steps - 1)
    def _():
        def part(i, _):
            at = pl.ds(pl.multiple_of(i * CHUNK, CHUNK), CHUNK)
            y, x_hat, rstd = norm_rows(acc[at, :], norm_ref[2:3], norm_ref[3:4])
            out_ref[at, :] = y.astype(out_ref.dtype)
            xhat_ref[at, :] = x_hat.astype(BF16)
            rstd_ref[at, :] = jnp.broadcast_to(rstd, (CHUNK, 128))
            return 0

        lax.fori_loop(0, rows // CHUNK, part, 0)


def ff_specs(layer, width, blocks):
    own = lambda j: jnp.minimum(j, blocks - 1)
    peer = lambda j: jnp.maximum(j - blocks, 0)
    w_in = [
        pl.BlockSpec((None, width, FF_BLOCK), lambda j, f=f: (layer, 0, f(j))) for f in (own, peer)
    ]
    w_back = [
        pl.BlockSpec((None, FF_BLOCK, width), lambda j, f=f: (layer, f(j), 0)) for f in (own, peer)
    ]
    return own, peer, w_in, w_back


def feed_grid(x, wi_own, wi_peer, wb_own, wb_peer, layer, norms, dtype, after=()):
    rows, width = x.shape
    half = wi_own.shape[2]
    blocks = half // FF_BLOCK
    own, peer, w_in, w_back = ff_specs(layer, width, blocks)
    full = whole((rows, width))
    return run(
        feed_grid_kernel,
        (x, wi_own, wi_peer, wb_own, wb_peer, norms),
        [full, *w_in, *w_back, layer_spec(norms, layer)],
        [
            pl.BlockSpec((rows, FF_BLOCK), lambda j: (0, own(j))),
            pl.BlockSpec((rows, FF_BLOCK), lambda j: (0, peer(j))),
            pl.BlockSpec((rows, FF_BLOCK), lambda j: (0, j)),
            full, full, whole((rows, 128)),
        ],
        [
            shape((rows, half), BF16),
            shape((rows, half), BF16),
            shape((rows, 2 * half), BF16),
            shape((rows, width), dtype),
            shape((rows, width), BF16),
            shape((rows, 128), F32),
        ],
        (2 * blocks,),
        "feed",
        [pltpu.VMEM((rows, width), F32)],
        after,
    )


def norm_back(y, x_hat, rstd, gain):
    scaled = y * gain
    mean = jnp.mean(scaled, axis=1, keepdims=True)
    along = jnp.mean(scaled * x_hat, axis=1, keepdims=True)
    gain_grad = jnp.sum(y * x_hat, axis=0, keepdims=True)
    shift_grad = jnp.sum(y, axis=0, keepdims=True)
    return (scaled - mean - x_hat * along) * rstd, gain_grad, shift_grad


def feed_back_kernel(
    layer, masked, *refs,
):
    count = 12 if masked else 11
    up_ref, *refs_in = refs[:count]
    live_ref = refs_in.pop(0) if masked else None
    xh2_ref, rs2_ref, xh1_ref, rs1_ref, slope_ref, wio_ref, wip_ref, wbo_ref, wbp_ref, norm_ref = refs_in
    gfb_ref, gho_ref, ghp_ref, ng_ref = refs[count : count + 4]
    up, live, xh2, rs2, xh1, rs1, slope, w_in, w_back, gfb, gh, acc, semaphores = refs[count + 4 :]
    rows, width = up.shape
    blocks = w_in.shape[0] // 2
    copies = Copies(semaphores)
    chunks = [pl.ds(i * FF_CHUNK, FF_CHUNK) for i in range(rows // FF_CHUNK)]

    def wide(value):
        return jnp.concatenate([value] * (width // 128), axis=1)

    first = []
    for at in chunks:
        pairs = [(up_ref, up), (xh2_ref, xh2), (rs2_ref, rs2)]
        if masked:
            pairs.append((live_ref, live))
        first.append([copies.start(source.at[at, :], target.at[at, :]) for source, target in pairs])
    waits = []
    for n in range(2 * blocks):
        wi, wb = (wio_ref, wbo_ref) if n < blocks else (wip_ref, wbp_ref)
        at = pl.ds(n % blocks * FF_BLOCK, FF_BLOCK)
        waits.append(copies.start(wb.at[layer, at, :], w_back.at[n]))
        waits.append(copies.start(slope_ref.at[:, pl.ds(n * FF_BLOCK, FF_BLOCK)], slope.at[n]))
        waits.append(copies.start(wi.at[layer, :, at], w_in.at[n]))
    late = [copies.start(xh1_ref, xh1), copies.start(rs1_ref, rs1)]
    sums = [None] * 4

    def add(kind, value):
        sums[kind] = value if sums[kind] is None else sums[kind] + value

    outgoing = []
    for at, arrivals in zip(chunks, first):
        for copy in arrivals:
            copy.wait()
        y = up[at, :].astype(F32)
        if masked:
            y = y * wide(live[at, :])
        grad, gain_grad, shift_grad = norm_back(
            y, xh2[at, :].astype(F32), wide(rs2[at, :]), norm_ref[2:3]
        )
        acc[at, :] = grad
        gfb[0, at, :] = grad.astype(BF16)
        add(2, gain_grad)
        add(3, shift_grad)
    outgoing.append(copies.start(gfb.at[0], gfb_ref.at[0]))
    for n in range(2 * blocks):
        for _ in range(3):
            waits.pop(0).wait()
        if n == 2 * blocks - 1:
            for copy in late:
                copy.wait()
        for at in chunks:
            act = dot_nt(gfb[0, at, :], w_back[n])
            gh_part = (act * slope[n, at, :].astype(F32)).astype(BF16)
            gh[n, at, :] = gh_part
            total = acc[at, :] + dot_nt(gh_part, w_in[n])
            if n < 2 * blocks - 1:
                acc[at, :] = total
                continue
            grad, gain_grad, shift_grad = norm_back(
                total, xh1[at, :].astype(F32), wide(rs1[at, :]), norm_ref[0:1]
            )
            gfb[1, at, :] = grad.astype(BF16)
            outgoing.append(copies.start(gfb.at[1, at, :], gfb_ref.at[1, at, :]))
            add(0, gain_grad)
            add(1, shift_grad)
        target = gho_ref if n < blocks else ghp_ref
        part = pl.ds(n % blocks * FF_BLOCK, FF_BLOCK)
        outgoing.append(copies.start(gh.at[n], target.at[:, part]))
    ng_ref[...] = jnp.concatenate(sums, axis=0)
    for copy in outgoing:
        copy.wait()


def feed_back(
    up, live, xh2, rs2, xh1, rs1, slope, wi_own, wi_peer, wb_own, wb_peer, layer, norms, after=()
):
    rows, width = up.shape
    half = wi_own.shape[2]
    blocks = half // FF_BLOCK
    chunks = rows // FF_CHUNK
    masked = live is not None
    args = (up,) + ((live,) if masked else ())
    args += (xh2, rs2, xh1, rs1, slope, wi_own, wi_peer, wb_own, wb_peer, norms)
    thin = pltpu.VMEM((rows, 128), F32)
    full = pltpu.VMEM((rows, width), BF16)
    return run(
        functools.partial(feed_back_kernel, layer, masked),
        args,
        [ANY] * (len(args) - 1) + [layer_spec(norms, layer)],
        [ANY] * 3 + [whole((4, width))],
        [
            shape((2, rows, width), BF16),
            shape((rows, half), BF16),
            shape((rows, half), BF16),
            shape((4, width), F32),
        ],
        (1,),
        "feed_back",
        [
            pltpu.VMEM((rows, width), up.dtype), thin if masked else pltpu.VMEM((8, 128), F32),
            full, thin, full, thin,
            pltpu.VMEM((2 * blocks, rows, FF_BLOCK), BF16),
            pltpu.VMEM((2 * blocks, width, FF_BLOCK), BF16),
            pltpu.VMEM((2 * blocks, FF_BLOCK, width), BF16),
            pltpu.VMEM((2, rows, width), BF16),
            pltpu.VMEM((2 * blocks, rows, FF_BLOCK), BF16),
            pltpu.VMEM((rows, width), F32),
            pltpu.SemaphoreType.DMA((5 * chunks + 8 * blocks + 3,)),
        ],
        after,
    )


def mix_back_kernel(
    layer,
    gfb_ref, wo_ref, wp_ref, rden_ref, mo_ref, mp_ref, qo_ref, qp_ref,
    gx_ref, dkv_ref,
    gb, w, rden, m, q, gx_out, semaphores,
):
    rows = MIX_CHUNK
    total_rows, half = m.shape[1:]
    pairs = half // 128
    copies = Copies(semaphores)
    arrivals, leaving = [], []
    for n in range(total_rows // rows):
        at = pl.ds(n * rows, rows)
        part = [copies.start(gfb_ref.at[1, at, :], gb.at[at, :])]
        if n == 0:
            part += [copies.start(ref.at[layer], w.at[n]) for n, ref in enumerate((wo_ref, wp_ref))]
        part.append(copies.start(rden_ref.at[at, :], rden.at[at, :]))
        for side, (m_in, q_in) in enumerate(((mo_ref, qo_ref), (mp_ref, qp_ref))):
            part.append(copies.start(m_in.at[at, :], m.at[side, at, :]))
            part.append(copies.start(q_in.at[at, :], q.at[side, at, :]))
        arrivals.append(part)
    r = lax.broadcasted_iota(jnp.int32, (256, 128), 0) % 128
    c = lax.broadcasted_iota(jnp.int32, (256, 128), 1)
    spread_c = jnp.where((r < HEAD) == (c < HEAD), -1.0 / HEAD, 0.0).astype(BF16)
    totals = [None] * (2 * pairs)
    for n in range(total_rows // rows):
        at = slice(n * rows, n * rows + rows)
        for copy in arrivals[n]:
            copy.wait()
        for side in range(2):
            gm = dot_nt(gb[at, :], w[side])
            for pair in range(pairs):
                base = side * half + pair * 128
                inverse = rden[at, base : base + 128].astype(F32)
                g = gm[:, pair * 128 : pair * 128 + 128] * inverse
                mixed = m[side, at, pair * 128 : pair * 128 + 128].astype(F32)
                prod = jnp.where(inverse < 1.0, g * mixed, 0.0)
                high = prod.astype(BF16)
                rest = (prod - high.astype(F32)).astype(BF16)
                minus_c = dot(jnp.concatenate([high, rest], axis=1), spread_c).astype(BF16)
                gx = jnp.concatenate([g.astype(BF16), minus_c], axis=1)
                gx_out[at, 2 * base : 2 * base + 256] = gx
        here = pl.ds(n * rows, rows)
        leaving.append(copies.start(gx_out.at[here, :], gx_ref.at[here, :]))
    for side in range(2):
        for pair in range(pairs):
            wide = 2 * (side * half + pair * 128)
            state = pair_state(
                q[side, :, pair * 256 : pair * 256 + 256], gx_out[:, wide : wide + 256]
            )
            dkv_ref[side * pairs + pair] = state.astype(BF16)
    for copy in leaving:
        copy.wait()


def mix_back(gfb, w_own, w_peer, layer, rden, m_own, m_peer, q_own, q_peer, after=()):
    _, rows, width = gfb.shape
    half = m_own.shape[1]
    heads = half // HEAD
    steps = rows // MIX_CHUNK
    return run(
        functools.partial(mix_back_kernel, layer),
        (gfb, w_own, w_peer, rden, m_own, m_peer, q_own, q_peer),
        [ANY] * 8,
        [ANY, whole((heads, 128, 256))],
        [
            shape((rows, 2 * width), BF16),
            shape((heads, 128, 256), BF16),
        ],
        (1,),
        "mix_back",
        [
            pltpu.VMEM((rows, width), BF16),
            pltpu.VMEM((2, half, width), BF16),
            pltpu.VMEM((rows, width), BF16),
            pltpu.VMEM((2, rows, half), BF16),
            pltpu.VMEM((2, rows, heads * 128), BF16),
            pltpu.VMEM((rows, 2 * width), BF16),
            pltpu.SemaphoreType.DMA((7 * steps + 2,)),
        ],
        after,
    )


def attend_back_kernel(
    here_ref, qo_ref, qp_ref, ko_ref, kp_ref, vo_ref, vp_ref, gx_ref, state_ref, dkv_ref,
    cos_ref, sin_ref,
    go_ref, gpq_ref, gpk_ref, gpv_ref,
    dstate,
):
    rows = qo_ref.shape[0]
    half = vo_ref.shape[1]
    pairs = half // 128

    @pl.when(pl.program_id(0) == 0)
    def _():
        carry = hands_on(here_ref, rows * pl.num_programs(0), 0)
        for at in range(2 * pairs):
            dstate[at] = dkv_ref[(at + pairs) % (2 * pairs)].astype(F32) * carry

    low = low_lanes(rows)
    wide_low, state_low = wide_low_lanes(rows), wide_low_lanes(128)
    row = lax.broadcasted_iota(jnp.int32, (rows, rows), 0)
    col = lax.broadcasted_iota(jnp.int32, (rows, rows), 1)
    causal, anti = col <= row, row <= col
    cos, sin = cos_ref[...], sin_ref[...]
    trig = jnp.where(low, cos, sin), jnp.where(low, sin, cos)
    for side, (q_ref, k_ref, v_ref) in enumerate(
        ((qo_ref, ko_ref, vo_ref), (qp_ref, kp_ref, vp_ref))
    ):
        for pair in range(pairs):
            at = side * pairs + pair
            vext = vext_of(v_ref[:, pair * 128 : pair * 128 + 128])
            gx = gx_ref[:, at * 256 : at * 256 + 256]
            gext = [own_lanes(gx, wide_low, odd) for odd in (0, 1)]
            both = jnp.concatenate(gext, axis=0)
            ds_both = dot_nt(both, vext)
            q_far = dot_nt(both, state_ref[0, at])
            dst_both = dot_nt(vext, both)
            left_over = dstate[at].astype(BF16)
            back = [own_lanes(left_over, state_low, odd) for odd in (0, 1)]
            k_far = dot_nt(vext, jnp.concatenate(back, axis=0))
            dstate[at] += pair_state(q_ref[:, pair * 256 : pair * 256 + 256], gx)
            dq, dk, left, right = [], [], [], []
            for odd in (0, 1):
                head = 2 * pair + odd
                here = slice(odd * rows, odd * rows + rows)
                q = q_ref[:, head * 128 : head * 128 + 128]
                k = k_ref[:, head * 128 : head * 128 + 128]
                score_t = jnp.where(anti, dot_nt(k, q), 0.0).astype(BF16)
                ds = jnp.where(causal, ds_both[here], 0.0).astype(BF16)
                ds_t = jnp.where(anti, dst_both[:, here], 0.0).astype(BF16)
                q_grad = (dot(ds, k) + q_far[here]) * trig[odd]
                k_grad = (dot(ds_t, q) + k_far[:, odd * 128 : odd * 128 + 128]) * trig[odd]
                left += [score_t, k]
                right += [gext[odd][:, :128], back[odd][:, :128]]
                q_grad = q_grad + pltpu.roll(q_grad, HEAD, 1)
                k_grad = k_grad + pltpu.roll(k_grad, HEAD, 1)
                dq.append(jnp.where(q > 0, q_grad, 0.0))
                dk.append(jnp.where(k > 0, k_grad, 0.0))
            dv = dot(jnp.concatenate(left, axis=1), jnp.concatenate(right, axis=0))
            for kind, value in enumerate(
                (jnp.where(low, dq[0], dq[1]), jnp.where(low, dk[0], dk[1]), dv)
            ):
                if side == 0:
                    base = kind * half + pair * 128
                    go_ref[:, base : base + 128] = value.astype(BF16)
                else:
                    out_ref = (gpq_ref, gpk_ref, gpv_ref)[kind]
                    out_ref[:, pair * 128 : pair * 128 + 128] = value.astype(BF16)


def attend_back_on_kernel(layer, *refs):
    inputs, (wo_ref, wp_ref, gfb_ref), (go_ref, *gp_refs, up_ref), scratch = (
        refs[:12], refs[12:15], refs[15:20], refs[20:],
    )
    dstate, g, w, gb, up, semaphores = scratch
    step, steps = pl.program_id(0), pl.num_programs(0)
    rows, third = go_ref.shape[0], wo_ref.shape[3]
    total = gb.shape[0]
    pieces = [
        (ref.at[layer, kind], w.at[side, :, pl.ds(kind * third, third)])
        for side, ref in enumerate((wo_ref, wp_ref))
        for kind in range(3)
    ] + [(gfb_ref.at[1], gb)]
    copies = [pltpu.make_async_copy(*piece, semaphores.at[n]) for n, piece in enumerate(pieces)]

    @pl.when(step == 0)
    def _():
        for copy in copies:
            copy.start()

    attend_back_kernel(*inputs, go_ref, *gp_refs, dstate)
    at = pl.ds(pl.multiple_of((steps - 1 - step) * rows, rows), rows)
    g[0, at, :] = go_ref[...]
    for kind, gp_ref in enumerate(gp_refs):
        g[1, at, kind * third : kind * third + third] = gp_ref[...]

    @pl.when(step == steps - 1)
    def _():
        for copy in copies:
            copy.wait()
        leaving = []
        for n in range(2):
            part = slice(n * total // 2, (n + 1) * total // 2)
            value = gb[part, :].astype(F32)
            value = value + dot_nt(g[0, part, :], w[0]) + dot_nt(g[1, part, :], w[1])
            up[part, :] = value.astype(BF16)
            here = pl.ds(n * total // 2, total // 2)
            copy = pltpu.make_async_copy(up.at[here, :], up_ref.at[here, :], semaphores.at[7 + n])
            copy.start()
            leaving.append(copy)
        for copy in leaving:
            copy.wait()


def attend_back(here, own, peer, gx, states, dkv, cos, sin, after=(), onward=None):
    rows = cos.shape[0]
    half = own[2].shape[1]
    heads = half // HEAD
    steps = rows // CHUNK
    back = lambda i: steps - 1 - i
    cat, narrow, trig = (row_spec(CHUNK, n, back) for n in (heads * 128, half, 128))
    args = (here, own[0], peer[0], own[1], peer[1], own[2], peer[2], gx, states, dkv, cos, sin)
    specs = [
        IN_SMEM,
        cat, cat, cat, cat, narrow, narrow,
        row_spec(CHUNK, heads * 256, back),
        pl.BlockSpec((1, heads, 128, 256), lambda i: (back(i), 0, 0, 0)),
        whole(dkv.shape), trig, trig,
    ]
    outs = [row_spec(CHUNK, 3 * half, back)] + [row_spec(CHUNK, half, back)] * 3
    shapes = [shape((rows, 3 * half), BF16)] + [shape((rows, half), BF16)] * 3
    kernel = attend_back_kernel
    scratch = [pltpu.VMEM((heads, 128, 256), F32)]
    if onward is not None:
        w_own, w_peer, layer, gfb = onward
        kernel = functools.partial(attend_back_on_kernel, layer)
        width = gfb.shape[2]
        args += (w_own, w_peer, gfb)
        specs += [ANY] * 3
        outs, shapes = outs + [ANY], shapes + [shape((rows, width), BF16)]
        scratch += [
            pltpu.VMEM((2, rows, 3 * half), BF16),
            pltpu.VMEM((2, width, 3 * half), BF16),
            pltpu.VMEM((rows, width), BF16),
            pltpu.VMEM((rows, width), BF16),
            pltpu.SemaphoreType.DMA((9,)),
        ]
    return run(
        kernel, args, specs, outs, shapes, (steps,), "attend_back", scratch, after,
    )


def input_back_kernel(go_ref, gpq_ref, gpk_ref, gpv_ref, wo_ref, wp_ref, first_ref, out_ref):
    half = wo_ref.shape[2]
    total = first_ref[...].astype(F32)
    for kind, gp_ref in enumerate((gpq_ref, gpk_ref, gpv_ref)):
        total = total + dot_nt(go_ref[:, kind * half : kind * half + half], wo_ref[kind])
        total = total + dot_nt(gp_ref[...], wp_ref[kind])
    out_ref[...] = total.astype(out_ref.dtype)


def input_back(g_own, g_peer, w_own, w_peer, layer, gfb, after=()):
    _, rows, width = gfb.shape
    block = rows // 2
    third, full = row_spec(block, g_own.shape[1] // 3), row_spec(block, width)
    return run(
        input_back_kernel,
        (g_own, *g_peer, w_own, w_peer, gfb),
        [
            row_spec(block, g_own.shape[1]), third, third, third, layer_spec(w_own, layer), layer_spec(w_peer, layer),
            pl.BlockSpec((None, block, width), lambda i: (1, i, 0)),
        ],
        full,
        shape((rows, width), F32),
        (rows // block,),
        "input_back",
        (),
        after,
    )


def weight_kernel(a_ref, b_ref, c_ref, d_ref, out_ref):
    out_ref[...] = (dot_tn(a_ref[...], b_ref[...]) + dot_tn(c_ref[...], d_ref[...])).astype(
        out_ref.dtype
    )


def weight_grad(a, b, c, d, block_m, block_n, name):
    rows, m = a.shape
    n = b.shape[1]
    left = pl.BlockSpec((rows, block_m), lambda i, j: (0, i))
    right = pl.BlockSpec((rows, block_n), lambda i, j: (0, j))
    return run(
        weight_kernel,
        (a, b, c, d),
        [left, right, left, right],
        pl.BlockSpec((block_m, block_n), lambda i, j: (i, j)),
        shape((m, n), BF16),
        (m // block_m, n // block_n),
        name,
    )


FF_ROWS = 448
NORM_ROW = 408


def fold_lanes(values, width):
    pieces = [values[:, at : at + width] for at in range(0, values.shape[1], width)]
    return jnp.concatenate(pieces, axis=0) if len(pieces) > 1 else values


def blocks_of(scr, rows, z_local, x_first, other, kept):
    x, y = lax.axis_index("x"), lax.axis_index("y")
    if x_first:
        spot = other * 2 + (x if kept else 1 - x)
    else:
        spot = (y if kept else 1 - y) * 2 + other
    start = pl.multiple_of((z_local * 4 + spot) * rows, 8)
    return scr[pl.ds(start, rows), :]


def spread(scr, rows, outs):
    ka, sa, kb, sb = outs
    for x_first, keep, send in ((True, ka, sa), (False, kb, sb)):
        for z in range(2):
            z_local = z if x_first else z + 2
            for other in range(2):
                for kept, out in ((True, keep), (False, send)):
                    value = blocks_of(scr, rows, z_local, x_first, other, kept)
                    out[z, other] = value.astype(BF16)


def q_pack_kernel(
    a_ref, b_ref, c_ref, d0_ref, d1_ref, d2_ref,
    ka_ref, sa_ref, kb_ref, sb_ref,
    left, right, out, scr, semaphores,
):
    parts, _, lanes = right.shape
    rows, m = a_ref.shape
    block = m // 16
    outs = (ka_ref, sa_ref, kb_ref, sb_ref)
    copies = Copies(semaphores)
    first = [
        copies.start(ref, left.at[pl.ds(side * rows, rows), :])
        for side, ref in enumerate((a_ref, c_ref))
    ]
    arrivals = [
        [
            copies.start(b_ref.at[:, pl.ds(n * lanes, lanes)], right.at[n, pl.ds(0, rows), :]),
            copies.start(d_ref, right.at[n, pl.ds(rows, rows), :]),
        ]
        for n, d_ref in enumerate((d0_ref, d1_ref, d2_ref))
    ]
    leaving = []
    for n in range(parts):
        for copy in (first if n == 0 else []) + arrivals[n]:
            copy.wait()
        scr[n % 2] = dot_tn(left[...], right[n])
        here = slice(n * block, n * block + block)
        spread(scr.at[n % 2], block, [out.at[which, :, :, here, :] for which in range(4)])
        for which in range(4):
            at = pl.ds(n * block, block)
            leaving.append(copies.start(out.at[which, :, :, at, :], outs[which].at[:, :, at, :]))
    for copy in leaving:
        copy.wait()


def q_pack(a, b, c, d, lanes, after=()):
    rows, m = a.shape
    parts = b.shape[1] // lanes
    buffer = (2, 2, m // 16 * parts, lanes)
    return run(
        q_pack_kernel,
        (a, b, c, *d),
        [ANY] * 6,
        [ANY] * 4,
        [shape(buffer, BF16)] * 4,
        (1,),
        "qkv_grad",
        [
            pltpu.VMEM((2 * rows, m), BF16),
            pltpu.VMEM((parts, 2 * rows, lanes), BF16),
            pltpu.VMEM((4,) + buffer, BF16),
            pltpu.VMEM((2, m, lanes), F32),
            pltpu.SemaphoreType.DMA((2 + 6 * parts,)),
        ],
        after,
    )


def pack_kernel(
    index_ref, ho_ref, gfb_ref, hg_ref, gfbg_ref, fi_ref, gho_ref, fg_ref, ghg_ref, mo_ref, mg_ref,
    norm_ref, norm_got_ref,
    ka_ref, sa_ref, kb_ref, sb_ref,
    h, gfb, f, gh, m, out, scr, semaphores,
):
    x, y = lax.axis_index("x"), lax.axis_index("y")
    outs = (ka_ref, sa_ref, kb_ref, sb_ref)
    lanes = out.shape[4]
    block = h.shape[2]
    columns = gh.shape[2]
    copies = Copies(semaphores)
    start = copies.start

    def both(sources, target, *at):
        rows = sources[0].shape[0]
        return [
            start(source, target.at[(*at, pl.ds(side * rows, rows))])
            for side, source in enumerate(sources)
        ]

    back_first = both((gfb_ref.at[0], gfbg_ref.at[0]), gfb, 0)
    back_parts = [
        both((ho_ref.at[:, pl.ds(n * block, block)], hg_ref.at[:, pl.ds(n * block, block)]), h, n)
        for n in range(4)
    ]
    in_first = both((fi_ref, fg_ref), f)
    in_parts = [
        both((gho_ref.at[:, pl.ds(n * columns, columns)], ghg_ref.at[:, pl.ds(n * columns, columns)]), gh, n)
        for n in range(2)
    ]
    out_parts = both((mo_ref, mg_ref), m) + both((gfb_ref.at[1], gfbg_ref.at[1]), gfb, 1)
    outgoing = []

    def wait(parts):
        for copy in parts:
            copy.wait()

    def place(slot, base, z, rows, at, tail=None):
        x_first = z < 2
        for other in range(2):
            for kept in (True, False):
                if x_first:
                    spot = other * 2 + (x if kept else 1 - x)
                else:
                    spot = (y if kept else 1 - y) * 2 + other
                value = scr[slot, pl.ds(pl.multiple_of(base + spot * rows, 8), rows), :]
                if tail is not None:
                    value = jnp.concatenate([value, tail(z * 4 + spot)], axis=0)
                value = fold_lanes(value, lanes).astype(BF16)
                which = (0 if x_first else 2) + (0 if kept else 1)
                out[which, z % 2, other, at : at + value.shape[0], :] = value

    wait(back_first)
    for z in range(4):
        wait(back_parts[z])
        scr[z % 2, :block, :] = dot_tn(h[z], gfb[0])
        place(z % 2, 0, z, block // 4, 0)
        for which in (0, 1) if z < 2 else (2, 3):
            rows = pl.ds(0, block // 2)
            outgoing.append(
                start(out.at[which, z % 2, :, rows, :], outs[which].at[z % 2, :, rows, :])
            )
    wait(in_first)
    at = block // 2
    for n in range(2):
        wait(in_parts[n])
        scr[n] = dot_tn(f[...], gh[n])
        rows = scr.shape[1] // 16
        for z in range(4):
            place(n, z * 4 * rows, z, rows, at)
        here = pl.ds(at, 2 * rows)
        at += 2 * rows
        for which in range(4):
            outgoing.append(start(out.at[which, :, :, here, :], outs[which].at[:, :, here, :]))
    wait(out_parts)
    scr[0, :block, :] = dot_tn(m[...], gfb[1])
    blank = jnp.zeros((8, scr.shape[2] - 128), F32)
    tail = lambda w: jnp.concatenate([norm_ref[w] + norm_got_ref[w], blank], axis=1)
    for z in range(4):
        place(0, z * (block // 4), z, block // 16, at, tail)
    here = pl.ds(at, 2 * (block // 16 + 8))
    for which in range(4):
        outgoing.append(start(out.at[which, :, :, here, :], outs[which].at[:, :, here, :]))
    for copy in outgoing:
        copy.wait()


def pack(index, h_own, gfb, h_got, gfb_got, ffn_in, gh_own, ffn_got, gh_got, m_own, m_got, norms, norms_got, after=()):
    rows, hidden = h_own.shape
    width = ffn_in.shape[1]
    half = m_own.shape[1]
    return run(
        pack_kernel,
        (index, h_own, gfb, h_got, gfb_got, ffn_in, gh_own, ffn_got, gh_got, m_own, m_got, norms, norms_got),
        [IN_SMEM] + [ANY] * 10 + [whole(norms.shape)] * 2,
        [ANY] * 4,
        [shape((2, 2, FF_ROWS, half), BF16)] * 4,
        (1,),
        "pack",
        [
            pltpu.VMEM((4, 2 * rows, hidden // 4), BF16),
            pltpu.VMEM((2, 2 * rows, width), BF16),
            pltpu.VMEM((2 * rows, width), BF16),
            pltpu.VMEM((2, 2 * rows, hidden // 2), BF16),
            pltpu.VMEM((2 * rows, half), BF16),
            pltpu.VMEM((4, 2, 2, FF_ROWS, half), BF16),
            pltpu.VMEM((2, width, width), F32),
            pltpu.SemaphoreType.DMA((40,)),
        ],
        after,
    )


def swap(values, axis="narrow"):
    return lax.ppermute(values, axis, [(0, 1), (1, 0)])


def sum_of(a_ref, b_ref, *at):
    return (a_ref[at].astype(F32) + b_ref[at].astype(F32)).astype(BF16)


def fold_split_kernel(ka, ga, kb, gb, sa_ref, sb_ref, held, out, semaphores):
    other = 1 - lax.axis_index("y"), 1 - lax.axis_index("x")
    copies = Copies(semaphores)
    arrivals = {}
    for z in range(2):
        for which, (k, g) in enumerate(((ka, ga), (kb, gb))):
            arrivals[which, z] = [
                copies.start(ref.at[z, other[which]], held.at[which, n, z])
                for n, ref in enumerate((k, g))
            ]
    leaving = []
    for (which, z), pair in arrivals.items():
        for copy in pair:
            copy.wait()
        out[which, z] = sum_of(held.at[which, 0], held.at[which, 1], z)
        leaving.append(copies.start(out.at[which, z], (sa_ref, sb_ref)[which].at[z]))
    for copy in leaving:
        copy.wait()


def fold_split(ka, ga, kb, gb, after=()):
    _, _, r, c = ka.shape
    return run(
        fold_split_kernel,
        (ka, ga, kb, gb),
        [ANY] * 4,
        [ANY] * 2,
        [shape((2, r, c), BF16)] * 2,
        (1,),
        "fold_split",
        [
            pltpu.VMEM((2, 2, 2, r, c), BF16),
            pltpu.VMEM((2, 2, r, c), BF16),
            pltpu.SemaphoreType.DMA((12,)),
        ],
        after,
        weight=FOLD_WEIGHT,
    )


def fold_near_kernel(groups, *refs):
    inputs, targets = refs[: 6 * groups], refs[6 * groups : 6 * groups + 4]
    *held, out, semaphores = refs[6 * groups + 4 :]
    mine = lax.axis_index("y"), lax.axis_index("x")
    low, high = lax.axis_index("z") % 2, lax.axis_index("z") // 2
    copies = Copies(semaphores)
    arrivals = []
    for group in range(groups):
        arrays = inputs[6 * group : 6 * group + 6]
        for which in range(2):
            *kept, got = arrays[3 * which : 3 * which + 3]
            place = held[group]
            arrivals.append(copies.start(got, place.at[which, 2]))
            for z in range(2):
                for n, ref in enumerate(kept):
                    arrivals.append(copies.start(ref.at[z, mine[which]], place.at[which, n, z]))
    for copy in arrivals:
        copy.wait()
    leaving = []
    for n, (half, z) in enumerate(((1 - high, 1 - low), (high, 1 - low), (1 - high, low), (high, low))):
        done = 0
        for place in held:
            rows = place.shape[3]
            total = sum(place[half, m, z].astype(F32) for m in range(3))
            out[n, done : done + rows, :] = total.astype(BF16)
            done += rows
        leaving.append(copies.start(out.at[n], targets[n]))
    for copy in leaving:
        copy.wait()


def fold_near(groups, after=()):
    arrays = [array for group in groups for array in group]
    rows, lanes = sum(group[0].shape[2] for group in groups), arrays[0].shape[3]
    return run(
        functools.partial(fold_near_kernel, len(groups)),
        arrays,
        [ANY] * len(arrays),
        [ANY] * 4,
        [shape((rows, lanes), BF16)] * 4,
        (1,),
        "fold_near",
        [pltpu.VMEM((2, 3, 2) + group[0].shape[2:], BF16) for group in groups]
        + [pltpu.VMEM((4, rows, lanes), BF16), pltpu.SemaphoreType.DMA((10 * len(groups) + 4,))],
        after,
        weight=FOLD_WEIGHT,
    )


def fold_far_kernel(k, g, send_ref, held, out, semaphores):
    copies = Copies(semaphores)
    for copy in [copies.start(ref, held.at[n]) for n, ref in enumerate((k, g))]:
        copy.wait()
    out[...] = sum_of(held.at[0], held.at[1], slice(None))
    copies.start(out, send_ref).wait()


def fold_far(keep, got, after=(), weight=FOLD_WEIGHT):
    return run(
        fold_far_kernel,
        (keep, got),
        [ANY] * 2,
        ANY,
        shape(keep.shape, BF16),
        (1,),
        "fold_far",
        [
            pltpu.VMEM((2,) + keep.shape, BF16),
            pltpu.VMEM(keep.shape, BF16),
            pltpu.SemaphoreType.DMA((3,)),
        ],
        after,
        weight=weight,
    )


def settle_kernel(norms, groups, *refs):
    inputs, (before, out, squares, *held, semaphores) = refs[: 3 * groups], refs[3 * groups :]
    copies = Copies(semaphores)
    arrivals = []
    for group in range(groups):
        sources = inputs[3 * group : 3 * group + 3]
        arrivals.append([copies.start(ref, held[group].at[n]) for n, ref in enumerate(sources)])
    done = 0
    parts = before[...]
    for group in range(groups):
        for copy in arrivals[group]:
            copy.wait()
        total = sum(held[group][n].astype(F32) for n in range(3))
        out[done : done + total.shape[0], :] = total
        if norms and done == 0:
            core = lax.axis_index("narrow")
            row, lane = (lax.broadcasted_iota(jnp.int32, total.shape, n) for n in (0, 1))
            shared = jnp.logical_and(row >= NORM_ROW, row < NORM_ROW + 8)
            other = jnp.logical_or(lane < core * norms, lane >= (core + 1) * norms)
            total = jnp.where(jnp.logical_and(shared, other), 0.0, total)
        done += total.shape[0]
        total = total * total
        part = total[:, :128] + total[:, 128:256] + total[:, 256:]
        parts = parts + jnp.sum(part.reshape(-1, 8, 128), axis=0)
    if squares.shape != parts.shape:
        parts = jnp.broadcast_to(jnp.sum(parts, axis=0, keepdims=True), squares.shape)
    squares[...] = parts


def settle(groups, before, norms=0, count=8, after=()):
    arrays = [array for group in groups for array in group]
    rows, lanes = sum(group[0].shape[0] for group in groups), arrays[0].shape[1]
    return run(
        functools.partial(settle_kernel, norms, len(groups)),
        (*arrays, before),
        [ANY] * len(arrays) + [whole((8, 128))],
        [whole((rows, lanes)), whole((count, 128))],
        [shape((rows, lanes), F32), shape((count, 128), F32)],
        (1,),
        "settle",
        [pltpu.VMEM((3,) + group[2].shape, BF16) for group in groups]
        + [pltpu.SemaphoreType.DMA((3 * len(groups),))],
        after,
    )


def shuffle(values, axis, bit):
    return lax.ppermute(values, axis, [(i, i ^ bit) for i in range(lax.axis_size(axis))])


def adamw(master, first, second, gradient, factor, step_rate, decay_rate):
    fix_one = 1.0 - BETA_ONE**STEP_NUMBER
    fix_two = 1.0 - BETA_TWO**STEP_NUMBER
    clipped = gradient * factor
    first = BETA_ONE * first + (1.0 - BETA_ONE) * clipped
    second = BETA_TWO * second + (1.0 - BETA_TWO) * clipped * clipped
    update = first / fix_one / (jnp.sqrt(second / fix_two) + ADAM_EPS)
    master = master - step_rate * (update + decay_rate * master)
    return (master, first, second)


def update_kernel(sums_ref, zero_ref, one_ref, *refs):
    states, news, clip_ref = refs[:15], refs[15:30], refs[30]
    layer = pl.program_id(0)
    total = jnp.sum(jnp.sum(sums_ref[...], axis=0, keepdims=True), axis=1, keepdims=True)
    clip_norm = jnp.sqrt(total)
    factor = jnp.minimum(1.0, CLIP / clip_norm)
    clip_ref[0] = clip_norm[0, 0]

    def kind(at, gradient, rate, decay):
        old = [ref[...] for ref in states[3 * at : 3 * at + 3]]
        for ref, value in zip(news[3 * at : 3 * at + 3], adamw(*old, gradient, factor, rate, decay)):
            ref[...] = value

    def all_kinds(grads):
        kind(0, grads[FF_ROWS:].reshape(news[0].shape), LR_MATRIX, DECAY_MATRIX)
        kind(1, jnp.concatenate([grads[384:408], grads[416:440]], axis=1), LR_MATRIX, DECAY_MATRIX)
        parts = [grads[at : at + 48] for at in range(192, 384, 48)]
        kind(2, jnp.concatenate(parts, axis=1), LR_MATRIX, DECAY_MATRIX)
        kind(3, jnp.concatenate([grads[:96], grads[96:192]], axis=1), LR_MATRIX, DECAY_MATRIX)

    @pl.when(layer == 0)
    def _():
        all_kinds(zero_ref[...])
        part = states[12].shape[1]
        columns = zero_ref[NORM_ROW : NORM_ROW + 8, :128]
        mine = jnp.where(lax.axis_index("narrow") == 0, columns[:, :part], columns[:, part : 2 * part])
        kind(4, mine, LR_NORMS, 0.0)

    @pl.when(layer == 1)
    def _():
        all_kinds(one_ref[...])


def update(sums, zero, one, states):
    specs = [layer_at(state) for state in states[:12]] + [whole(state.shape) for state in states[12:]]
    *news, clip_norm = run(
        update_kernel,
        (sums, zero, one, *states),
        [whole(sums.shape), whole(zero.shape), whole(one.shape)] + specs,
        specs + [IN_SMEM],
        [shape(state.shape, F32) for state in states] + [shape((1,), F32)],
        (LAYERS,),
        "update",
    )
    return news, clip_norm


def layer_at(array):
    rest = array.shape[1:]
    return pl.BlockSpec((None,) + rest, lambda l: (l,) + (0,) * len(rest))


def shards(
    stream, seq_lengths, cotangent, w_qkv, w_out, w_in, w_back, norm_params,
    qkv_master, qkv_first, qkv_second, out_master, out_first, out_second,
    in_master, in_first, in_second, back_master, back_first, back_second,
    norm_master, norm_first, norm_second,
    wide_axes,
):
    rows, width = stream.shape
    half = w_qkv.shape[3]
    every = wide_axes + ("narrow",)
    wide = math.prod(lax.axis_size(axis) for axis in wide_axes)
    by_axes = len(wide_axes) == 3
    here = seq_lengths
    cos, sin, live = tables(here, rows)

    qkv = jnp.transpose(w_qkv, (0, 2, 1, 3))
    qkv_peer, out_peer = swap(qkv), swap(w_out)
    in_peer = swap(lax.optimization_barrier((w_in, cos, out_peer))[0])
    back_peer = None

    low = stream
    kept = []
    got = [None] * LAYERS
    for layer in range(LAYERS):
        last = layer == LAYERS - 1
        if layer == 0:
            *own, kv_own = project(low, (qkv,), layer, cos, sin)
            *peer, kv_peer = project(low, (qkv_peer,), layer, cos, sin)
            kv, kv_at = (swap(kv_peer), swap(kv_own)), (0, 0)
            back_peer = swap(lax.optimization_barrier((w_back, *kv))[0])
        else:
            *parts, kv = project(low, (qkv, qkv_peer), layer, cos, sin)
            own, peer = parts[:3], parts[3:]
            kv, kv_at = (swap(kv),) * 2, (0, 1)
        low_got = swap(low)
        m_own, m_peer, rden, ffn_in, xh1, rs1, states = attend(
            here, own, peer, kv, kv_at, w_out, out_peer, layer, low, norm_params
        )
        h_own, h_peer, slope, out, xh2, rs2 = (feed if last else feed_grid)(
            ffn_in, w_in, in_peer, w_back, back_peer, layer, norm_params, F32 if last else BF16,
            got[layer - 1] + (low_got,) if last else (),
        )
        got[layer] = (low_got, swap(m_peer), swap(ffn_in), swap(h_peer))
        kept.append((low, own, peer, m_own, m_peer, rden, ffn_in, xh1, rs1, states, h_own, slope, xh2, rs2))
        low = out

    count = wide * lax.axis_size("narrow")
    up = cotangent
    norm_grads = [None] * LAYERS
    shares = [None] * LAYERS
    by_x, by_y = (lambda v: swap(v, "x")), (lambda v: swap(v, "y"))
    near, far = (lambda v: shuffle(v, "z", 1)), (lambda v: shuffle(v, "z", 2))
    after = got[LAYERS - 1][1:3]
    for layer in reversed(range(LAYERS)):
        (low, own, peer, m_own, m_peer, rden, ffn_in, xh1, rs1, states, h_own, slope, xh2, rs2) = (
            kept[layer]
        )
        low_got, m_got, ffn_got, h_got = got[layer]
        last = layer == 0
        gfb, gh_own, gh_peer, norm_grads[layer] = feed_back(
            up, None if last else live, xh2, rs2, xh1, rs1, slope, w_in, in_peer, w_back, back_peer,
            layer, norm_params, after,
        )
        gfb_got, gh_got = swap(gfb), swap(gh_peer)
        mix = (gfb, w_out, out_peer, layer, rden, m_own, m_peer, own[0], peer[0])
        back = (here, own, peer)
        norm_sum = jnp.stack(norm_grads) if last else None
        if not by_axes:
            back_grad = weight_grad(h_own, gfb[0], h_got, gfb_got[0], 512, width, "back_grad")
            in_grad = weight_grad(ffn_in, gh_own, ffn_got, gh_got, width, 512, "in_grad")
            out_grad = weight_grad(m_own, gfb[1], m_got, gfb_got[1], half, width, "out_grad")
            gx, dkv = mix_back(*mix)
            g_own, *g_peer = attend_back(*back, gx, states, swap(dkv), cos, sin)
            up = input_back(g_own, g_peer, qkv, qkv_peer, layer, gfb)
            g_got = jnp.concatenate([swap(g) for g in g_peer], axis=1)
            qkv_grad = weight_grad(low, g_own, low_got, g_got, width, half, "qkv_grad")
            shares[layer] = [
                lax.psum_scatter(g, wide_axes, scatter_dimension=0, tiled=True).astype(F32)
                for g in (qkv_grad, out_grad, in_grad, back_grad)
            ]
            shares[layer][0] = shares[layer][0].reshape(-1, 3, half)
            after = ()
            continue
        if last:
            norms = jnp.transpose(norm_sum.reshape(8, wide, width // wide), (1, 0, 2))
            norms = jnp.pad(norms, ((0, 0), (0, 0), (0, 128 - width // wide)))
            norms_got = swap(norms)
            sa, sb = fold_split(*q_first, (gfb,))
            q_second = q_first[:2] + (by_y(sa),) + q_first[2:] + (by_x(sb),)
            after = (sa,)
        else:
            norms = norms_got = jnp.zeros((wide, 8, 128), F32)
            after = (h_got,)
        gx, dkv = mix_back(*mix, after)
        dkv_got = swap(dkv)
        ka, sa, kb, sb = pack(
            here, h_own, gfb, h_got, gfb_got, ffn_in, gh_own, ffn_got, gh_got, m_own, m_got,
            norms, norms_got, (dkv_got,),
        )
        ff_first = (ka, by_x(sa), kb, by_y(sb))
        if last:
            send, side, keep, own_part = fold_near((ff_second, q_second), (ka,))
            one_cross, one_own = (keep, near(send)), (own_part, near(side))
            g_own, *g_peer = attend_back(*back, gx, states, dkv_got, cos, sin, (keep,))
            send = fold_far(*one_cross, (g_own,), 0)
            one_parts = one_own + (far(send),)
            after = (send,)
        else:
            g_own, *g_peer, up = attend_back(
                *back, gx, states, dkv_got, cos, sin, (ka,), (qkv, qkv_peer, layer, gfb)
            )
            after = (g_own,)
        g_got = [swap(g) for g in g_peer]
        if last:
            sa, sb = fold_split(*ff_first, after)
            ff_second = ff_first[:2] + (by_y(sa),) + ff_first[2:] + (by_x(sb),)
            after = (sa,)
        q_ka, q_sa, q_kb, q_sb = q_pack(low, g_own, low_got, g_got, half, after)
        q_first = (q_ka, by_x(q_sa), q_kb, by_y(q_sb))
        if not last:
            sa, sb = fold_split(*ff_first, (q_ka,))
            ff_second = ff_first[:2] + (by_y(sa),) + ff_first[2:] + (by_x(sb),)
            after = (sa,)
            continue
        send, side, keep, own_part = fold_near((ff_second,), (q_ka,))
        ff_cross, ff_own = (keep, near(send)), (own_part, near(side))
        up = input_back(g_own, g_peer, qkv, qkv_peer, layer, gfb, (keep,))
        sa, sb = fold_split(*q_first, (up,))
        q_second = q_first[:2] + (by_y(sa),) + q_first[2:] + (by_x(sb),)
        ff_send = fold_far(*ff_cross, (sa,))
        ff_parts = ff_own + (far(ff_send),)
        one, squares = settle((one_parts,), jnp.zeros((8, 128), F32), after=(ff_send,))
        send, side, keep, own_part = fold_near((q_second,), (one,))
        q_cross, q_own = (keep, near(send)), (own_part, near(side))
        send = fold_far(*q_cross, (), 0)
        part = width // wide // 2
        zero, squares = settle((ff_parts, q_own + (far(send),)), squares, part, count)

    states = (
        qkv_master, qkv_first, qkv_second, out_master, out_first, out_second,
        in_master, in_first, in_second, back_master, back_first, back_second,
        norm_master, norm_first, norm_second,
    )
    exchange = lambda rows_in: lax.all_to_all(rows_in, every, 0, 0, tiled=True)
    if by_axes:
        sums = exchange(squares)
        flip = lambda array: jnp.transpose(array, (0, 2, 1, 3))
        states = tuple(flip(v) for v in states[:3]) + states[3:12] + tuple(
            v.reshape(8, -1) for v in states[12:]
        )
        new, clip_norm = update(sums, zero, one, states)
        new = [flip(v) for v in new[:3]] + new[3:12] + [v.reshape(LAYERS, 4, -1) for v in new[12:]]
        return (out, up, *new, clip_norm)
    gradients = [jnp.stack([shares[l][kind] for l in range(LAYERS)]) for kind in range(4)]
    gradients.append(lax.psum_scatter(norm_sum, every, scatter_dimension=2, tiled=True))
    squares = sum(jnp.sum(g * g) for g in gradients)
    clip_norm = jnp.sqrt(exchange(jnp.broadcast_to(squares, (count, 128))).sum(0)[:1])
    factor = jnp.minimum(1.0, CLIP / clip_norm[0])
    new = []
    for kind, gradient in enumerate(gradients):
        rates = (LR_MATRIX, DECAY_MATRIX) if kind < 4 else (LR_NORMS, 0.0)
        new += adamw(*states[3 * kind : 3 * kind + 3], gradient, factor, *rates)
    return (out, up, *new, clip_norm)


def solution(mesh):
    wide_axes = ("wide",)
    if mesh.shape["wide"] == 16:
        wide_axes = ("z", "y", "x")
        mesh = Mesh(mesh.devices.reshape(4, 2, 2, 2), wide_axes + ("narrow",))
    rows = P(wide_axes + ("narrow",), None)
    qkv = P(None, wide_axes, None, "narrow")
    deep = P(None, ("narrow",) + wide_axes, None)
    in_part = P(None, wide_axes, "narrow")
    norm = P(None, None, wide_axes + ("narrow",))
    states = (qkv,) * 3 + (deep,) * 3 + (in_part,) * 3 + (deep,) * 3 + (norm,) * 3
    in_specs = (
        rows, P(wide_axes, None), rows,
        P(None, None, None, "narrow"), P(None, "narrow", None), P(None, None, "narrow"),
        P(None, "narrow", None), P(),
    ) + states
    out_specs = (rows, rows) + states + (P(),)
    return jax.shard_map(
        functools.partial(shards, wide_axes=wide_axes),
        mesh=mesh, in_specs=in_specs, out_specs=out_specs, check_vma=False,
    )
```
